32 devices in a mesh: blk: 8 (over z, x), grp: 4 (over y, core).
Axes of the slice: x: 2, y: 2, z: 4, core: 2. Of those that a mesh axis runs over, the one named last changes fastest.
Arguments:
- picture_embedding_matrix: bfloat16 [13312, 1152], P(('blk', 'grp')), may hold values from -0.1875 to 0.1875
- caption_embedding_matrix: bfloat16 [13312, 1152], P(('blk', 'grp')), may hold values from -0.1875 to 0.1875
- matching_target_entry: int32 [32, 416], P(('blk', 'grp')), may hold values from 0 to 415, each once within a row
- sharpness_factor: float32 [1], replicated, may hold values from 5 to 20
- score_shift_array: float32 [1], replicated, may hold values from -4 to -1
Outputs:
- image_grad: bfloat16 [13312, 1152], P(('blk', 'grp'))
- text_grad: bfloat16 [13312, 1152], P(('blk', 'grp'))
The draws below stay inside these ranges and needn't reach their ends.
Inputs may be any that keep to these rules, and one draw needn't show every extreme that they name: Each row of matching_target_entry is a permutation of 0 to 415.
All inputs are finite; a program needn't handle non-finite values.
Results may differ from the reference program's by a relative error of at most 0.0056.
Values may be sent and summed in bfloat16 or wider, within the bound.
No kernel may reach another device: no remote copies, remote signals or barrier semaphores. Data moves between devices by JAX's collectives and lax.ppermute only.
A program may use at most 64 MiB of HBM per device.

```python
import math
import jax
import jax.numpy as jnp
from jax import lax

D = 1152
ROWS = 416
BLOCKS = 32
PAIRS = 13312
N_BLK = 8
N_GRP = 4


def block_levels(own_key, extent, cuts, smallest, top_value):
    level, own = 1.0, jax.random.fold_in(own_key, 6)
    for position, parts in cuts:
        draws = jnp.exp(jax.random.uniform(jax.random.fold_in(own, position), (parts,), jnp.float32, smallest / len(cuts), top_value / len(cuts)))
        level = level * jnp.repeat(draws, extent[position] // parts).reshape([-1 if axis == position else 1 for axis in range(len(extent))])
    return level


def noise(stream_key, shape, spread, most, cuts=(), held_as=jnp.bfloat16):
    level = block_levels(stream_key, shape, cuts, -0.22, 0.18) if cuts else 1.0
    drawn = jax.random.normal(stream_key, shape, jnp.float32) * spread * level
    return jnp.minimum(jnp.maximum(drawn, -most), most).astype(held_as)


def setup_inputs(seed: int = 0) -> dict:
    keys = jax.random.split(jax.random.key(seed), 6)
    picture_embedding_matrix = noise(keys[0], (PAIRS, D), D ** -0.5, 0.1875, ((0, 32),))
    caption_embedding_matrix = noise(keys[1], (PAIRS, D), D ** -0.5, 0.1875, ((0, 32),))
    matching_target_entry = jax.vmap(lambda own: jax.random.permutation(own, ROWS))(jax.random.split(keys[2], BLOCKS)).reshape((BLOCKS, ROWS)).astype(jnp.int32)
    sharpness_factor = jnp.clip(jnp.exp(jax.random.uniform(keys[3], (1,), jnp.float32, math.log(5.0), math.log(20.0))), 5.0, 20.0)
    score_shift_array = jnp.clip(jax.random.uniform(keys[4], (1,), jnp.float32, -4.0, -1.0), -4.0, -1.0)
    return {"picture_embedding_matrix": picture_embedding_matrix, "caption_embedding_matrix": caption_embedding_matrix, "matching_target_entry": matching_target_entry, "sharpness_factor": sharpness_factor, "score_shift_array": score_shift_array}


def tile_derivative_sequence(picture_tile, already_seen, matched_entry, sharpness_multiplier, shift_amount_term):
    score_matrix = jnp.dot(picture_tile, already_seen.T, preferred_element_type=jnp.float32) * sharpness_multiplier + shift_amount_term
    column = lax.broadcasted_iota(jnp.int32, score_matrix.shape, 1)
    label = (column == matched_entry[:, None]).astype(jnp.float32)
    score_derivative = (jax.nn.sigmoid(score_matrix) - label).astype(jnp.bfloat16)
    picture_slice = (sharpness_multiplier * jnp.dot(score_derivative, already_seen, preferred_element_type=jnp.float32)).astype(jnp.bfloat16)
    running_subtotal = sharpness_multiplier * jnp.dot(score_derivative.T, picture_tile, preferred_element_type=jnp.float32)
    row_count = picture_tile.shape[0]
    own_part = running_subtotal[:row_count]
    other_parts = running_subtotal[row_count:].reshape(3, row_count, -1).astype(jnp.bfloat16)
    return picture_slice, own_part, other_parts


def reference(picture_embedding_matrix, caption_embedding_matrix, matching_target_entry, sharpness_factor, score_shift_array):
    width = picture_embedding_matrix.shape[1]
    grid_text = caption_embedding_matrix.reshape(N_BLK, N_GRP, ROWS, width)
    beside_blk = jnp.roll(grid_text, 1, axis=0)
    beside_grp = jnp.roll(grid_text, 1, axis=1)
    corner = jnp.roll(beside_blk, 1, axis=1)
    visited_all = jnp.concatenate([grid_text, beside_blk, beside_grp, corner], axis=2)
    visited_all = visited_all.reshape(N_BLK * N_GRP, 4 * ROWS, width)
    image_blocks = picture_embedding_matrix.reshape(N_BLK * N_GRP, ROWS, width)
    sharpness_multiplier = sharpness_factor[0]
    shift_amount_term = score_shift_array[0]

    def one_block(elements_here):
        return tile_derivative_sequence(elements_here[0], elements_here[1], elements_here[2], sharpness_multiplier, shift_amount_term)

    image_parts, local_part_list, other_parts = lax.map(one_block, (image_blocks, visited_all, matching_target_entry))
    image_grad = image_parts.reshape(N_BLK * N_GRP * ROWS, width)
    local_part_list = local_part_list.reshape(N_BLK, N_GRP, ROWS, width)
    other_parts = other_parts.reshape(N_BLK, N_GRP, 3, ROWS, width)
    from_blk = jnp.roll(other_parts[:, :, 0], -1, axis=0).astype(jnp.float32)
    from_grp = jnp.roll(other_parts[:, :, 1], -1, axis=1).astype(jnp.float32)
    corner_source_part = jnp.roll(jnp.roll(other_parts[:, :, 2], -1, axis=0), -1, axis=1).astype(jnp.float32)
    text_total = local_part_list + from_blk + corner_source_part + from_grp
    text_grad = text_total.astype(jnp.bfloat16).reshape(N_BLK * N_GRP * ROWS, width)
    return image_grad, text_grad
```

```python
import jax
import jax.numpy as jnp
from jax import lax
from jax.sharding import PartitionSpec as P


def shifted(shard, axis, by):
    devices = lax.axis_size(axis)
    return lax.ppermute(shard, axis, [(i, (i + by) % devices) for i in range(devices)])


def dot_nt(a, b):
    return lax.dot_general(a, b, (((1,), (1,)), ((), ())), preferred_element_type=jnp.float32)


def dot_tn(a, b):
    return lax.dot_general(a, b, (((0,), (0,)), ((), ())), preferred_element_type=jnp.float32)


def dot_nn(a, b):
    return jnp.dot(a, b, preferred_element_type=jnp.float32)


def body(image, text, target, factor, shift):
    scale = factor[0]
    bias = shift[0]
    text_prev = shifted(text, "blk", 1)
    image_next = shifted(image, "grp", -1)

    own = jax.nn.sigmoid(dot_nt(image, text) * scale + bias)
    column = lax.broadcasted_iota(jnp.int32, own.shape, 1)
    own = (own - (column == target[0][:, None]).astype(jnp.float32)).astype(jnp.bfloat16)

    def derivative(a, b):
        return jax.nn.sigmoid(dot_nt(a, b) * scale + bias).astype(jnp.bfloat16)

    next_own = derivative(image_next, text)
    own_prev = derivative(image, text_prev)
    next_prev = derivative(image_next, text_prev)

    text_sent = scale * (dot_tn(own_prev, image) + dot_tn(next_prev, image_next))
    text_back = shifted(text_sent.astype(jnp.bfloat16), "blk", -1)
    image_sent = scale * (dot_nn(next_own, text) + dot_nn(next_prev, text_prev))
    image_back = shifted(image_sent.astype(jnp.bfloat16), "grp", 1)

    image_grad = scale * (dot_nn(own, text) + dot_nn(own_prev, text_prev))
    text_grad = scale * (dot_tn(own, image) + dot_tn(next_own, image_next))
    image_grad = (image_grad + image_back.astype(jnp.float32)).astype(jnp.bfloat16)
    text_grad = (text_grad + text_back.astype(jnp.float32)).astype(jnp.bfloat16)
    return image_grad, text_grad


def solution(mesh):
    block = P(("blk", "grp"), None)
    return jax.shard_map(
        body, mesh=mesh, in_specs=(block, block, block, P(), P()), out_specs=(block, block), check_vma=False
    )
```

```python
import jax
import jax.numpy as jnp
from jax import lax
from jax.sharding import PartitionSpec as P

CHUNKS = 2


def shifted(shard, axis, by):
    devices = lax.axis_size(axis)
    return lax.ppermute(shard, axis, [(i, (i + by) % devices) for i in range(devices)])


def dot_nt(a, b):
    return lax.dot_general(a, b, (((1,), (1,)), ((), ())), preferred_element_type=jnp.float32)


def dot_tn(a, b):
    return lax.dot_general(a, b, (((0,), (0,)), ((), ())), preferred_element_type=jnp.float32)


def dot_nn(a, b):
    return jnp.dot(a, b, preferred_element_type=jnp.float32)


def row_cuts(rows):
    tiles = rows // 16
    cuts = [tiles * i // CHUNKS * 16 for i in range(CHUNKS)] + [rows]
    return list(zip(cuts[:-1], cuts[1:]))


def body(image, text, target, factor, shift):
    scale = factor[0]
    bias = shift[0]
    cuts = row_cuts(text.shape[0])
    text_prev = [shifted(text[lo:hi], "blk", 1) for lo, hi in cuts]
    image_next = shifted(image, "grp", -1)

    own = jax.nn.sigmoid(dot_nt(image, text) * scale + bias)
    column = lax.broadcasted_iota(jnp.int32, own.shape, 1)
    own = (own - (column == target[0][:, None]).astype(jnp.float32)).astype(jnp.bfloat16)

    def derivative(a, b):
        return jax.nn.sigmoid(dot_nt(a, b) * scale + bias).astype(jnp.bfloat16)

    image_grad = dot_nn(own, text)
    text_grad = dot_tn(own, image)

    next_own = derivative(image_next, text)
    image_sent = dot_nn(next_own, text)
    text_grad = scale * (text_grad + dot_tn(next_own, image_next))

    text_back = []
    for part in text_prev:
        own_prev = derivative(image, part)
        next_prev = derivative(image_next, part)
        text_sent = scale * (dot_tn(own_prev, image) + dot_tn(next_prev, image_next))
        text_back.append(shifted(text_sent.astype(jnp.bfloat16), "blk", -1))
        image_sent = image_sent + dot_nn(next_prev, part)
        image_grad = image_grad + dot_nn(own_prev, part)

    image_back = shifted((scale * image_sent).astype(jnp.bfloat16), "grp", 1)
    image_grad, text_grad = lax.optimization_barrier((scale * image_grad, text_grad))
    text_back = jnp.concatenate(text_back, axis=0)
    image_grad = (image_grad + image_back.astype(jnp.float32)).astype(jnp.bfloat16)
    text_grad = (text_grad + text_back.astype(jnp.float32)).astype(jnp.bfloat16)
    return image_grad, text_grad


def solution(mesh):
    block = P(("blk", "grp"), None)
    return jax.shard_map(
        body, mesh=mesh, in_specs=(block, block, block, P(), P()), out_specs=(block, block), check_vma=False
    )
```

```python
import jax
import jax.numpy as jnp
from jax import lax
from jax.experimental import pallas as pl
from jax.experimental.pallas import tpu as pltpu
from jax.sharding import PartitionSpec as P

CHUNKS = 2
MIB = 2**20
SMEM = pl.BlockSpec(memory_space=pltpu.SMEM)
VMEM = pl.BlockSpec(memory_space=pltpu.VMEM)
HBM = pl.BlockSpec(memory_space=pltpu.HBM)
ANY = pl.BlockSpec(memory_space=pl.ANY)


def shifted(shard, axis, by):
    devices = lax.axis_size(axis)
    return lax.ppermute(shard, axis, [(i, (i + by) % devices) for i in range(devices)])


def dot_nt(a, b):
    return lax.dot_general(a, b, (((1,), (1,)), ((), ())), preferred_element_type=jnp.float32)


def dot_tn(a, b):
    return lax.dot_general(a, b, (((0,), (0,)), ((), ())), preferred_element_type=jnp.float32)


def dot_nn(a, b):
    return jnp.dot(a, b, preferred_element_type=jnp.float32)


def row_cuts(rows):
    tiles = rows // 16
    cuts = [tiles * i // CHUNKS * 16 for i in range(CHUNKS)] + [rows]
    return list(zip(cuts[:-1], cuts[1:]))


def fetch(sources, after):
    count = len(sources)

    def kernel(*refs):
        sems = refs[-1]
        outs = refs[-1 - count : -1]
        copies = [
            pltpu.make_async_copy(refs[i].at[pl.ds(lo, hi - lo), :], outs[i], sems.at[i])
            for i, (_, lo, hi) in enumerate(sources)
        ]
        for copy in copies:
            copy.start()
        for copy in copies:
            copy.wait()

    return pl.pallas_call(
        kernel,
        out_shape=[jax.ShapeDtypeStruct((hi - lo, a.shape[1]), a.dtype) for a, lo, hi in sources],
        in_specs=[HBM] * count + [ANY] * len(after),
        out_specs=[VMEM] * count,
        scratch_shapes=[pltpu.SemaphoreType.DMA((count,))],
        compiler_params=pltpu.CompilerParams(vmem_limit_bytes=2 * MIB),
        name="fetch",
    )(*[a for a, _, _ in sources], *after)


def partial_kernel(scale_ref, bias_ref, image_ref, next_ref, part_ref, *refs):
    sent_ref, own_ref, other_ref = refs[-3:]
    scale = scale_ref[0]
    bias = bias_ref[0]
    part = part_ref[...]
    own = jax.nn.sigmoid(dot_nt(part, image_ref[...]) * scale + bias).astype(jnp.bfloat16)
    own_ref[...] = own
    total = dot_nn(own, image_ref[...])
    other = jax.nn.sigmoid(dot_nt(part, next_ref[...]) * scale + bias).astype(jnp.bfloat16)
    other_ref[...] = other
    total += dot_nn(other, next_ref[...])
    sent_ref[...] = (scale * total).astype(jnp.bfloat16)


def partial(factor, shift, image, image_next, part, after):
    rows, width = part.shape
    columns = image.shape[0]
    return pl.pallas_call(
        partial_kernel,
        out_shape=(
            jax.ShapeDtypeStruct((rows, width), jnp.bfloat16),
            jax.ShapeDtypeStruct((rows, columns), jnp.bfloat16),
            jax.ShapeDtypeStruct((rows, columns), jnp.bfloat16),
        ),
        in_specs=[SMEM, SMEM, VMEM, VMEM, VMEM] + [ANY] * len(after),
        out_specs=(VMEM, VMEM, VMEM),
        compiler_params=pltpu.CompilerParams(vmem_limit_bytes=16 * MIB),
        cost_estimate=pl.CostEstimate(
            flops=8 * rows * columns * width,
            bytes_accessed=2 * (2 * columns + 2 * rows) * width,
            transcendentals=2 * rows * columns,
        ),
        name="partial",
    )(factor, shift, image, image_next, part, *after)


def add_rows(total, back, lo, result, after):
    rows, width = back.shape

    def kernel(total_ref, back_ref, *refs):
        result_ref, buffer, sem = refs[-3:]
        buffer[...] = (total_ref[pl.ds(lo, rows), :] + back_ref[...].astype(jnp.float32)).astype(jnp.bfloat16)
        copy = pltpu.make_async_copy(buffer, result_ref.at[pl.ds(lo, rows), :], sem)
        copy.start()
        copy.wait()

    kept = [] if result is None else [result]
    return pl.pallas_call(
        kernel,
        out_shape=jax.ShapeDtypeStruct(total.shape, jnp.bfloat16),
        in_specs=[VMEM, VMEM] + [HBM] * (len(kept) + len(after)),
        out_specs=HBM,
        scratch_shapes=[pltpu.VMEM((rows, width), jnp.bfloat16), pltpu.SemaphoreType.DMA],
        input_output_aliases={2: 0} if kept else {},
        compiler_params=pltpu.CompilerParams(vmem_limit_bytes=4 * MIB),
        name="add_rows",
    )(total, back, *kept, *after)


def body(image, text, target, factor, shift):
    scale = factor[0]
    bias = shift[0]
    cuts = row_cuts(text.shape[0])
    first = fetch([(text, *cuts[0])], [])
    *rest, held = fetch([(text, *cut) for cut in cuts[1:]] + [(image, 0, image.shape[0])], first)
    text_prev = [shifted(part, "blk", 1) for part in first]
    image_next = shifted(held, "grp", -1)
    text_prev += [shifted(part, "blk", 1) for part in rest]

    own = jax.nn.sigmoid(dot_nt(held, text) * scale + bias)
    column = lax.broadcasted_iota(jnp.int32, own.shape, 1)
    own = (own - (column == target[0][:, None]).astype(jnp.float32)).astype(jnp.bfloat16)

    image_grad = dot_nn(own, text)
    text_grad = dot_tn(own, held)

    next_own = jax.nn.sigmoid(dot_nt(image_next, text) * scale + bias).astype(jnp.bfloat16)
    image_sent = dot_nn(next_own, text)
    text_grad = scale * (text_grad + dot_tn(next_own, image_next))

    text_back = []
    after = []
    for part in text_prev:
        sent, own_prev, next_prev = partial(factor, shift, held, image_next, part, after)
        after = [sent]
        text_back.append(shifted(sent, "blk", -1))
        image_sent = image_sent + dot_tn(next_prev, part)
        image_grad = image_grad + dot_tn(own_prev, part)

    image_back = shifted((scale * image_sent).astype(jnp.bfloat16), "grp", 1)
    image_grad = add_rows(scale * image_grad, image_back, 0, None, [])
    result = None
    for (lo, _), back in zip(cuts, text_back):
        result = add_rows(text_grad, back, lo, result, [image_grad] if lo == cuts[-1][0] else [])
    return image_grad, result


def solution(mesh):
    block = P(("blk", "grp"), None)
    return jax.shard_map(
        body, mesh=mesh, in_specs=(block, block, block, P(), P()), out_specs=(block, block), check_vma=False
    )
```

```python
import jax
import jax.numpy as jnp
from jax import lax
from jax.experimental import pallas as pl
from jax.experimental.pallas import tpu as pltpu
from jax.sharding import PartitionSpec as P

MIB = 2**20
SMEM = pl.BlockSpec(memory_space=pltpu.SMEM)
VMEM = pl.BlockSpec(memory_space=pltpu.VMEM)
HBM = pl.BlockSpec(memory_space=pltpu.HBM)
ANY = pl.BlockSpec(memory_space=pl.ANY)


def shifted(shard, axis, by):
    devices = lax.axis_size(axis)
    return lax.ppermute(shard, axis, [(i, (i + by) % devices) for i in range(devices)])


def dot_nt(a, b):
    return lax.dot_general(a, b, (((1,), (1,)), ((), ())), preferred_element_type=jnp.float32)


def dot_tn(a, b):
    return lax.dot_general(a, b, (((0,), (0,)), ((), ())), preferred_element_type=jnp.float32)


def dot_nn(a, b):
    return jnp.dot(a, b, preferred_element_type=jnp.float32)


def row_cuts(rows):
    tiles = rows // 16
    cuts = [0, tiles * 2 // 5 * 16, tiles * 17 // 20 * 16, rows]
    return list(zip(cuts[:-1], cuts[1:]))


def fetch(sources, after):
    count = len(sources)

    def kernel(*refs):
        sems = refs[-1]
        outs = refs[-1 - count : -1]
        copies = [
            pltpu.make_async_copy(refs[i].at[pl.ds(lo, hi - lo), :], outs[i], sems.at[i])
            for i, (_, lo, hi) in enumerate(sources)
        ]
        for copy in copies:
            copy.start()
        for copy in copies:
            copy.wait()

    return pl.pallas_call(
        kernel,
        out_shape=[jax.ShapeDtypeStruct((hi - lo, a.shape[1]), a.dtype) for a, lo, hi in sources],
        in_specs=[HBM] * count + [ANY] * len(after),
        out_specs=[VMEM] * count,
        scratch_shapes=[pltpu.SemaphoreType.DMA((count,))],
        compiler_params=pltpu.CompilerParams(vmem_limit_bytes=2 * MIB),
        name="fetch",
    )(*[a for a, _, _ in sources], *after)


def partial_kernel(scale_ref, bias_ref, image_ref, next_ref, part_ref, *refs):
    sent_ref, own_ref, other_ref = refs[-3:]
    scale = scale_ref[0]
    bias = bias_ref[0]
    part = part_ref[...]
    own = jax.nn.sigmoid(dot_nt(part, image_ref[...]) * scale + bias).astype(jnp.bfloat16)
    own_ref[...] = own
    total = dot_nn(own, image_ref[...])
    other = jax.nn.sigmoid(dot_nt(part, next_ref[...]) * scale + bias).astype(jnp.bfloat16)
    other_ref[...] = other
    total += dot_nn(other, next_ref[...])
    sent_ref[...] = (scale * total).astype(jnp.bfloat16)


def partial(factor, shift, image, image_next, part, after):
    rows, width = part.shape
    columns = image.shape[0]
    return pl.pallas_call(
        partial_kernel,
        out_shape=(
            jax.ShapeDtypeStruct((rows, width), jnp.bfloat16),
            jax.ShapeDtypeStruct((rows, columns), jnp.bfloat16),
            jax.ShapeDtypeStruct((rows, columns), jnp.bfloat16),
        ),
        in_specs=[SMEM, SMEM, VMEM, VMEM, VMEM] + [ANY] * len(after),
        out_specs=(VMEM, VMEM, VMEM),
        compiler_params=pltpu.CompilerParams(vmem_limit_bytes=16 * MIB),
        cost_estimate=pl.CostEstimate(
            flops=8 * rows * columns * width,
            bytes_accessed=2 * (2 * columns + 2 * rows) * width,
            transcendentals=2 * rows * columns,
        ),
        name="partial",
    )(factor, shift, image, image_next, part, *after)


def add_rows(total, back, lo, result, after):
    rows, width = back.shape
    step = rows // 16 // 3 * 16 if rows >= 96 else rows
    cuts = [(i, min(i + step, rows)) for i in range(0, rows, step)]

    def kernel(total_ref, back_ref, *refs):
        result_ref, mark_ref, buffer, sems = refs[-4:]
        copies = []
        for i, (a, b) in enumerate(cuts):
            buffer[a:b, :] = (total_ref[lo + a : lo + b, :] + back_ref[a:b, :].astype(jnp.float32)).astype(jnp.bfloat16)
            copies.append(
                pltpu.make_async_copy(
                    buffer.at[pl.ds(a, b - a), :], result_ref.at[pl.ds(lo + a, b - a), :], sems.at[i]
                )
            )
            copies[-1].start()
        mark_ref[...] = jnp.zeros(mark_ref.shape, mark_ref.dtype)
        for copy in copies:
            copy.wait()

    kept = [] if result is None else [result]
    return pl.pallas_call(
        kernel,
        out_shape=(
            jax.ShapeDtypeStruct(total.shape, jnp.bfloat16),
            jax.ShapeDtypeStruct((8, 128), jnp.float32),
        ),
        in_specs=[VMEM, VMEM] + [HBM] * len(kept) + [ANY] * len(after),
        out_specs=(HBM, VMEM),
        scratch_shapes=[pltpu.VMEM((rows, width), jnp.bfloat16), pltpu.SemaphoreType.DMA((len(cuts),))],
        input_output_aliases={2: 0} if kept else {},
        compiler_params=pltpu.CompilerParams(vmem_limit_bytes=4 * MIB),
        name="add_rows",
    )(total, back, *kept, *after)


def body(image, text, target, factor, shift):
    scale = factor[0]
    bias = shift[0]
    cuts = row_cuts(text.shape[0])
    first = text[: cuts[0][1]]
    rest = fetch([(text, *cut) for cut in cuts[1:]], [first])
    text_prev = [shifted(part, "blk", 1) for part in [first, *rest]]
    image_next = shifted(image, "grp", -1)

    own = jax.nn.sigmoid(dot_nt(image, text) * scale + bias)
    column = lax.broadcasted_iota(jnp.int32, own.shape, 1)
    own = (own - (column == target[0][:, None]).astype(jnp.float32)).astype(jnp.bfloat16)

    image_grad = dot_nn(own, text)
    text_grad = dot_tn(own, image)

    next_own = jax.nn.sigmoid(dot_nt(image_next, text) * scale + bias).astype(jnp.bfloat16)
    image_sent = dot_nn(next_own, text)
    text_grad = scale * (text_grad + dot_tn(next_own, image_next))

    text_back = []
    after = [text_prev[1]]
    for part in text_prev:
        sent, own_prev, next_prev = partial(factor, shift, image, image_next, part, after)
        after = [sent]
        text_back.append(shifted(sent, "blk", -1))
        image_sent = image_sent + dot_tn(next_prev, part)
        image_grad = image_grad + dot_tn(own_prev, part)

    image_back = shifted((scale * image_sent).astype(jnp.bfloat16), "grp", 1)
    image_grad, image_mark = add_rows(scale * image_grad, image_back, 0, None, [])
    result = None
    for (lo, _), back in zip(cuts, text_back):
        result, _ = add_rows(text_grad, back, lo, result, [image_mark] if lo == cuts[-1][0] else [])
    return image_grad, result


def solution(mesh):
    block = P(("blk", "grp"), None)
    return jax.shard_map(
        body, mesh=mesh, in_specs=(block, block, block, P(), P()), out_specs=(block, block), check_vma=False
    )
```

```python
import jax
import jax.numpy as jnp
from jax import lax
from jax.experimental import pallas as pl
from jax.experimental.pallas import tpu as pltpu
from jax.sharding import PartitionSpec as P

MIB = 2**20
SMEM = pl.BlockSpec(memory_space=pltpu.SMEM)
VMEM = pl.BlockSpec(memory_space=pltpu.VMEM)
HBM = pl.BlockSpec(memory_space=pltpu.HBM)
ANY = pl.BlockSpec(memory_space=pl.ANY)


def shifted(shard, axis, by):
    devices = lax.axis_size(axis)
    return lax.ppermute(shard, axis, [(i, (i + by) % devices) for i in range(devices)])


def dot_nt(a, b):
    return lax.dot_general(a, b, (((1,), (1,)), ((), ())), preferred_element_type=jnp.float32)


def dot_tn(a, b):
    return lax.dot_general(a, b, (((0,), (0,)), ((), ())), preferred_element_type=jnp.float32)


def dot_nn(a, b):
    return jnp.dot(a, b, preferred_element_type=jnp.float32)


def row_cuts(rows):
    tiles = rows // 16
    cuts = [0, tiles * 6 // 26 * 16, tiles * 16 // 26 * 16, tiles * 23 // 26 * 16, rows]
    return list(zip(cuts[:-1], cuts[1:]))


def fetch(array, lo, hi, after):
    def kernel(array_ref, *refs):
        out_ref, sem = refs[-2:]
        copy = pltpu.make_async_copy(array_ref.at[pl.ds(lo, hi - lo), :], out_ref, sem)
        copy.start()
        copy.wait()

    return pl.pallas_call(
        kernel,
        out_shape=jax.ShapeDtypeStruct((hi - lo, array.shape[1]), array.dtype),
        in_specs=[ANY] * (1 + len(after)),
        out_specs=VMEM,
        scratch_shapes=[pltpu.SemaphoreType.DMA],
        compiler_params=pltpu.CompilerParams(vmem_limit_bytes=2 * MIB),
        name="fetch",
    )(array, *after)


def pass_on(array, after):
    return pl.pallas_call(
        lambda *refs: None,
        out_shape=jax.ShapeDtypeStruct(array.shape, array.dtype),
        in_specs=[ANY] * (1 + len(after)),
        out_specs=ANY,
        input_output_aliases={0: 0},
        compiler_params=pltpu.CompilerParams(vmem_limit_bytes=MIB),
        name="pass_on",
    )(array, *after)


def chunk_kernel(scale_ref, bias_ref, image_ref, next_ref, upper_ref, lower_ref, *refs):
    sent_ref, joined_ref, own_ref, other_ref = refs[-4:]
    scale, bias = scale_ref[0], bias_ref[0]
    rows = upper_ref.shape[0]
    joined_ref[:rows, :] = upper_ref[...]
    joined_ref[rows:, :] = lower_ref[...]
    part = joined_ref[...]
    image = image_ref[...]
    own = jax.nn.sigmoid(dot_nt(part, image) * scale + bias).astype(jnp.bfloat16)
    own_ref[...] = own
    total = dot_nn(own, image)
    image = next_ref[...]
    other = jax.nn.sigmoid(dot_nt(part, image) * scale + bias).astype(jnp.bfloat16)
    other_ref[...] = other
    total += dot_nn(other, image)
    sent_ref[...] = (scale * total).astype(jnp.bfloat16)


def chunk(factor, shift, image, image_next, upper, lower, after):
    rows, width = upper.shape[0] + lower.shape[0], upper.shape[1]
    columns = image.shape[0]
    text = jax.ShapeDtypeStruct((rows, width), jnp.bfloat16)
    tile = jax.ShapeDtypeStruct((rows, columns), jnp.bfloat16)
    return pl.pallas_call(
        chunk_kernel,
        out_shape=(text, text, tile, tile),
        in_specs=[SMEM] * 2 + [VMEM] * 4 + [ANY] * len(after),
        out_specs=(VMEM,) * 4,
        compiler_params=pltpu.CompilerParams(vmem_limit_bytes=16 * MIB),
        cost_estimate=pl.CostEstimate(
            flops=8 * rows * columns * width,
            bytes_accessed=2 * (2 * columns + 3 * rows) * width,
            transcendentals=2 * rows * columns,
        ),
        name="chunk",
    )(factor, shift, image, image_next, upper, lower, *after)


def add_rows(total, back, lo, result, after, mark=False):
    rows, width = back.shape
    step = rows // 16 // 3 * 16 if rows >= 96 else rows
    cuts = [(i, min(i + step, rows)) for i in range(0, rows, step)]

    def kernel(total_ref, back_ref, *refs):
        buffer, sems = refs[-2:]
        result_ref = refs[-4] if mark else refs[-3]
        copies = []
        for i, (a, b) in enumerate(cuts):
            buffer[a:b, :] = (total_ref[lo + a : lo + b, :] + back_ref[a:b, :].astype(jnp.float32)).astype(jnp.bfloat16)
            copies.append(
                pltpu.make_async_copy(
                    buffer.at[pl.ds(a, b - a), :], result_ref.at[pl.ds(lo + a, b - a), :], sems.at[i]
                )
            )
            copies[-1].start()
        if mark:
            refs[-3][...] = jnp.zeros((8, 128), jnp.float32)
        for copy in copies:
            copy.wait()

    kept = [] if result is None else [result]
    out = jax.ShapeDtypeStruct(total.shape, jnp.bfloat16)
    return pl.pallas_call(
        kernel,
        out_shape=(out, jax.ShapeDtypeStruct((8, 128), jnp.float32)) if mark else out,
        in_specs=[VMEM, VMEM] + [HBM] * len(kept) + [ANY] * len(after),
        out_specs=(HBM, VMEM) if mark else HBM,
        scratch_shapes=[pltpu.VMEM((rows, width), jnp.bfloat16), pltpu.SemaphoreType.DMA((len(cuts),))],
        input_output_aliases={2: 0} if kept else {},
        compiler_params=pltpu.CompilerParams(vmem_limit_bytes=4 * MIB),
        name="add_rows",
    )(total, back, *kept, *after)


def body(image, text, target, factor, shift):
    scale = factor[0]
    bias = shift[0]
    cuts = row_cuts(text.shape[0])
    first = text[: cuts[0][1]]
    part = [shifted(first, "blk", 1)]
    image_next = shifted(image, "grp", -1)
    part.append(shifted(fetch(text, *cuts[1], [first]), "blk", 1))

    target = fetch(target, 0, 1, [part[0]])
    part.append(shifted(fetch(text, *cuts[2], [target]), "blk", 1))
    own = jax.nn.sigmoid(dot_nt(image, text) * scale + bias)
    column = lax.broadcasted_iota(jnp.int32, own.shape, 1)
    own = (own - (column == target[0][:, None]).astype(jnp.float32)).astype(jnp.bfloat16)
    part.append(shifted(fetch(text, *cuts[3], [own]), "blk", 1))
    image_grad = dot_nn(own, text)
    text_grad = dot_tn(own, image)

    image_next = pass_on(image_next, [image_grad, text_grad])
    sent0, part0, own0, next0 = chunk(factor, shift, image, image_next, part[0], part[1], [])
    next_own = jax.nn.sigmoid(dot_nt(image_next, text) * scale + bias).astype(jnp.bfloat16)
    text_grad = scale * (text_grad + dot_tn(next_own, image_next))
    image_sent = dot_nn(next_own, text) + dot_tn(next0, part0)
    image_grad = image_grad + dot_tn(own0, part0)

    sent0 = pass_on(sent0, [part[2], image_sent])
    back0 = shifted(sent0, "blk", -1)

    sent1, part1, own1, next1 = chunk(factor, shift, image, image_next, part[2], part[3], [sent0])
    image_sent = (scale * (image_sent + dot_tn(next1, part1))).astype(jnp.bfloat16)
    image_back = shifted(image_sent, "grp", 1)
    sent1 = pass_on(sent1, [image_sent])
    back1 = shifted(sent1, "blk", -1)
    image_grad = scale * (image_grad + dot_tn(own1, part1))

    result = add_rows(text_grad, back0, 0, None, [])
    image_grad, mark = add_rows(image_grad, image_back, 0, None, [], mark=True)
    result = add_rows(text_grad, back1, cuts[2][0], result, [mark])
    return image_grad, result


def solution(mesh):
    block = P(("blk", "grp"), None)
    return jax.shard_map(
        body, mesh=mesh, in_specs=(block, block, block, P(), P()), out_specs=(block, block), check_vma=False
    )
```

```python
import jax
import jax.numpy as jnp
from jax import lax
from jax.experimental import pallas as pl
from jax.experimental.pallas import tpu as pltpu
from jax.sharding import PartitionSpec as P

MIB = 2**20
SMEM = pl.BlockSpec(memory_space=pltpu.SMEM)
VMEM = pl.BlockSpec(memory_space=pltpu.VMEM)
HBM = pl.BlockSpec(memory_space=pltpu.HBM)
ANY = pl.BlockSpec(memory_space=pl.ANY)


def shifted(shard, axis, by):
    devices = lax.axis_size(axis)
    return lax.ppermute(shard, axis, [(i, (i + by) % devices) for i in range(devices)])


def dot_nt(a, b):
    return lax.dot_general(a, b, (((1,), (1,)), ((), ())), preferred_element_type=jnp.float32)


def dot_tn(a, b):
    return lax.dot_general(a, b, (((0,), (0,)), ((), ())), preferred_element_type=jnp.float32)


def dot_nn(a, b):
    return jnp.dot(a, b, preferred_element_type=jnp.float32)


def row_cuts(rows):
    tiles = rows // 16
    cuts = [0, tiles * 6 // 26 * 16, tiles * 16 // 26 * 16, tiles * 20 // 26 * 16, rows]
    return list(zip(cuts[:-1], cuts[1:]))


def fetch(array, lo, hi, after):
    def kernel(array_ref, *refs):
        out_ref, sem = refs[-2:]
        copy = pltpu.make_async_copy(array_ref.at[pl.ds(lo, hi - lo), :], out_ref, sem)
        copy.start()
        copy.wait()

    return pl.pallas_call(
        kernel,
        out_shape=jax.ShapeDtypeStruct((hi - lo, array.shape[1]), array.dtype),
        in_specs=[ANY] * (1 + len(after)),
        out_specs=VMEM,
        scratch_shapes=[pltpu.SemaphoreType.DMA],
        compiler_params=pltpu.CompilerParams(vmem_limit_bytes=2 * MIB),
        name="fetch",
    )(array, *after)


def pass_on(array, after):
    return pl.pallas_call(
        lambda *refs: None,
        out_shape=jax.ShapeDtypeStruct(array.shape, array.dtype),
        in_specs=[ANY] * (1 + len(after)),
        out_specs=ANY,
        input_output_aliases={0: 0},
        compiler_params=pltpu.CompilerParams(vmem_limit_bytes=MIB),
        name="pass_on",
    )(array, *after)


def chunk_kernel(scale_ref, bias_ref, image_ref, next_ref, upper_ref, lower_ref, *refs):
    sent_ref, joined_ref, own_ref, other_ref = refs[-4:]
    scale, bias = scale_ref[0], bias_ref[0]
    rows = upper_ref.shape[0]
    joined_ref[:rows, :] = upper_ref[...]
    joined_ref[rows:, :] = lower_ref[...]
    part = joined_ref[...]
    image = image_ref[...]
    own = jax.nn.sigmoid(dot_nt(part, image) * scale + bias).astype(jnp.bfloat16)
    own_ref[...] = own
    total = dot_nn(own, image)
    image = next_ref[...]
    other = jax.nn.sigmoid(dot_nt(part, image) * scale + bias).astype(jnp.bfloat16)
    other_ref[...] = other
    total += dot_nn(other, image)
    sent_ref[...] = (scale * total).astype(jnp.bfloat16)


def chunk(factor, shift, image, image_next, upper, lower, after):
    rows, width = upper.shape[0] + lower.shape[0], upper.shape[1]
    columns = image.shape[0]
    text = jax.ShapeDtypeStruct((rows, width), jnp.bfloat16)
    tile = jax.ShapeDtypeStruct((rows, columns), jnp.bfloat16)
    return pl.pallas_call(
        chunk_kernel,
        out_shape=(text, text, tile, tile),
        in_specs=[SMEM] * 2 + [VMEM] * 4 + [ANY] * len(after),
        out_specs=(VMEM,) * 4,
        compiler_params=pltpu.CompilerParams(vmem_limit_bytes=16 * MIB),
        cost_estimate=pl.CostEstimate(
            flops=8 * rows * columns * width,
            bytes_accessed=2 * (2 * columns + 3 * rows) * width,
            transcendentals=2 * rows * columns,
        ),
        name="chunk",
    )(factor, shift, image, image_next, upper, lower, *after)


def add_rows(total, back, lo, result, after, mark=False):
    rows, width = back.shape
    step = rows // 16 // 3 * 16 if rows >= 96 else rows
    cuts = [(i, min(i + step, rows)) for i in range(0, rows, step)]

    def kernel(total_ref, back_ref, *refs):
        buffer, sems = refs[-2:]
        result_ref = refs[-4] if mark else refs[-3]
        copies = []
        for i, (a, b) in enumerate(cuts):
            buffer[a:b, :] = (total_ref[lo + a : lo + b, :] + back_ref[a:b, :].astype(jnp.float32)).astype(jnp.bfloat16)
            copies.append(
                pltpu.make_async_copy(
                    buffer.at[pl.ds(a, b - a), :], result_ref.at[pl.ds(lo + a, b - a), :], sems.at[i]
                )
            )
            copies[-1].start()
        if mark:
            refs[-3][...] = jnp.zeros((8, 128), jnp.float32)
        for copy in copies:
            copy.wait()

    kept = [] if result is None else [result]
    out = jax.ShapeDtypeStruct(total.shape, jnp.bfloat16)
    return pl.pallas_call(
        kernel,
        out_shape=(out, jax.ShapeDtypeStruct((8, 128), jnp.float32)) if mark else out,
        in_specs=[VMEM, VMEM] + [HBM] * len(kept) + [ANY] * len(after),
        out_specs=(HBM, VMEM) if mark else HBM,
        scratch_shapes=[pltpu.VMEM((rows, width), jnp.bfloat16), pltpu.SemaphoreType.DMA((len(cuts),))],
        input_output_aliases={2: 0} if kept else {},
        compiler_params=pltpu.CompilerParams(vmem_limit_bytes=4 * MIB),
        name="add_rows",
    )(total, back, *kept, *after)


def body(image, text, target, factor, shift):
    scale = factor[0]
    bias = shift[0]
    cuts = row_cuts(text.shape[0])
    first = text[: cuts[0][1]]
    part = [shifted(first, "blk", 1)]
    image_next = shifted(image, "grp", -1)
    part.append(shifted(fetch(text, *cuts[1], [first]), "blk", 1))

    target = fetch(target, 0, 1, [part[0]])
    part.append(shifted(fetch(text, *cuts[2], [target]), "blk", 1))
    own = jax.nn.sigmoid(dot_nt(image, text) * scale + bias)
    column = lax.broadcasted_iota(jnp.int32, own.shape, 1)
    own = (own - (column == target[0][:, None]).astype(jnp.float32)).astype(jnp.bfloat16)
    part.append(shifted(fetch(text, *cuts[3], [own]), "blk", 1))
    image_grad = dot_nn(own, text)
    text_grad = dot_tn(own, image)

    image_next = pass_on(image_next, [image_grad, text_grad])
    sent0, part0, own0, next0 = chunk(factor, shift, image, image_next, part[0], part[1], [])
    next_own = jax.nn.sigmoid(dot_nt(image_next, text) * scale + bias).astype(jnp.bfloat16)
    text_grad = scale * (text_grad + dot_tn(next_own, image_next))
    image_sent = dot_nn(next_own, text) + dot_tn(next0, part0)
    image_grad = image_grad + dot_tn(own0, part0)

    sent0 = pass_on(sent0, [part[2], image_sent])
    back0 = shifted(sent0, "blk", -1)

    sent1, part1, own1, next1 = chunk(factor, shift, image, image_next, part[2], part[3], [sent0])
    image_sent = (scale * (image_sent + dot_tn(next1, part1))).astype(jnp.bfloat16)
    image_back = shifted(image_sent, "grp", 1)
    sent1 = pass_on(sent1, [image_sent])
    back1 = shifted(sent1, "blk", -1)
    image_grad = scale * (image_grad + dot_tn(own1, part1))

    result = add_rows(text_grad, back0, 0, None, [])
    image_grad, mark = add_rows(image_grad, image_back, 0, None, [], mark=True)
    result = add_rows(text_grad, back1, cuts[2][0], result, [mark])
    return image_grad, result


def solution(mesh):
    block = P(("blk", "grp"), None)
    return jax.shard_map(
        body, mesh=mesh, in_specs=(block, block, block, P(), P()), out_specs=(block, block), check_vma=False
    )
```

```python
import jax
import jax.numpy as jnp
from jax import lax
from jax.experimental import pallas as pl
from jax.experimental.pallas import tpu as pltpu
from jax.sharding import PartitionSpec as P

MIB = 2**20
SMEM = pl.BlockSpec(memory_space=pltpu.SMEM)
VMEM = pl.BlockSpec(memory_space=pltpu.VMEM)
HBM = pl.BlockSpec(memory_space=pltpu.HBM)
ANY = pl.BlockSpec(memory_space=pl.ANY)


def shifted(shard, axis, by):
    devices = lax.axis_size(axis)
    return lax.ppermute(shard, axis, [(i, (i + by) % devices) for i in range(devices)])


def dot_nt(a, b):
    return lax.dot_general(a, b, (((1,), (1,)), ((), ())), preferred_element_type=jnp.float32)


def dot_tn(a, b):
    return lax.dot_general(a, b, (((0,), (0,)), ((), ())), preferred_element_type=jnp.float32)


def dot_nn(a, b):
    return jnp.dot(a, b, preferred_element_type=jnp.float32)


def row_cuts(rows):
    tiles = rows // 16
    cuts = [0, tiles * 4 // 26 * 16, tiles * 16 // 26 * 16, tiles * 23 // 26 * 16, rows]
    return list(zip(cuts[:-1], cuts[1:]))


def fetch(array, spans, after, space, limit):
    count = len(spans)

    def kernel(array_ref, *refs):
        sems = refs[-1]
        copies = [
            pltpu.make_async_copy(array_ref.at[pl.ds(lo, hi - lo), :], out_ref, sems.at[i])
            for i, ((lo, hi), out_ref) in enumerate(zip(spans, refs[-1 - count : -1]))
        ]
        for copy in copies:
            copy.start()
        for copy in copies:
            copy.wait()

    return pl.pallas_call(
        kernel,
        out_shape=[jax.ShapeDtypeStruct((hi - lo, array.shape[1]), array.dtype) for lo, hi in spans],
        in_specs=[ANY] * (1 + len(after)),
        out_specs=[space] * count,
        scratch_shapes=[pltpu.SemaphoreType.DMA((count,))],
        compiler_params=pltpu.CompilerParams(vmem_limit_bytes=limit),
        name="fetch",
    )(array, *after)


def pass_on(array, after):
    return pl.pallas_call(
        lambda *refs: None,
        out_shape=jax.ShapeDtypeStruct(array.shape, array.dtype),
        in_specs=[ANY] * (1 + len(after)),
        out_specs=ANY,
        input_output_aliases={0: 0},
        compiler_params=pltpu.CompilerParams(vmem_limit_bytes=MIB),
        name="pass_on",
    )(array, *after)


def chunk_kernel(scale_ref, bias_ref, image_ref, next_ref, upper_ref, lower_ref, *refs):
    sent_ref, joined_ref, own_ref, other_ref = refs[-4:]
    scale, bias = scale_ref[0], bias_ref[0]
    rows = upper_ref.shape[0]
    joined_ref[:rows, :] = upper_ref[...]
    joined_ref[rows:, :] = lower_ref[...]
    part = joined_ref[...]
    image = image_ref[...]
    own = jax.nn.sigmoid(dot_nt(part, image) * scale + bias).astype(jnp.bfloat16)
    own_ref[...] = own
    total = dot_nn(own, image)
    image = next_ref[...]
    other = jax.nn.sigmoid(dot_nt(part, image) * scale + bias).astype(jnp.bfloat16)
    other_ref[...] = other
    total += dot_nn(other, image)
    sent_ref[...] = (scale * total).astype(jnp.bfloat16)


def chunk(factor, shift, image, image_next, upper, lower, after):
    rows, width = upper.shape[0] + lower.shape[0], upper.shape[1]
    columns = image.shape[0]
    text = jax.ShapeDtypeStruct((rows, width), jnp.bfloat16)
    tile = jax.ShapeDtypeStruct((rows, columns), jnp.bfloat16)
    return pl.pallas_call(
        chunk_kernel,
        out_shape=(text, text, tile, tile),
        in_specs=[SMEM] * 2 + [VMEM] * 4 + [ANY] * len(after),
        out_specs=(VMEM,) * 4,
        compiler_params=pltpu.CompilerParams(vmem_limit_bytes=16 * MIB),
        cost_estimate=pl.CostEstimate(
            flops=8 * rows * columns * width,
            bytes_accessed=2 * (2 * columns + 3 * rows) * width,
            transcendentals=2 * rows * columns,
        ),
        name="chunk",
    )(factor, shift, image, image_next, upper, lower, *after)


def add_rows(total, back, lo, result, after, mark=False):
    rows, width = back.shape
    step = rows // 16 // 3 * 16 if rows >= 96 else rows
    cuts = [(i, min(i + step, rows)) for i in range(0, rows, step)]

    def kernel(total_ref, back_ref, *refs):
        buffer, sems = refs[-2:]
        result_ref = refs[-4] if mark else refs[-3]
        copies = []
        for i, (a, b) in enumerate(cuts):
            buffer[a:b, :] = (total_ref[lo + a : lo + b, :] + back_ref[a:b, :].astype(jnp.float32)).astype(jnp.bfloat16)
            copies.append(
                pltpu.make_async_copy(
                    buffer.at[pl.ds(a, b - a), :], result_ref.at[pl.ds(lo + a, b - a), :], sems.at[i]
                )
            )
            copies[-1].start()
        if mark:
            refs[-3][...] = jnp.zeros((8, 128), jnp.float32)
        for copy in copies:
            copy.wait()

    kept = [] if result is None else [result]
    out = jax.ShapeDtypeStruct(total.shape, jnp.bfloat16)
    return pl.pallas_call(
        kernel,
        out_shape=(out, jax.ShapeDtypeStruct((8, 128), jnp.float32)) if mark else out,
        in_specs=[VMEM, VMEM] + [HBM] * len(kept) + [ANY] * len(after),
        out_specs=(HBM, VMEM) if mark else HBM,
        scratch_shapes=[pltpu.VMEM((rows, width), jnp.bfloat16), pltpu.SemaphoreType.DMA((len(cuts),))],
        input_output_aliases={2: 0} if kept else {},
        compiler_params=pltpu.CompilerParams(vmem_limit_bytes=4 * MIB),
        name="add_rows",
    )(total, back, *kept, *after)


def body(image, text, target, factor, shift):
    scale = factor[0]
    bias = shift[0]
    cuts = row_cuts(text.shape[0])
    part = [shifted(rows, "blk", 1) for rows in fetch(text, cuts[:2], [], ANY, 60 * MIB)]
    image_next = shifted(image, "grp", -1)

    [target] = fetch(target, [(0, 1)], [part[0]], VMEM, MIB)
    [rows] = fetch(text, cuts[2:3], [target], VMEM, 2 * MIB)
    part.append(shifted(rows, "blk", 1))
    own = jax.nn.sigmoid(dot_nt(image, text) * scale + bias)
    column = lax.broadcasted_iota(jnp.int32, own.shape, 1)
    own = (own - (column == target[0][:, None]).astype(jnp.float32)).astype(jnp.bfloat16)
    [rows] = fetch(text, cuts[3:], [own], VMEM, 2 * MIB)
    part.append(shifted(rows, "blk", 1))
    image_grad = dot_nn(own, text)
    text_grad = dot_tn(own, image)

    image_next = pass_on(image_next, [image_grad, text_grad])
    sent0, part0, own0, next0 = chunk(factor, shift, image, image_next, part[0], part[1], [])
    next_own = jax.nn.sigmoid(dot_nt(image_next, text) * scale + bias).astype(jnp.bfloat16)
    text_grad = scale * (text_grad + dot_tn(next_own, image_next))
    image_sent = dot_nn(next_own, text) + dot_tn(next0, part0)
    image_grad = image_grad + dot_tn(own0, part0)

    sent0 = pass_on(sent0, [part[2], image_sent])
    back0 = shifted(sent0, "blk", -1)

    sent1, part1, own1, next1 = chunk(factor, shift, image, image_next, part[2], part[3], [sent0])
    image_sent = (scale * (image_sent + dot_tn(next1, part1))).astype(jnp.bfloat16)
    image_back = shifted(image_sent, "grp", 1)
    sent1 = pass_on(sent1, [image_sent])
    back1 = shifted(sent1, "blk", -1)
    image_grad = scale * (image_grad + dot_tn(own1, part1))

    result = add_rows(text_grad, back0, 0, None, [])
    image_grad, mark = add_rows(image_grad, image_back, 0, None, [], mark=True)
    result = add_rows(text_grad, back1, cuts[2][0], result, [mark])
    return image_grad, result


def solution(mesh):
    block = P(("blk", "grp"), None)
    return jax.shard_map(
        body, mesh=mesh, in_specs=(block, block, block, P(), P()), out_specs=(block, block), check_vma=False
    )
```

```python
import functools

import jax
import jax.numpy as jnp
from jax import lax
from jax.experimental import pallas as pl
from jax.experimental.pallas import tpu as pltpu
from jax.sharding import PartitionSpec as P

MIB = 2**20
ENDS = (6, 16, 18, 23)
SMEM = pl.BlockSpec(memory_space=pltpu.SMEM)
VMEM = pl.BlockSpec(memory_space=pltpu.VMEM)
HBM = pl.BlockSpec(memory_space=pltpu.HBM)
ANY = pl.BlockSpec(memory_space=pl.ANY)


def shifted(shard, axis, by):
    devices = lax.axis_size(axis)
    return lax.ppermute(shard, axis, [(i, (i + by) % devices) for i in range(devices)])


def dot_nt(a, b):
    return lax.dot_general(a, b, (((1,), (1,)), ((), ())), preferred_element_type=jnp.float32)


def dot_tn(a, b):
    return lax.dot_general(a, b, (((0,), (0,)), ((), ())), preferred_element_type=jnp.float32)


def dot_nn(a, b):
    return jnp.dot(a, b, preferred_element_type=jnp.float32)


def row_cuts(rows):
    tiles = rows // 16
    cuts = [0] + [tiles * ends // 26 * 16 for ends in ENDS] + [rows]
    return list(zip(cuts[:-1], cuts[1:]))


def shifted_with_relay(shard, axis, order):
    devices = lax.axis_size(axis)
    near = lax.ppermute(shard, axis, [(i, i + 1) for i in range(devices - 1)])
    relay = lax.ppermute(shard, axis, [(devices - 1, devices - 2)])
    far = lax.ppermute(order(relay), axis, [(devices - 2, 0)])
    return near, far


def fetch(array, lo, hi, after):
    def kernel(array_ref, *refs):
        out_ref, sem = refs[-2:]
        copy = pltpu.make_async_copy(array_ref.at[pl.ds(lo, hi - lo), :], out_ref, sem)
        copy.start()
        copy.wait()

    return pl.pallas_call(
        kernel,
        out_shape=jax.ShapeDtypeStruct((hi - lo, array.shape[1]), array.dtype),
        in_specs=[ANY] * (1 + len(after)),
        out_specs=VMEM,
        scratch_shapes=[pltpu.SemaphoreType.DMA],
        compiler_params=pltpu.CompilerParams(vmem_limit_bytes=2 * MIB),
        name="fetch",
    )(array, *after)


def pass_on(array, after):
    return pl.pallas_call(
        lambda *refs: None,
        out_shape=jax.ShapeDtypeStruct(array.shape, array.dtype),
        in_specs=[ANY] * (1 + len(after)),
        out_specs=ANY,
        input_output_aliases={0: 0},
        compiler_params=pltpu.CompilerParams(vmem_limit_bytes=MIB),
        name="pass_on",
    )(array, *after)


def chunk_kernel(lows, scale_ref, bias_ref, image_ref, next_ref, *refs):
    sent_ref, joined_ref, own_ref, other_ref = refs[-4:]
    scale, bias = scale_ref[0], bias_ref[0]
    for i, lo in enumerate(lows):
        rows = pl.ds(lo, refs[i].shape[0])
        if lo in lows[:i]:
            joined_ref[rows, :] += refs[i][...]
        else:
            joined_ref[rows, :] = refs[i][...]
    part = joined_ref[...]
    image = image_ref[...]
    own = jax.nn.sigmoid(dot_nt(part, image) * scale + bias).astype(jnp.bfloat16)
    own_ref[...] = own
    total = dot_nn(own, image)
    image = next_ref[...]
    other = jax.nn.sigmoid(dot_nt(part, image) * scale + bias).astype(jnp.bfloat16)
    other_ref[...] = other
    total += dot_nn(other, image)
    sent_ref[...] = (scale * total).astype(jnp.bfloat16)


def chunk(factor, shift, image, image_next, pieces, after):
    width = image.shape[1]
    columns = image.shape[0]
    rows = max(lo + piece.shape[0] for lo, piece in pieces)
    text = jax.ShapeDtypeStruct((rows, width), jnp.bfloat16)
    tile = jax.ShapeDtypeStruct((rows, columns), jnp.bfloat16)
    return pl.pallas_call(
        functools.partial(chunk_kernel, [lo for lo, _ in pieces]),
        out_shape=(text, text, tile, tile),
        in_specs=[SMEM] * 2 + [VMEM] * (2 + len(pieces)) + [ANY] * len(after),
        out_specs=(VMEM,) * 4,
        compiler_params=pltpu.CompilerParams(vmem_limit_bytes=16 * MIB),
        cost_estimate=pl.CostEstimate(
            flops=8 * rows * columns * width,
            bytes_accessed=2 * (2 * columns + 3 * rows) * width,
            transcendentals=2 * rows * columns,
        ),
        name="chunk",
    )(factor, shift, image, image_next, *[piece for _, piece in pieces], *after)


def add_rows(total, back, lo, result, after, mark=False):
    rows, width = back.shape
    step = rows // 16 // 3 * 16 if rows >= 96 else rows
    cuts = [(i, min(i + step, rows)) for i in range(0, rows, step)]

    def kernel(total_ref, back_ref, *refs):
        buffer, sems = refs[-2:]
        result_ref = refs[-4] if mark else refs[-3]
        copies = []
        for i, (a, b) in enumerate(cuts):
            buffer[a:b, :] = (total_ref[lo + a : lo + b, :] + back_ref[a:b, :].astype(jnp.float32)).astype(jnp.bfloat16)
            copies.append(
                pltpu.make_async_copy(
                    buffer.at[pl.ds(a, b - a), :], result_ref.at[pl.ds(lo + a, b - a), :], sems.at[i]
                )
            )
            copies[-1].start()
        if mark:
            refs[-3][...] = jnp.zeros((8, 128), jnp.float32)
        for copy in copies:
            copy.wait()

    kept = [] if result is None else [result]
    out = jax.ShapeDtypeStruct(total.shape, jnp.bfloat16)
    return pl.pallas_call(
        kernel,
        out_shape=(out, jax.ShapeDtypeStruct((8, 128), jnp.float32)) if mark else out,
        in_specs=[VMEM, VMEM] + [HBM] * len(kept) + [ANY] * len(after),
        out_specs=(HBM, VMEM) if mark else HBM,
        scratch_shapes=[pltpu.VMEM((rows, width), jnp.bfloat16), pltpu.SemaphoreType.DMA((len(cuts),))],
        input_output_aliases={2: 0} if kept else {},
        compiler_params=pltpu.CompilerParams(vmem_limit_bytes=4 * MIB),
        name="add_rows",
    )(total, back, *kept, *after)


def body(image, text, target, factor, shift):
    scale = factor[0]
    bias = shift[0]
    cuts = row_cuts(text.shape[0])
    first = text[: cuts[0][1]]
    part = [shifted(first, "blk", 1)]
    image_next = shifted(image, "grp", -1)
    part.append(shifted(fetch(text, *cuts[1], [first]), "blk", 1))

    target = fetch(target, 0, 1, [part[0]])
    relayed = fetch(text, *cuts[2], [target])
    own = jax.nn.sigmoid(dot_nt(image, text) * scale + bias)
    column = lax.broadcasted_iota(jnp.int32, own.shape, 1)
    own = (own - (column == target[0][:, None]).astype(jnp.float32)).astype(jnp.bfloat16)
    rows = fetch(text, *cuts[3], [own])
    image_grad = dot_nn(own, text)
    text_grad = dot_tn(own, image)
    near, far = shifted_with_relay(relayed, "blk", lambda relay: pass_on(relay, [image_grad, text_grad]))
    part.append(shifted(rows, "blk", 1))
    part.append(shifted(fetch(text, *cuts[4], [text_grad]), "blk", 1))

    image_next = pass_on(image_next, [image_grad, text_grad])
    sent0, part0, own0, next0 = chunk(
        factor, shift, image, image_next, [(0, part[0]), (cuts[1][0], part[1])], []
    )
    next_own = jax.nn.sigmoid(dot_nt(image_next, text) * scale + bias).astype(jnp.bfloat16)
    text_grad = scale * (text_grad + dot_tn(next_own, image_next))
    image_sent = dot_nn(next_own, text) + dot_tn(next0, part0)
    image_grad = image_grad + dot_tn(own0, part0)

    sent0 = pass_on(sent0, [part[2], image_sent])
    back0 = shifted(sent0, "blk", -1)

    base = cuts[2][0]
    pieces = [(0, near), (0, far), (cuts[3][0] - base, part[2]), (cuts[4][0] - base, part[3])]
    sent1, part1, own1, next1 = chunk(factor, shift, image, image_next, pieces, [sent0])
    image_sent = (scale * (image_sent + dot_tn(next1, part1))).astype(jnp.bfloat16)
    image_back = shifted(image_sent, "grp", 1)
    sent1 = pass_on(sent1, [image_sent])
    back1 = shifted(sent1, "blk", -1)
    image_grad = scale * (image_grad + dot_tn(own1, part1))

    result = add_rows(text_grad, back0, 0, None, [])
    image_grad, mark = add_rows(image_grad, image_back, 0, None, [], mark=True)
    result = add_rows(text_grad, back1, cuts[2][0], result, [mark])
    return image_grad, result


def solution(mesh):
    block = P(("blk", "grp"), None)
    return jax.shard_map(
        body, mesh=mesh, in_specs=(block, block, block, P(), P()), out_specs=(block, block), check_vma=False
    )
```

```python
import functools

import jax
import jax.numpy as jnp
from jax import lax
from jax.experimental import pallas as pl
from jax.experimental.pallas import tpu as pltpu
from jax.sharding import PartitionSpec as P

MIB = 2**20
APART = 32
SMEM = pl.BlockSpec(memory_space=pltpu.SMEM)
VMEM = pl.BlockSpec(memory_space=pltpu.VMEM)
HBM = pl.BlockSpec(memory_space=pltpu.HBM)
ANY = pl.BlockSpec(memory_space=pl.ANY)


def shifted(shard, axis, by):
    devices = lax.axis_size(axis)
    return lax.ppermute(shard, axis, [(i, (i + by) % devices) for i in range(devices)])


def dot_nt(a, b):
    return lax.dot_general(a, b, (((1,), (1,)), ((), ())), preferred_element_type=jnp.float32)


def dot_tn(a, b):
    return lax.dot_general(a, b, (((0,), (0,)), ((), ())), preferred_element_type=jnp.float32)


def dot_nn(a, b):
    return jnp.dot(a, b, preferred_element_type=jnp.float32)


def row_cuts(rows):
    tiles = rows // 16
    cuts = [0] + [tiles * ends // 26 * 16 for ends in (6, 16, 23)] + [rows]
    return list(zip(cuts[:-1], cuts[1:]))


def fetch(array, lo, hi, after):
    def kernel(array_ref, *refs):
        out_ref, sem = refs[-2:]
        copy = pltpu.make_async_copy(array_ref.at[pl.ds(lo, hi - lo), :], out_ref, sem)
        copy.start()
        copy.wait()

    return pl.pallas_call(
        kernel,
        out_shape=jax.ShapeDtypeStruct((hi - lo, array.shape[1]), array.dtype),
        in_specs=[ANY] * (1 + len(after)),
        out_specs=VMEM,
        scratch_shapes=[pltpu.SemaphoreType.DMA],
        compiler_params=pltpu.CompilerParams(vmem_limit_bytes=2 * MIB),
        name="fetch",
    )(array, *after)


def pass_on(array, after):
    return pl.pallas_call(
        lambda *refs: None,
        out_shape=jax.ShapeDtypeStruct(array.shape, array.dtype),
        in_specs=[ANY] * (1 + len(after)),
        out_specs=ANY,
        input_output_aliases={0: 0},
        compiler_params=pltpu.CompilerParams(vmem_limit_bytes=MIB),
        name="pass_on",
    )(array, *after)


def chunk_kernel(apart, scale_ref, bias_ref, image_ref, next_ref, upper_ref, lower_ref, *refs):
    joined_ref, own_ref, other_ref, *sent_refs = refs[-4 - bool(apart) :]
    scale, bias = scale_ref[0], bias_ref[0]
    rows = upper_ref.shape[0]
    joined_ref[:rows, :] = upper_ref[...]
    joined_ref[rows:, :] = lower_ref[...]
    part = joined_ref[...]
    image = image_ref[...]
    own = jax.nn.sigmoid(dot_nt(part, image) * scale + bias).astype(jnp.bfloat16)
    own_ref[...] = own
    total = dot_nn(own, image)
    image = next_ref[...]
    other = jax.nn.sigmoid(dot_nt(part, image) * scale + bias).astype(jnp.bfloat16)
    other_ref[...] = other
    total += dot_nn(other, image)
    total = (scale * total).astype(jnp.bfloat16)
    start = 0
    for sent_ref in sent_refs:
        sent_ref[...] = total[start : start + sent_ref.shape[0], :]
        start += sent_ref.shape[0]


def chunk(factor, shift, image, image_next, upper, lower, after, apart=0):
    rows, width = upper.shape[0] + lower.shape[0], upper.shape[1]
    columns = image.shape[0]
    tile = jax.ShapeDtypeStruct((rows, columns), jnp.bfloat16)
    shapes = [jax.ShapeDtypeStruct((rows, width), jnp.bfloat16), tile, tile]
    shapes += [jax.ShapeDtypeStruct((r, width), jnp.bfloat16) for r in (rows - apart, apart) if r]
    return pl.pallas_call(
        functools.partial(chunk_kernel, apart),
        out_shape=shapes,
        in_specs=[SMEM] * 2 + [VMEM] * 4 + [ANY] * len(after),
        out_specs=[VMEM] * len(shapes),
        compiler_params=pltpu.CompilerParams(vmem_limit_bytes=16 * MIB),
        cost_estimate=pl.CostEstimate(
            flops=8 * rows * columns * width,
            bytes_accessed=2 * (2 * columns + 3 * rows) * width,
            transcendentals=2 * rows * columns,
        ),
        name="chunk",
    )(factor, shift, image, image_next, upper, lower, *after)


def add_rows(total, pieces, result, after, mark=False):
    width = total.shape[1]
    arrays = [array for _, backs in pieces for array in backs]
    steps = []
    first = 0
    for lo, backs in pieces:
        rows = backs[0].shape[0]
        step = rows // 16 // 3 * 16 if rows >= 96 else rows
        for start in range(0, rows, step):
            stop = min(start + step, rows)
            steps.append((lo, start, stop, range(first, first + len(backs))))
        first += len(backs)
    low = min(lo for lo, _ in pieces)
    high = max(lo + backs[0].shape[0] for lo, backs in pieces)

    def kernel(total_ref, *refs):
        buffer, sems = refs[-2:]
        result_ref = refs[-4] if mark else refs[-3]
        copies = []
        for i, (lo, start, stop, backs) in enumerate(steps):
            rows = total_ref[lo + start : lo + stop, :]
            for back in backs:
                rows += refs[back][start:stop, :].astype(jnp.float32)
            held = buffer.at[pl.ds(lo + start - low, stop - start), :]
            held[...] = rows.astype(jnp.bfloat16)
            copies.append(
                pltpu.make_async_copy(held, result_ref.at[pl.ds(lo + start, stop - start), :], sems.at[i])
            )
            copies[-1].start()
        if mark:
            refs[-3][...] = jnp.zeros((8, 128), jnp.float32)
        for copy in copies:
            copy.wait()

    kept = [] if result is None else [result]
    out = jax.ShapeDtypeStruct(total.shape, jnp.bfloat16)
    return pl.pallas_call(
        kernel,
        out_shape=(out, jax.ShapeDtypeStruct((8, 128), jnp.float32)) if mark else out,
        in_specs=[VMEM] * (1 + len(arrays)) + [HBM] * len(kept) + [ANY] * len(after),
        out_specs=(HBM, VMEM) if mark else HBM,
        scratch_shapes=[pltpu.VMEM((high - low, width), jnp.bfloat16), pltpu.SemaphoreType.DMA((len(steps),))],
        input_output_aliases={1 + len(arrays): 0} if kept else {},
        compiler_params=pltpu.CompilerParams(vmem_limit_bytes=4 * MIB),
        name="add_rows",
    )(total, *arrays, *kept, *after)


def body(image, text, target, factor, shift):
    scale = factor[0]
    bias = shift[0]
    cuts = row_cuts(text.shape[0])
    first = text[: cuts[0][1]]
    part = [shifted(first, "blk", 1)]
    image_next = shifted(image, "grp", -1)
    part.append(shifted(fetch(text, *cuts[1], [first]), "blk", 1))

    target = fetch(target, 0, 1, [part[0]])
    part.append(shifted(fetch(text, *cuts[2], [target]), "blk", 1))
    own = jax.nn.sigmoid(dot_nt(image, text) * scale + bias)
    column = lax.broadcasted_iota(jnp.int32, own.shape, 1)
    own = (own - (column == target[0][:, None]).astype(jnp.float32)).astype(jnp.bfloat16)
    part.append(shifted(fetch(text, *cuts[3], [own]), "blk", 1))
    image_grad = dot_nn(own, text)
    text_grad = dot_tn(own, image)

    image_next = pass_on(image_next, [image_grad, text_grad])
    part0, own0, next0, sent0, apart = chunk(factor, shift, image, image_next, part[0], part[1], [], apart=APART)
    next_own = jax.nn.sigmoid(dot_nt(image_next, text) * scale + bias).astype(jnp.bfloat16)
    text_grad = scale * (text_grad + dot_tn(next_own, image_next))
    image_sent = dot_nn(next_own, text) + dot_tn(next0, part0)
    image_grad = image_grad + dot_tn(own0, part0)

    devices = lax.axis_size("blk")
    sent0, apart = pass_on(sent0, [part[2], image_sent]), pass_on(apart, [part[2], image_sent])
    back0 = shifted(sent0, "blk", -1)
    half_way = lax.ppermute(apart, "blk", [(1, 2)])
    near = lax.ppermute(apart, "blk", [(i, (i - 1) % devices) for i in range(devices) if i != 1])

    part1, own1, next1, sent1 = chunk(factor, shift, image, image_next, part[2], part[3], [sent0, half_way])
    image_sent = (scale * (image_sent + dot_tn(next1, part1))).astype(jnp.bfloat16)
    image_back = shifted(image_sent, "grp", 1)
    sent1 = pass_on(sent1, [image_sent])
    back1 = shifted(sent1, "blk", -1)
    far = lax.ppermute(half_way, "blk", [(2, 0)])
    image_grad = scale * (image_grad + dot_tn(own1, part1))

    result = add_rows(text_grad, [(0, [back0]), (cuts[2][0] - APART, [near, far])], None, [])
    image_grad, mark = add_rows(image_grad, [(0, [image_back])], None, [], mark=True)
    result = add_rows(text_grad, [(cuts[2][0], [back1])], result, [mark])
    return image_grad, result


def solution(mesh):
    block = P(("blk", "grp"), None)
    return jax.shard_map(
        body, mesh=mesh, in_specs=(block, block, block, P(), P()), out_specs=(block, block), check_vma=False
    )
```

```python
import functools

import jax
import jax.numpy as jnp
from jax import lax
from jax.experimental import pallas as pl
from jax.experimental.pallas import tpu as pltpu
from jax.sharding import PartitionSpec as P

MIB = 2**20
ENDS = (6, 16, 21, 23)
SMEM = pl.BlockSpec(memory_space=pltpu.SMEM)
VMEM = pl.BlockSpec(memory_space=pltpu.VMEM)
HBM = pl.BlockSpec(memory_space=pltpu.HBM)
ANY = pl.BlockSpec(memory_space=pl.ANY)


def shifted(shard, axis, by):
    devices = lax.axis_size(axis)
    return lax.ppermute(shard, axis, [(i, (i + by) % devices) for i in range(devices)])


def dot_nt(a, b):
    return lax.dot_general(a, b, (((1,), (1,)), ((), ())), preferred_element_type=jnp.float32)


def dot_tn(a, b):
    return lax.dot_general(a, b, (((0,), (0,)), ((), ())), preferred_element_type=jnp.float32)


def dot_nn(a, b):
    return jnp.dot(a, b, preferred_element_type=jnp.float32)


def row_cuts(rows):
    tiles = rows // 16
    cuts = [0] + [tiles * ends // 26 * 16 for ends in ENDS] + [rows]
    return list(zip(cuts[:-1], cuts[1:]))


def fetch(array, lo, hi, after):
    def kernel(array_ref, *refs):
        out_ref, sem = refs[-2:]
        copy = pltpu.make_async_copy(array_ref.at[pl.ds(lo, hi - lo), :], out_ref, sem)
        copy.start()
        copy.wait()

    return pl.pallas_call(
        kernel,
        out_shape=jax.ShapeDtypeStruct((hi - lo, array.shape[1]), array.dtype),
        in_specs=[ANY] * (1 + len(after)),
        out_specs=VMEM,
        scratch_shapes=[pltpu.SemaphoreType.DMA],
        compiler_params=pltpu.CompilerParams(vmem_limit_bytes=2 * MIB),
        name="fetch",
    )(array, *after)


def pass_on(array, after):
    return pl.pallas_call(
        lambda *refs: None,
        out_shape=jax.ShapeDtypeStruct(array.shape, array.dtype),
        in_specs=[ANY] * (1 + len(after)),
        out_specs=ANY,
        input_output_aliases={0: 0},
        compiler_params=pltpu.CompilerParams(vmem_limit_bytes=MIB),
        name="pass_on",
    )(array, *after)


def chunk_kernel(lows, scale_ref, bias_ref, image_ref, next_ref, *refs):
    sent_ref, joined_ref, own_ref, other_ref = refs[-4:]
    scale, bias = scale_ref[0], bias_ref[0]
    for i, lo in enumerate(lows):
        rows = pl.ds(lo, refs[i].shape[0])
        if lo in lows[:i]:
            joined_ref[rows, :] += refs[i][...]
        else:
            joined_ref[rows, :] = refs[i][...]
    part = joined_ref[...]
    image = image_ref[...]
    own = jax.nn.sigmoid(dot_nt(part, image) * scale + bias).astype(jnp.bfloat16)
    own_ref[...] = own
    total = dot_nn(own, image)
    image = next_ref[...]
    other = jax.nn.sigmoid(dot_nt(part, image) * scale + bias).astype(jnp.bfloat16)
    other_ref[...] = other
    total += dot_nn(other, image)
    sent_ref[...] = (scale * total).astype(jnp.bfloat16)


def chunk(factor, shift, image, image_next, pieces, after):
    width = image.shape[1]
    columns = image.shape[0]
    rows = max(lo + piece.shape[0] for lo, piece in pieces)
    text = jax.ShapeDtypeStruct((rows, width), jnp.bfloat16)
    tile = jax.ShapeDtypeStruct((rows, columns), jnp.bfloat16)
    return pl.pallas_call(
        functools.partial(chunk_kernel, [lo for lo, _ in pieces]),
        out_shape=(text, text, tile, tile),
        in_specs=[SMEM] * 2 + [VMEM] * (2 + len(pieces)) + [ANY] * len(after),
        out_specs=(VMEM,) * 4,
        compiler_params=pltpu.CompilerParams(vmem_limit_bytes=16 * MIB),
        cost_estimate=pl.CostEstimate(
            flops=8 * rows * columns * width,
            bytes_accessed=2 * (2 * columns + 3 * rows) * width,
            transcendentals=2 * rows * columns,
        ),
        name="chunk",
    )(factor, shift, image, image_next, *[piece for _, piece in pieces], *after)


def add_rows(total, back, lo, result, after, mark=False):
    rows, width = back.shape
    step = rows // 16 // 3 * 16 if rows >= 96 else rows
    cuts = [(i, min(i + step, rows)) for i in range(0, rows, step)]

    def kernel(total_ref, back_ref, *refs):
        buffer, sems = refs[-2:]
        result_ref = refs[-4] if mark else refs[-3]
        copies = []
        for i, (a, b) in enumerate(cuts):
            buffer[a:b, :] = (total_ref[lo + a : lo + b, :] + back_ref[a:b, :].astype(jnp.float32)).astype(jnp.bfloat16)
            copies.append(
                pltpu.make_async_copy(
                    buffer.at[pl.ds(a, b - a), :], result_ref.at[pl.ds(lo + a, b - a), :], sems.at[i]
                )
            )
            copies[-1].start()
        if mark:
            refs[-3][...] = jnp.zeros((8, 128), jnp.float32)
        for copy in copies:
            copy.wait()

    kept = [] if result is None else [result]
    out = jax.ShapeDtypeStruct(total.shape, jnp.bfloat16)
    return pl.pallas_call(
        kernel,
        out_shape=(out, jax.ShapeDtypeStruct((8, 128), jnp.float32)) if mark else out,
        in_specs=[VMEM, VMEM] + [HBM] * len(kept) + [ANY] * len(after),
        out_specs=(HBM, VMEM) if mark else HBM,
        scratch_shapes=[pltpu.VMEM((rows, width), jnp.bfloat16), pltpu.SemaphoreType.DMA((len(cuts),))],
        input_output_aliases={2: 0} if kept else {},
        compiler_params=pltpu.CompilerParams(vmem_limit_bytes=4 * MIB),
        name="add_rows",
    )(total, back, *kept, *after)


def body(image, text, target, factor, shift):
    scale = factor[0]
    bias = shift[0]
    cuts = row_cuts(text.shape[0])
    first = text[: cuts[0][1]]
    part = [shifted(first, "blk", 1)]
    devices = lax.axis_size("blk")
    relayed = fetch(text, *cuts[3], [first])
    half_way = lax.ppermute(relayed, "blk", [(devices - 1, devices - 2)])
    image_next = shifted(image, "grp", -1)
    part.append(shifted(fetch(text, *cuts[1], [relayed]), "blk", 1))

    target = fetch(target, 0, 1, [part[0], half_way])
    far = lax.ppermute(half_way, "blk", [(devices - 2, 0)])
    own = jax.nn.sigmoid(dot_nt(image, text) * scale + bias)
    column = lax.broadcasted_iota(jnp.int32, own.shape, 1)
    own = (own - (column == target[0][:, None]).astype(jnp.float32)).astype(jnp.bfloat16)
    part.append(shifted(fetch(text, *cuts[2], [own]), "blk", 1))
    image_grad = dot_nn(own, text)
    text_grad = dot_tn(own, image)
    relayed = pass_on(relayed, [image_grad, text_grad])
    near = lax.ppermute(relayed, "blk", [(i, i + 1) for i in range(devices - 1)])
    part.append(shifted(fetch(text, *cuts[4], [relayed]), "blk", 1))

    image_next = pass_on(image_next, [image_grad, text_grad])
    sent0, part0, own0, next0 = chunk(
        factor, shift, image, image_next, [(0, part[0]), (cuts[1][0], part[1])], []
    )
    next_own = jax.nn.sigmoid(dot_nt(image_next, text) * scale + bias).astype(jnp.bfloat16)
    text_grad = scale * (text_grad + dot_tn(next_own, image_next))
    image_sent = dot_nn(next_own, text) + dot_tn(next0, part0)
    image_grad = image_grad + dot_tn(own0, part0)

    sent0 = pass_on(sent0, [part[2], near, far, image_sent])
    back0 = shifted(sent0, "blk", -1)

    base = cuts[2][0]
    pieces = [(0, part[2]), (cuts[3][0] - base, near), (cuts[3][0] - base, far), (cuts[4][0] - base, part[3])]
    sent1, part1, own1, next1 = chunk(factor, shift, image, image_next, pieces, [sent0])
    image_sent = (scale * (image_sent + dot_tn(next1, part1))).astype(jnp.bfloat16)
    image_back = shifted(image_sent, "grp", 1)
    sent1 = pass_on(sent1, [image_sent])
    back1 = shifted(sent1, "blk", -1)
    image_grad = scale * (image_grad + dot_tn(own1, part1))

    result = add_rows(text_grad, back0, 0, None, [])
    image_grad, mark = add_rows(image_grad, image_back, 0, None, [], mark=True)
    result = add_rows(text_grad, back1, cuts[2][0], result, [mark])
    return image_grad, result


def solution(mesh):
    block = P(("blk", "grp"), None)
    return jax.shard_map(
        body, mesh=mesh, in_specs=(block, block, block, P(), P()), out_specs=(block, block), check_vma=False
    )
```

```python
import functools

import jax
import jax.numpy as jnp
from jax import lax
from jax.experimental import pallas as pl
from jax.experimental.pallas import tpu as pltpu
from jax.sharding import PartitionSpec as P

MIB = 2**20
FIRST = 10
WAIT = 10**10
SMEM = pl.BlockSpec(memory_space=pltpu.SMEM)
VMEM = pl.BlockSpec(memory_space=pltpu.VMEM)
HBM = pl.BlockSpec(memory_space=pltpu.HBM)
ANY = pl.BlockSpec(memory_space=pl.ANY)


def shifted(shard, axis, by):
    devices = lax.axis_size(axis)
    return lax.ppermute(shard, axis, [(i, (i + by) % devices) for i in range(devices)])


def dot_nt(a, b):
    return lax.dot_general(a, b, (((1,), (1,)), ((), ())), preferred_element_type=jnp.float32)


def dot_tn(a, b):
    return lax.dot_general(a, b, (((0,), (0,)), ((), ())), preferred_element_type=jnp.float32)


def dot_nn(a, b):
    return jnp.dot(a, b, preferred_element_type=jnp.float32)


def shifted_half(shard, by, parity):
    blocks, groups = lax.axis_size("blk"), lax.axis_size("grp")
    pairs = [
        (b * groups + g, (b + by) % blocks * groups + g) for b in range(blocks) for g in range(parity, groups, 2)
    ]
    return lax.ppermute(shard, ("blk", "grp"), pairs)


def fetch(array, lo, hi, after):
    def kernel(array_ref, *refs):
        out_ref, sem = refs[-2:]
        copy = pltpu.make_async_copy(array_ref.at[pl.ds(lo, hi - lo), :], out_ref, sem)
        copy.start()
        copy.wait()

    return pl.pallas_call(
        kernel,
        out_shape=jax.ShapeDtypeStruct((hi - lo, array.shape[1]), array.dtype),
        in_specs=[ANY] * (1 + len(after)),
        out_specs=VMEM,
        scratch_shapes=[pltpu.SemaphoreType.DMA],
        compiler_params=pltpu.CompilerParams(vmem_limit_bytes=2 * MIB),
        name="fetch",
    )(array, *after)


def pass_on(array, after, flops=0):
    return pl.pallas_call(
        lambda *refs: None,
        out_shape=jax.ShapeDtypeStruct(array.shape, array.dtype),
        in_specs=[ANY] * (1 + len(after)),
        out_specs=ANY,
        input_output_aliases={0: 0},
        compiler_params=pltpu.CompilerParams(vmem_limit_bytes=MIB),
        cost_estimate=pl.CostEstimate(flops=flops, bytes_accessed=0, transcendentals=0),
        name="pass_on",
    )(array, *after)


def chunk_kernel(lo, scale_ref, bias_ref, image_ref, next_ref, even_ref, odd_ref, *refs):
    sent_ref, part_ref, own_ref, other_ref = refs[-4:]
    scale, bias = scale_ref[0], bias_ref[0]
    rows = pl.ds(lo, part_ref.shape[0])
    part = even_ref[rows, :] + odd_ref[rows, :]
    part_ref[...] = part
    image = image_ref[...]
    own = jax.nn.sigmoid(dot_nt(part, image) * scale + bias).astype(jnp.bfloat16)
    own_ref[...] = own
    total = dot_nn(own, image)
    image = next_ref[...]
    other = jax.nn.sigmoid(dot_nt(part, image) * scale + bias).astype(jnp.bfloat16)
    other_ref[...] = other
    total += dot_nn(other, image)
    sent_ref[...] = (scale * total).astype(jnp.bfloat16)


def chunk(factor, shift, image, image_next, texts, lo, hi, after):
    rows, (columns, width) = hi - lo, image.shape
    text = jax.ShapeDtypeStruct((rows, width), jnp.bfloat16)
    tile = jax.ShapeDtypeStruct((rows, columns), jnp.bfloat16)
    return pl.pallas_call(
        functools.partial(chunk_kernel, lo),
        out_shape=(text, text, tile, tile),
        in_specs=[SMEM] * 2 + [VMEM] * 4 + [ANY] * len(after),
        out_specs=(VMEM,) * 4,
        compiler_params=pltpu.CompilerParams(vmem_limit_bytes=16 * MIB),
        cost_estimate=pl.CostEstimate(
            flops=8 * rows * columns * width,
            bytes_accessed=2 * (2 * columns + 4 * rows) * width,
            transcendentals=2 * rows * columns,
        ),
        name="chunk",
    )(factor, shift, image, image_next, *texts, *after)


def add_rows(total, pieces, result, after, mark=False):
    width = total.shape[1]
    arrays = [array for _, backs in pieces for array in backs]
    steps = []
    first = 0
    for lo, backs in pieces:
        rows = backs[0].shape[0]
        step = rows // 16 // 3 * 16 if rows >= 96 else rows
        for start in range(0, rows, step):
            stop = min(start + step, rows)
            steps.append((lo, start, stop, range(first, first + len(backs))))
        first += len(backs)
    low = min(lo for lo, _ in pieces)
    high = max(lo + backs[0].shape[0] for lo, backs in pieces)

    def kernel(total_ref, *refs):
        buffer, sems = refs[-2:]
        result_ref = refs[-4] if mark else refs[-3]
        copies = []
        for i, (lo, start, stop, backs) in enumerate(steps):
            rows = total_ref[lo + start : lo + stop, :]
            for back in backs:
                rows += refs[back][start:stop, :].astype(jnp.float32)
            held = buffer.at[pl.ds(lo + start - low, stop - start), :]
            held[...] = rows.astype(jnp.bfloat16)
            copies.append(
                pltpu.make_async_copy(held, result_ref.at[pl.ds(lo + start, stop - start), :], sems.at[i])
            )
            copies[-1].start()
        if mark:
            refs[-3][...] = jnp.zeros((8, 128), jnp.float32)
        for copy in copies:
            copy.wait()

    kept = [] if result is None else [result]
    out = jax.ShapeDtypeStruct(total.shape, jnp.bfloat16)
    return pl.pallas_call(
        kernel,
        out_shape=(out, jax.ShapeDtypeStruct((8, 128), jnp.float32)) if mark else out,
        in_specs=[VMEM] * (1 + len(arrays)) + [HBM] * len(kept) + [ANY] * len(after),
        out_specs=(HBM, VMEM) if mark else HBM,
        scratch_shapes=[pltpu.VMEM((high - low, width), jnp.bfloat16), pltpu.SemaphoreType.DMA((len(steps),))],
        input_output_aliases={1 + len(arrays): 0} if kept else {},
        compiler_params=pltpu.CompilerParams(vmem_limit_bytes=4 * MIB),
        name="add_rows",
    )(total, *arrays, *kept, *after)


def body(image, text, target, factor, shift):
    scale = factor[0]
    bias = shift[0]
    count = text.shape[0]
    cut = count // 16 * FIRST // 26 * 16
    even = shifted_half(text, 1, 0)
    image_next = shifted(image, "grp", -1)

    own = jax.nn.sigmoid(dot_nt(image, text) * scale + bias)
    column = lax.broadcasted_iota(jnp.int32, own.shape, 1)
    own = (own - (column == target[0][:, None]).astype(jnp.float32)).astype(jnp.bfloat16)
    odd = shifted_half(fetch(text, 0, count, [own]), 1, 1)
    image_grad = dot_nn(own, text)
    text_grad = dot_tn(own, image)

    even = pass_on(even, [image_grad, text_grad], WAIT)
    image_next = pass_on(image_next, [even])
    odd = pass_on(odd, [image_next])
    sent0, part0, own0, next0 = chunk(factor, shift, image, image_next, [even, odd], 0, cut, [])
    back0 = shifted(sent0, "blk", -1)

    image_next = pass_on(image_next, [sent0])
    sent1, part1, own1, next1 = chunk(factor, shift, image, image_next, [even, odd], cut, count, [])
    next_own = jax.nn.sigmoid(dot_nt(image_next, text) * scale + bias).astype(jnp.bfloat16)
    text_grad = scale * (text_grad + dot_tn(next_own, image_next))
    image_sent = dot_nn(next_own, text) + dot_tn(next0, part0)
    image_sent = (scale * (image_sent + dot_tn(next1, part1))).astype(jnp.bfloat16)
    image_back = shifted(image_sent, "grp", 1)
    back1 = shifted(sent1, "blk", -1)
    result, mark = add_rows(text_grad, [(0, [back0])], None, [], mark=True)
    own0, own1 = pass_on(own0, [mark]), pass_on(own1, [mark])
    image_grad = image_grad + dot_tn(own0, part0)
    image_grad = scale * (image_grad + dot_tn(own1, part1))
    image_grad, mark = add_rows(image_grad, [(0, [image_back])], None, [], mark=True)
    result = add_rows(text_grad, [(cut, [back1])], result, [mark])
    return image_grad, result


def solution(mesh):
    block = P(("blk", "grp"), None)
    return jax.shard_map(
        body, mesh=mesh, in_specs=(block, block, block, P(), P()), out_specs=(block, block), check_vma=False
    )
```

```python
import jax
import jax.numpy as jnp
from jax import lax
from jax.experimental import pallas as pl
from jax.experimental.pallas import tpu as pltpu
from jax.sharding import PartitionSpec as P

MIB = 2**20
SMEM = pl.BlockSpec(memory_space=pltpu.SMEM)
VMEM = pl.BlockSpec(memory_space=pltpu.VMEM)
HBM = pl.BlockSpec(memory_space=pltpu.HBM)
ANY = pl.BlockSpec(memory_space=pl.ANY)


def shifted(shard, axis, by):
    devices = lax.axis_size(axis)
    return lax.ppermute(shard, axis, [(i, (i + by) % devices) for i in range(devices)])


def dot_nt(a, b):
    return lax.dot_general(a, b, (((1,), (1,)), ((), ())), preferred_element_type=jnp.float32)


def dot_tn(a, b):
    return lax.dot_general(a, b, (((0,), (0,)), ((), ())), preferred_element_type=jnp.float32)


def dot_nn(a, b):
    return jnp.dot(a, b, preferred_element_type=jnp.float32)


def row_cuts(rows):
    tiles = rows // 16
    cuts = [0, tiles * 6 // 26 * 16, tiles * 16 // 26 * 16, tiles * 23 // 26 * 16, rows]
    return list(zip(cuts[:-1], cuts[1:]))


def fetch(array, lo, hi, after):
    def kernel(array_ref, *refs):
        out_ref, sem = refs[-2:]
        copy = pltpu.make_async_copy(array_ref.at[pl.ds(lo, hi - lo), :], out_ref, sem)
        copy.start()
        copy.wait()

    return pl.pallas_call(
        kernel,
        out_shape=jax.ShapeDtypeStruct((hi - lo, array.shape[1]), array.dtype),
        in_specs=[ANY] * (1 + len(after)),
        out_specs=VMEM,
        scratch_shapes=[pltpu.SemaphoreType.DMA],
        compiler_params=pltpu.CompilerParams(vmem_limit_bytes=2 * MIB),
        name="fetch",
    )(array, *after)


def pass_on(array, after):
    return pl.pallas_call(
        lambda *refs: None,
        out_shape=jax.ShapeDtypeStruct(array.shape, array.dtype),
        in_specs=[ANY] * (1 + len(after)),
        out_specs=ANY,
        input_output_aliases={0: 0},
        compiler_params=pltpu.CompilerParams(vmem_limit_bytes=MIB),
        name="pass_on",
    )(array, *after)


def chunk_kernel(scale_ref, bias_ref, image_ref, next_ref, upper_ref, lower_ref, *refs):
    sent_ref, joined_ref, own_ref, other_ref = refs[-4:]
    scale, bias = scale_ref[0], bias_ref[0]
    rows = upper_ref.shape[0]
    joined_ref[:rows, :] = upper_ref[...]
    joined_ref[rows:, :] = lower_ref[...]
    part = joined_ref[...]
    image = image_ref[...]
    own = jax.nn.sigmoid(dot_nt(part, image) * scale + bias).astype(jnp.bfloat16)
    own_ref[...] = own
    total = dot_nn(own, image)
    image = next_ref[...]
    other = jax.nn.sigmoid(dot_nt(part, image) * scale + bias).astype(jnp.bfloat16)
    other_ref[...] = other
    total += dot_nn(other, image)
    sent_ref[...] = (scale * total).astype(jnp.bfloat16)


def chunk(factor, shift, image, image_next, upper, lower, after):
    rows, width = upper.shape[0] + lower.shape[0], upper.shape[1]
    columns = image.shape[0]
    text = jax.ShapeDtypeStruct((rows, width), jnp.bfloat16)
    tile = jax.ShapeDtypeStruct((rows, columns), jnp.bfloat16)
    return pl.pallas_call(
        chunk_kernel,
        out_shape=(text, text, tile, tile),
        in_specs=[SMEM] * 2 + [VMEM] * 4 + [ANY] * len(after),
        out_specs=(VMEM,) * 4,
        compiler_params=pltpu.CompilerParams(vmem_limit_bytes=16 * MIB),
        cost_estimate=pl.CostEstimate(
            flops=8 * rows * columns * width,
            bytes_accessed=2 * (2 * columns + 3 * rows) * width,
            transcendentals=2 * rows * columns,
        ),
        name="chunk",
    )(factor, shift, image, image_next, upper, lower, *after)


def add_rows(total, back, lo, result, after, mark=False):
    rows, width = back.shape
    step = rows // 16 // 3 * 16 if rows >= 96 else rows
    cuts = [(i, min(i + step, rows)) for i in range(0, rows, step)]

    def kernel(total_ref, back_ref, *refs):
        buffer, sems = refs[-2:]
        result_ref = refs[-4] if mark else refs[-3]
        copies = []
        for i, (a, b) in enumerate(cuts):
            buffer[a:b, :] = (total_ref[lo + a : lo + b, :] + back_ref[a:b, :].astype(jnp.float32)).astype(jnp.bfloat16)
            copies.append(
                pltpu.make_async_copy(
                    buffer.at[pl.ds(a, b - a), :], result_ref.at[pl.ds(lo + a, b - a), :], sems.at[i]
                )
            )
            copies[-1].start()
        if mark:
            refs[-3][...] = jnp.zeros((8, 128), jnp.float32)
        for copy in copies:
            copy.wait()

    kept = [] if result is None else [result]
    out = jax.ShapeDtypeStruct(total.shape, jnp.bfloat16)
    return pl.pallas_call(
        kernel,
        out_shape=(out, jax.ShapeDtypeStruct((8, 128), jnp.float32)) if mark else out,
        in_specs=[VMEM, VMEM] + [HBM] * len(kept) + [ANY] * len(after),
        out_specs=(HBM, VMEM) if mark else HBM,
        scratch_shapes=[pltpu.VMEM((rows, width), jnp.bfloat16), pltpu.SemaphoreType.DMA((len(cuts),))],
        input_output_aliases={2: 0} if kept else {},
        compiler_params=pltpu.CompilerParams(vmem_limit_bytes=4 * MIB),
        name="add_rows",
    )(total, back, *kept, *after)


def body(image, text, target, factor, shift):
    scale = factor[0]
    bias = shift[0]
    cuts = row_cuts(image.shape[0])
    first = image[: cuts[0][1]]
    part = [shifted(first, "blk", -1)]
    text_prev = shifted(text, "grp", 1)
    part.append(shifted(fetch(image, *cuts[1], [first]), "blk", -1))

    target = fetch(target, 0, 1, [part[0]])
    part.append(shifted(fetch(image, *cuts[2], [target]), "blk", -1))
    own = jax.nn.sigmoid(dot_nt(image, text) * scale + bias)
    column = lax.broadcasted_iota(jnp.int32, own.shape, 1)
    own = (own - (column == target[0][:, None]).astype(jnp.float32)).astype(jnp.bfloat16)
    part.append(shifted(fetch(image, *cuts[3], [own]), "blk", -1))
    image_grad = dot_nn(own, text)
    text_grad = dot_tn(own, image)

    text_prev = pass_on(text_prev, [image_grad, text_grad])
    sent0, part0, own0, prev0 = chunk(factor, shift, text, text_prev, part[0], part[1], [])
    back0 = shifted(sent0, "blk", 1)
    prev_own = jax.nn.sigmoid(dot_nt(text_prev, image) * scale + bias).astype(jnp.bfloat16)
    image_grad = scale * (image_grad + dot_tn(prev_own, text_prev))
    text_sent = dot_nn(prev_own, image) + dot_tn(prev0, part0)
    text_grad = text_grad + dot_tn(own0, part0)

    sent1, part1, own1, prev1 = chunk(factor, shift, text, text_prev, part[2], part[3], [text_sent])
    text_sent = (scale * (text_sent + dot_tn(prev1, part1))).astype(jnp.bfloat16)
    text_back = shifted(text_sent, "grp", -1)
    sent1 = pass_on(sent1, [text_sent])
    back1 = shifted(sent1, "blk", 1)
    text_grad = scale * (text_grad + dot_tn(own1, part1))

    result = add_rows(image_grad, back0, 0, None, [])
    text_grad, mark = add_rows(text_grad, text_back, 0, None, [], mark=True)
    result = add_rows(image_grad, back1, cuts[2][0], result, [mark])
    return result, text_grad


def solution(mesh):
    block = P(("blk", "grp"), None)
    return jax.shard_map(
        body, mesh=mesh, in_specs=(block, block, block, P(), P()), out_specs=(block, block), check_vma=False
    )
```

```python
import functools

import jax
import jax.numpy as jnp
from jax import lax
from jax.experimental import pallas as pl
from jax.experimental.pallas import tpu as pltpu
from jax.sharding import PartitionSpec as P

MIB = 2**20
ENDS = (8, 23)
SMEM = pl.BlockSpec(memory_space=pltpu.SMEM)
VMEM = pl.BlockSpec(memory_space=pltpu.VMEM)
HBM = pl.BlockSpec(memory_space=pltpu.HBM)
ANY = pl.BlockSpec(memory_space=pl.ANY)


def shifted(shard, axis, by):
    devices = lax.axis_size(axis)
    return lax.ppermute(shard, axis, [(i, (i + by) % devices) for i in range(devices)])


def dot_nt(a, b):
    return lax.dot_general(a, b, (((1,), (1,)), ((), ())), preferred_element_type=jnp.float32)


def dot_tn(a, b):
    return lax.dot_general(a, b, (((0,), (0,)), ((), ())), preferred_element_type=jnp.float32)


def dot_nn(a, b):
    return jnp.dot(a, b, preferred_element_type=jnp.float32)


def row_cuts(rows):
    tiles = rows // 16
    cuts = [0] + [tiles * ends // 26 * 16 for ends in ENDS] + [rows]
    return list(zip(cuts[:-1], cuts[1:]))


def fetch(array, lo, hi, after):
    def kernel(array_ref, *refs):
        out_ref, sem = refs[-2:]
        copy = pltpu.make_async_copy(array_ref.at[pl.ds(lo, hi - lo), :], out_ref, sem)
        copy.start()
        copy.wait()

    return pl.pallas_call(
        kernel,
        out_shape=jax.ShapeDtypeStruct((hi - lo, array.shape[1]), array.dtype),
        in_specs=[ANY] * (1 + len(after)),
        out_specs=VMEM,
        scratch_shapes=[pltpu.SemaphoreType.DMA],
        compiler_params=pltpu.CompilerParams(vmem_limit_bytes=2 * MIB),
        name="fetch",
    )(array, *after)


def pass_on(array, after):
    return pl.pallas_call(
        lambda *refs: None,
        out_shape=jax.ShapeDtypeStruct(array.shape, array.dtype),
        in_specs=[ANY] * (1 + len(after)),
        out_specs=ANY,
        input_output_aliases={0: 0},
        compiler_params=pltpu.CompilerParams(vmem_limit_bytes=MIB),
        name="pass_on",
    )(array, *after)


def chunk_kernel(count, scale_ref, bias_ref, image_ref, next_ref, *refs):
    sent_ref, joined_ref, own_ref, other_ref = refs[-4:]
    scale, bias = scale_ref[0], bias_ref[0]
    start = 0
    for piece_ref in refs[:count]:
        rows = piece_ref.shape[0]
        joined_ref[start : start + rows, :] = piece_ref[...]
        start += rows
    part = joined_ref[...]
    image = image_ref[...]
    own = jax.nn.sigmoid(dot_nt(part, image) * scale + bias).astype(jnp.bfloat16)
    own_ref[...] = own
    total = dot_nn(own, image)
    image = next_ref[...]
    other = jax.nn.sigmoid(dot_nt(part, image) * scale + bias).astype(jnp.bfloat16)
    other_ref[...] = other
    total += dot_nn(other, image)
    sent_ref[...] = (scale * total).astype(jnp.bfloat16)


def chunk(factor, shift, image, image_next, pieces, after):
    rows, (columns, width) = sum(piece.shape[0] for piece in pieces), image.shape
    text = jax.ShapeDtypeStruct((rows, width), jnp.bfloat16)
    tile = jax.ShapeDtypeStruct((rows, columns), jnp.bfloat16)
    return pl.pallas_call(
        functools.partial(chunk_kernel, len(pieces)),
        out_shape=(text, text, tile, tile),
        in_specs=[SMEM] * 2 + [VMEM] * (2 + len(pieces)) + [ANY] * len(after),
        out_specs=(VMEM,) * 4,
        compiler_params=pltpu.CompilerParams(vmem_limit_bytes=16 * MIB),
        cost_estimate=pl.CostEstimate(
            flops=8 * rows * columns * width,
            bytes_accessed=2 * (2 * columns + 3 * rows) * width,
            transcendentals=2 * rows * columns,
        ),
        name="chunk",
    )(factor, shift, image, image_next, *pieces, *after)


def add_rows(total, back, lo, result, after, mark=False):
    rows, width = back.shape
    step = rows // 16 // 3 * 16 if rows >= 96 else rows
    cuts = [(i, min(i + step, rows)) for i in range(0, rows, step)]

    def kernel(total_ref, back_ref, *refs):
        buffer, sems = refs[-2:]
        result_ref = refs[-4] if mark else refs[-3]
        copies = []
        for i, (a, b) in enumerate(cuts):
            buffer[a:b, :] = (total_ref[lo + a : lo + b, :] + back_ref[a:b, :].astype(jnp.float32)).astype(jnp.bfloat16)
            copies.append(
                pltpu.make_async_copy(
                    buffer.at[pl.ds(a, b - a), :], result_ref.at[pl.ds(lo + a, b - a), :], sems.at[i]
                )
            )
            copies[-1].start()
        if mark:
            refs[-3][...] = jnp.zeros((8, 128), jnp.float32)
        for copy in copies:
            copy.wait()

    kept = [] if result is None else [result]
    out = jax.ShapeDtypeStruct(total.shape, jnp.bfloat16)
    return pl.pallas_call(
        kernel,
        out_shape=(out, jax.ShapeDtypeStruct((8, 128), jnp.float32)) if mark else out,
        in_specs=[VMEM, VMEM] + [HBM] * len(kept) + [ANY] * len(after),
        out_specs=(HBM, VMEM) if mark else HBM,
        scratch_shapes=[pltpu.VMEM((rows, width), jnp.bfloat16), pltpu.SemaphoreType.DMA((len(cuts),))],
        input_output_aliases={2: 0} if kept else {},
        compiler_params=pltpu.CompilerParams(vmem_limit_bytes=4 * MIB),
        name="add_rows",
    )(total, back, *kept, *after)


def body(image, text, target, factor, shift):
    scale = factor[0]
    bias = shift[0]
    cuts = row_cuts(text.shape[0])
    first = text[: cuts[0][1]]
    part = [shifted(first, "blk", 1)]
    image_next = shifted(image, "grp", -1)
    part.append(shifted(fetch(text, *cuts[1], [first]), "blk", 1))

    target = fetch(target, 0, 1, [part[0]])
    own = jax.nn.sigmoid(dot_nt(image, text) * scale + bias)
    column = lax.broadcasted_iota(jnp.int32, own.shape, 1)
    own = (own - (column == target[0][:, None]).astype(jnp.float32)).astype(jnp.bfloat16)
    part.append(shifted(fetch(text, *cuts[2], [own]), "blk", 1))
    image_grad = dot_nn(own, text)
    text_grad = dot_tn(own, image)

    image_next = pass_on(image_next, [image_grad, text_grad])
    sent0, part0, own0, next0 = chunk(factor, shift, image, image_next, part[:1], [])
    next_own = jax.nn.sigmoid(dot_nt(image_next, text) * scale + bias).astype(jnp.bfloat16)
    text_grad = scale * (text_grad + dot_tn(next_own, image_next))
    image_sent = dot_nn(next_own, text) + dot_tn(next0, part0)
    image_grad = image_grad + dot_tn(own0, part0)

    sent0 = pass_on(sent0, [part[1], image_sent])
    back0 = shifted(sent0, "blk", -1)

    sent1, part1, own1, next1 = chunk(factor, shift, image, image_next, part[1:], [sent0])
    image_sent = (scale * (image_sent + dot_tn(next1, part1))).astype(jnp.bfloat16)
    image_back = shifted(image_sent, "grp", 1)
    sent1 = pass_on(sent1, [image_sent])
    back1 = shifted(sent1, "blk", -1)
    result, mark = add_rows(text_grad, back0, 0, None, [], mark=True)
    own1 = pass_on(own1, [mark])
    image_grad = scale * (image_grad + dot_tn(own1, part1))
    image_grad, mark = add_rows(image_grad, image_back, 0, None, [], mark=True)
    result = add_rows(text_grad, back1, cuts[1][0], result, [mark])
    return image_grad, result


def solution(mesh):
    block = P(("blk", "grp"), None)
    return jax.shard_map(
        body, mesh=mesh, in_specs=(block, block, block, P(), P()), out_specs=(block, block), check_vma=False
    )
```

```python
import functools

import jax
import jax.numpy as jnp
from jax import lax
from jax.experimental import pallas as pl
from jax.experimental.pallas import tpu as pltpu
from jax.sharding import PartitionSpec as P

MIB = 2**20
FIRST = 8
WAIT = 10**10
SMEM = pl.BlockSpec(memory_space=pltpu.SMEM)
VMEM = pl.BlockSpec(memory_space=pltpu.VMEM)
HBM = pl.BlockSpec(memory_space=pltpu.HBM)
ANY = pl.BlockSpec(memory_space=pl.ANY)


def shifted(shard, axis, by):
    devices = lax.axis_size(axis)
    return lax.ppermute(shard, axis, [(i, (i + by) % devices) for i in range(devices)])


def dot_nt(a, b):
    return lax.dot_general(a, b, (((1,), (1,)), ((), ())), preferred_element_type=jnp.float32)


def dot_tn(a, b):
    return lax.dot_general(a, b, (((0,), (0,)), ((), ())), preferred_element_type=jnp.float32)


def dot_nn(a, b):
    return jnp.dot(a, b, preferred_element_type=jnp.float32)


def shifted_half(shard, by, parity):
    blocks, groups = lax.axis_size("blk"), lax.axis_size("grp")
    pairs = [
        (b * groups + g, (b + by * (g % 2 == parity)) % blocks * groups + g) for b in range(blocks) for g in range(groups)
    ]
    return lax.ppermute(shard, ("blk", "grp"), pairs)


def fetch(array, lo, hi, after):
    def kernel(array_ref, *refs):
        out_ref, sem = refs[-2:]
        copy = pltpu.make_async_copy(array_ref.at[pl.ds(lo, hi - lo), :], out_ref, sem)
        copy.start()
        copy.wait()

    return pl.pallas_call(
        kernel,
        out_shape=jax.ShapeDtypeStruct((hi - lo, array.shape[1]), array.dtype),
        in_specs=[ANY] * (1 + len(after)),
        out_specs=VMEM,
        scratch_shapes=[pltpu.SemaphoreType.DMA],
        compiler_params=pltpu.CompilerParams(vmem_limit_bytes=2 * MIB),
        name="fetch",
    )(array, *after)


def pass_on(array, after, flops=0):
    return pl.pallas_call(
        lambda *refs: None,
        out_shape=jax.ShapeDtypeStruct(array.shape, array.dtype),
        in_specs=[ANY] * (1 + len(after)),
        out_specs=ANY,
        input_output_aliases={0: 0},
        compiler_params=pltpu.CompilerParams(vmem_limit_bytes=MIB),
        cost_estimate=pl.CostEstimate(flops=flops, bytes_accessed=0, transcendentals=0),
        name="pass_on",
    )(array, *after)


def chunk_kernel(lo, parity_ref, scale_ref, bias_ref, image_ref, next_ref, even_ref, odd_ref, *refs):
    sent_ref, part_ref, own_ref, other_ref = refs[-4:]
    scale, bias = scale_ref[0], bias_ref[0]
    rows = pl.ds(lo, part_ref.shape[0])

    @pl.when(parity_ref[0] == 0)
    def _():
        part_ref[...] = even_ref[rows, :]

    @pl.when(parity_ref[0] != 0)
    def _():
        part_ref[...] = odd_ref[rows, :]

    part = part_ref[...]
    image = image_ref[...]
    own = jax.nn.sigmoid(dot_nt(part, image) * scale + bias).astype(jnp.bfloat16)
    own_ref[...] = own
    total = dot_nn(own, image)
    image = next_ref[...]
    other = jax.nn.sigmoid(dot_nt(part, image) * scale + bias).astype(jnp.bfloat16)
    other_ref[...] = other
    total += dot_nn(other, image)
    sent_ref[...] = (scale * total).astype(jnp.bfloat16)


def chunk(parity, factor, shift, image, image_next, texts, lo, hi, after):
    rows, (columns, width) = hi - lo, image.shape
    text = jax.ShapeDtypeStruct((rows, width), jnp.bfloat16)
    tile = jax.ShapeDtypeStruct((rows, columns), jnp.bfloat16)
    return pl.pallas_call(
        functools.partial(chunk_kernel, lo),
        out_shape=(text, text, tile, tile),
        in_specs=[SMEM] * 3 + [VMEM] * 4 + [ANY] * len(after),
        out_specs=(VMEM,) * 4,
        compiler_params=pltpu.CompilerParams(vmem_limit_bytes=16 * MIB),
        cost_estimate=pl.CostEstimate(
            flops=8 * rows * columns * width,
            bytes_accessed=2 * (2 * columns + 4 * rows) * width,
            transcendentals=2 * rows * columns,
        ),
        name="chunk",
    )(parity, factor, shift, image, image_next, *texts, *after)


def add_rows(total, pieces, result, after, mark=False, flops=0):
    width = total.shape[1]
    arrays = [array for _, backs in pieces for array in backs]
    steps = []
    first = 0
    for lo, backs in pieces:
        rows = backs[0].shape[0]
        step = rows // 16 // 3 * 16 if rows >= 96 else rows
        for start in range(0, rows, step):
            stop = min(start + step, rows)
            steps.append((lo, start, stop, range(first, first + len(backs))))
        first += len(backs)
    low = min(lo for lo, _ in pieces)
    high = max(lo + backs[0].shape[0] for lo, backs in pieces)

    def kernel(total_ref, *refs):
        buffer, sems = refs[-2:]
        result_ref = refs[-4] if mark else refs[-3]
        copies = []
        for i, (lo, start, stop, backs) in enumerate(steps):
            rows = total_ref[lo + start : lo + stop, :]
            for back in backs:
                rows += refs[back][start:stop, :].astype(jnp.float32)
            held = buffer.at[pl.ds(lo + start - low, stop - start), :]
            held[...] = rows.astype(jnp.bfloat16)
            copies.append(
                pltpu.make_async_copy(held, result_ref.at[pl.ds(lo + start, stop - start), :], sems.at[i])
            )
            copies[-1].start()
        if mark:
            refs[-3][...] = jnp.zeros((8, 128), jnp.float32)
        for copy in copies:
            copy.wait()

    kept = [] if result is None else [result]
    out = jax.ShapeDtypeStruct(total.shape, jnp.bfloat16)
    return pl.pallas_call(
        kernel,
        out_shape=(out, jax.ShapeDtypeStruct((8, 128), jnp.float32)) if mark else out,
        in_specs=[VMEM] * (1 + len(arrays)) + [HBM] * len(kept) + [ANY] * len(after),
        out_specs=(HBM, VMEM) if mark else HBM,
        scratch_shapes=[pltpu.VMEM((high - low, width), jnp.bfloat16), pltpu.SemaphoreType.DMA((len(steps),))],
        input_output_aliases={1 + len(arrays): 0} if kept else {},
        compiler_params=pltpu.CompilerParams(vmem_limit_bytes=4 * MIB),
        cost_estimate=pl.CostEstimate(flops=flops, bytes_accessed=0, transcendentals=0),
        name="add_rows",
    )(total, *arrays, *kept, *after)


def body(image, text, target, factor, shift):
    scale = factor[0]
    bias = shift[0]
    count = text.shape[0]
    cut = count // 16 * FIRST // 26 * 16
    parity = (lax.axis_index("grp") % 2).astype(jnp.int32).reshape(1)
    even = shifted_half(text, 1, 0)
    held = fetch(image, 0, count, [])
    image_next = shifted(held, "grp", -1)

    own = jax.nn.sigmoid(dot_nt(image, text) * scale + bias)
    column = lax.broadcasted_iota(jnp.int32, own.shape, 1)
    own = (own - (column == target[0][:, None]).astype(jnp.float32)).astype(jnp.bfloat16)
    odd = shifted_half(fetch(text, 0, count, [held]), 1, 1)
    image_grad = dot_nn(own, text)
    text_grad = dot_tn(own, image)

    even = pass_on(even, [image_grad, text_grad], WAIT)
    image_next = pass_on(image_next, [even], WAIT)
    odd = pass_on(odd, [image_next])
    sent0, part0, own0, next0 = chunk(parity, factor, shift, image, image_next, [even, odd], 0, cut, [])
    back0 = shifted(sent0, "blk", -1)
    image_next = pass_on(image_next, [sent0], WAIT)
    sent1, part1, own1, next1 = chunk(parity, factor, shift, image, image_next, [even, odd], cut, count, [])
    back1 = shifted(sent1, "blk", -1)
    image_next = pass_on(image_next, [sent1], WAIT)
    next_own = jax.nn.sigmoid(dot_nt(image_next, text) * scale + bias).astype(jnp.bfloat16)
    image_sent = dot_nn(next_own, text) + dot_tn(next0, part0)
    image_sent = (scale * (image_sent + dot_tn(next1, part1))).astype(jnp.bfloat16)
    image_back = shifted(image_sent, "grp", 1)
    text_grad = scale * (text_grad + dot_tn(next_own, image_next))
    image_grad = image_grad + dot_tn(own0, part0)
    image_grad = scale * (image_grad + dot_tn(own1, part1))

    result = add_rows(text_grad, [(0, [back0])], None, [])
    result, mark = add_rows(text_grad, [(cut, [back1])], result, [], mark=True, flops=2 * WAIT)
    image_grad = add_rows(image_grad, [(0, [image_back])], None, [mark])
    return image_grad, result


def solution(mesh):
    block = P(("blk", "grp"), None)
    return jax.shard_map(
        body, mesh=mesh, in_specs=(block, block, block, P(), P()), out_specs=(block, block), check_vma=False
    )
```

```python
import functools

import jax
import jax.numpy as jnp
from jax import lax
from jax.experimental import pallas as pl
from jax.experimental.pallas import tpu as pltpu
from jax.sharding import PartitionSpec as P

MIB = 2**20
ENDS = (8, 22)
SMEM = pl.BlockSpec(memory_space=pltpu.SMEM)
VMEM = pl.BlockSpec(memory_space=pltpu.VMEM)
HBM = pl.BlockSpec(memory_space=pltpu.HBM)
ANY = pl.BlockSpec(memory_space=pl.ANY)


def shifted(shard, axis, by):
    devices = lax.axis_size(axis)
    return lax.ppermute(shard, axis, [(i, (i + by) % devices) for i in range(devices)])


def dot_nt(a, b):
    return lax.dot_general(a, b, (((1,), (1,)), ((), ())), preferred_element_type=jnp.float32)


def dot_tn(a, b):
    return lax.dot_general(a, b, (((0,), (0,)), ((), ())), preferred_element_type=jnp.float32)


def dot_nn(a, b):
    return jnp.dot(a, b, preferred_element_type=jnp.float32)


def row_cuts(rows):
    tiles = rows // 16
    cuts = [0] + [tiles * ends // 26 * 16 for ends in ENDS] + [rows]
    return list(zip(cuts[:-1], cuts[1:]))


def fetch(array, lo, hi, after):
    def kernel(array_ref, *refs):
        out_ref, sem = refs[-2:]
        copy = pltpu.make_async_copy(array_ref.at[pl.ds(lo, hi - lo), :], out_ref, sem)
        copy.start()
        copy.wait()

    return pl.pallas_call(
        kernel,
        out_shape=jax.ShapeDtypeStruct((hi - lo, array.shape[1]), array.dtype),
        in_specs=[ANY] * (1 + len(after)),
        out_specs=VMEM,
        scratch_shapes=[pltpu.SemaphoreType.DMA],
        compiler_params=pltpu.CompilerParams(vmem_limit_bytes=2 * MIB),
        name="fetch",
    )(array, *after)


def pass_on(array, after):
    return pl.pallas_call(
        lambda *refs: None,
        out_shape=jax.ShapeDtypeStruct(array.shape, array.dtype),
        in_specs=[ANY] * (1 + len(after)),
        out_specs=ANY,
        input_output_aliases={0: 0},
        compiler_params=pltpu.CompilerParams(vmem_limit_bytes=MIB),
        name="pass_on",
    )(array, *after)


def chunk_kernel(count, scale_ref, bias_ref, image_ref, next_ref, *refs):
    sent_ref, joined_ref, own_ref, other_ref = refs[-4:]
    scale, bias = scale_ref[0], bias_ref[0]
    start = 0
    for piece_ref in refs[:count]:
        rows = piece_ref.shape[0]
        joined_ref[start : start + rows, :] = piece_ref[...]
        start += rows
    part = joined_ref[...]
    image = image_ref[...]
    own = jax.nn.sigmoid(dot_nt(part, image) * scale + bias).astype(jnp.bfloat16)
    own_ref[...] = own
    total = dot_nn(own, image)
    image = next_ref[...]
    other = jax.nn.sigmoid(dot_nt(part, image) * scale + bias).astype(jnp.bfloat16)
    other_ref[...] = other
    total += dot_nn(other, image)
    sent_ref[...] = (scale * total).astype(jnp.bfloat16)


def chunk(factor, shift, image, image_next, pieces, after):
    rows, (columns, width) = sum(piece.shape[0] for piece in pieces), image.shape
    text = jax.ShapeDtypeStruct((rows, width), jnp.bfloat16)
    tile = jax.ShapeDtypeStruct((rows, columns), jnp.bfloat16)
    return pl.pallas_call(
        functools.partial(chunk_kernel, len(pieces)),
        out_shape=(text, text, tile, tile),
        in_specs=[SMEM] * 2 + [VMEM] * (2 + len(pieces)) + [ANY] * len(after),
        out_specs=(VMEM,) * 4,
        compiler_params=pltpu.CompilerParams(vmem_limit_bytes=16 * MIB),
        cost_estimate=pl.CostEstimate(
            flops=8 * rows * columns * width,
            bytes_accessed=2 * (2 * columns + 3 * rows) * width,
            transcendentals=2 * rows * columns,
        ),
        name="chunk",
    )(factor, shift, image, image_next, *pieces, *after)


def add_rows(total, back, lo, result, after, mark=False):
    rows, width = back.shape
    step = rows // 16 // 3 * 16 if rows >= 96 else rows
    cuts = [(i, min(i + step, rows)) for i in range(0, rows, step)]

    def kernel(total_ref, back_ref, *refs):
        buffer, sems = refs[-2:]
        result_ref = refs[-4] if mark else refs[-3]
        copies = []
        for i, (a, b) in enumerate(cuts):
            buffer[a:b, :] = (total_ref[lo + a : lo + b, :] + back_ref[a:b, :].astype(jnp.float32)).astype(jnp.bfloat16)
            copies.append(
                pltpu.make_async_copy(
                    buffer.at[pl.ds(a, b - a), :], result_ref.at[pl.ds(lo + a, b - a), :], sems.at[i]
                )
            )
            copies[-1].start()
        if mark:
            refs[-3][...] = jnp.zeros((8, 128), jnp.float32)
        for copy in copies:
            copy.wait()

    kept = [] if result is None else [result]
    out = jax.ShapeDtypeStruct(total.shape, jnp.bfloat16)
    return pl.pallas_call(
        kernel,
        out_shape=(out, jax.ShapeDtypeStruct((8, 128), jnp.float32)) if mark else out,
        in_specs=[VMEM, VMEM] + [HBM] * len(kept) + [ANY] * len(after),
        out_specs=(HBM, VMEM) if mark else HBM,
        scratch_shapes=[pltpu.VMEM((rows, width), jnp.bfloat16), pltpu.SemaphoreType.DMA((len(cuts),))],
        input_output_aliases={2: 0} if kept else {},
        compiler_params=pltpu.CompilerParams(vmem_limit_bytes=4 * MIB),
        name="add_rows",
    )(total, back, *kept, *after)


def body(image, text, target, factor, shift):
    scale = factor[0]
    bias = shift[0]
    cuts = row_cuts(text.shape[0])
    first = text[: cuts[0][1]]
    part = [shifted(first, "blk", 1)]
    image_next = shifted(image, "grp", -1)
    part.append(shifted(fetch(text, *cuts[1], [first]), "blk", 1))

    target = fetch(target, 0, 1, [part[0]])
    own = jax.nn.sigmoid(dot_nt(image, text) * scale + bias)
    column = lax.broadcasted_iota(jnp.int32, own.shape, 1)
    own = (own - (column == target[0][:, None]).astype(jnp.float32)).astype(jnp.bfloat16)
    part.append(shifted(fetch(text, *cuts[2], [own]), "blk", 1))
    image_grad = dot_nn(own, text)
    text_grad = dot_tn(own, image)

    image_next = pass_on(image_next, [image_grad, text_grad])
    sent0, part0, own0, next0 = chunk(factor, shift, image, image_next, part[:1], [])
    next_own = jax.nn.sigmoid(dot_nt(image_next, text) * scale + bias).astype(jnp.bfloat16)
    text_grad = scale * (text_grad + dot_tn(next_own, image_next))
    image_sent = dot_nn(next_own, text) + dot_tn(next0, part0)
    image_grad = image_grad + dot_tn(own0, part0)

    sent0 = pass_on(sent0, [part[1], image_sent])
    back0 = shifted(sent0, "blk", -1)

    sent1, part1, own1, next1 = chunk(factor, shift, image, image_next, part[1:], [sent0])
    image_sent = (scale * (image_sent + dot_tn(next1, part1))).astype(jnp.bfloat16)
    image_back = shifted(image_sent, "grp", 1)
    sent1 = pass_on(sent1, [image_sent])
    back1 = shifted(sent1, "blk", -1)
    result, mark = add_rows(text_grad, back0, 0, None, [], mark=True)
    own1 = pass_on(own1, [mark])
    image_grad = scale * (image_grad + dot_tn(own1, part1))
    image_grad, mark = add_rows(image_grad, image_back, 0, None, [], mark=True)
    result = add_rows(text_grad, back1, cuts[1][0], result, [mark])
    return image_grad, result


def solution(mesh):
    block = P(("blk", "grp"), None)
    return jax.shard_map(
        body, mesh=mesh, in_specs=(block, block, block, P(), P()), out_specs=(block, block), check_vma=False
    )
```

```python
import jax
import jax.numpy as jnp
from jax import lax
from jax.experimental import pallas as pl
from jax.experimental.pallas import tpu as pltpu
from jax.sharding import PartitionSpec as P

MIB = 2**20
SMEM = pl.BlockSpec(memory_space=pltpu.SMEM)
VMEM = pl.BlockSpec(memory_space=pltpu.VMEM)
HBM = pl.BlockSpec(memory_space=pltpu.HBM)
ANY = pl.BlockSpec(memory_space=pl.ANY)


def shifted(shard, axis, by):
    devices = lax.axis_size(axis)
    return lax.ppermute(shard, axis, [(i, (i + by) % devices) for i in range(devices)])


def dot_nt(a, b):
    return lax.dot_general(a, b, (((1,), (1,)), ((), ())), preferred_element_type=jnp.float32)


def dot_tn(a, b):
    return lax.dot_general(a, b, (((0,), (0,)), ((), ())), preferred_element_type=jnp.float32)


def dot_nn(a, b):
    return jnp.dot(a, b, preferred_element_type=jnp.float32)


def row_cuts(rows):
    tiles = rows // 16
    cuts = [0, tiles * 6 // 26 * 16, tiles * 16 // 26 * 16, tiles * 24 // 26 * 16, rows]
    return list(zip(cuts[:-1], cuts[1:]))


def fetch(array, lo, hi, after):
    def kernel(array_ref, *refs):
        out_ref, sem = refs[-2:]
        copy = pltpu.make_async_copy(array_ref.at[pl.ds(lo, hi - lo), :], out_ref, sem)
        copy.start()
        copy.wait()

    return pl.pallas_call(
        kernel,
        out_shape=jax.ShapeDtypeStruct((hi - lo, array.shape[1]), array.dtype),
        in_specs=[ANY] * (1 + len(after)),
        out_specs=VMEM,
        scratch_shapes=[pltpu.SemaphoreType.DMA],
        compiler_params=pltpu.CompilerParams(vmem_limit_bytes=2 * MIB),
        name="fetch",
    )(array, *after)


def pass_on(array, after):
    return pl.pallas_call(
        lambda *refs: None,
        out_shape=jax.ShapeDtypeStruct(array.shape, array.dtype),
        in_specs=[ANY] * (1 + len(after)),
        out_specs=ANY,
        input_output_aliases={0: 0},
        compiler_params=pltpu.CompilerParams(vmem_limit_bytes=MIB),
        name="pass_on",
    )(array, *after)


def chunk_kernel(scale_ref, bias_ref, image_ref, next_ref, upper_ref, lower_ref, *refs):
    sent_ref, joined_ref, own_ref, other_ref = refs[-4:]
    scale, bias = scale_ref[0], bias_ref[0]
    rows = upper_ref.shape[0]
    joined_ref[:rows, :] = upper_ref[...]
    joined_ref[rows:, :] = lower_ref[...]
    part = joined_ref[...]
    image = image_ref[...]
    own = jax.nn.sigmoid(dot_nt(part, image) * scale + bias).astype(jnp.bfloat16)
    own_ref[...] = own
    total = dot_nn(own, image)
    image = next_ref[...]
    other = jax.nn.sigmoid(dot_nt(part, image) * scale + bias).astype(jnp.bfloat16)
    other_ref[...] = other
    total += dot_nn(other, image)
    sent_ref[...] = (scale * total).astype(jnp.bfloat16)


def chunk(factor, shift, image, image_next, upper, lower, after):
    rows, width = upper.shape[0] + lower.shape[0], upper.shape[1]
    columns = image.shape[0]
    text = jax.ShapeDtypeStruct((rows, width), jnp.bfloat16)
    tile = jax.ShapeDtypeStruct((rows, columns), jnp.bfloat16)
    return pl.pallas_call(
        chunk_kernel,
        out_shape=(text, text, tile, tile),
        in_specs=[SMEM] * 2 + [VMEM] * 4 + [ANY] * len(after),
        out_specs=(VMEM,) * 4,
        compiler_params=pltpu.CompilerParams(vmem_limit_bytes=16 * MIB),
        cost_estimate=pl.CostEstimate(
            flops=8 * rows * columns * width,
            bytes_accessed=2 * (2 * columns + 3 * rows) * width,
            transcendentals=2 * rows * columns,
        ),
        name="chunk",
    )(factor, shift, image, image_next, upper, lower, *after)


def add_rows(total, back, lo, result, after, mark=False):
    rows, width = back.shape
    step = rows // 16 // 3 * 16 if rows >= 96 else rows
    cuts = [(i, min(i + step, rows)) for i in range(0, rows, step)]

    def kernel(total_ref, back_ref, *refs):
        buffer, sems = refs[-2:]
        result_ref = refs[-4] if mark else refs[-3]
        copies = []
        for i, (a, b) in enumerate(cuts):
            buffer[a:b, :] = (total_ref[lo + a : lo + b, :] + back_ref[a:b, :].astype(jnp.float32)).astype(jnp.bfloat16)
            copies.append(
                pltpu.make_async_copy(
                    buffer.at[pl.ds(a, b - a), :], result_ref.at[pl.ds(lo + a, b - a), :], sems.at[i]
                )
            )
            copies[-1].start()
        if mark:
            refs[-3][...] = jnp.zeros((8, 128), jnp.float32)
        for copy in copies:
            copy.wait()

    kept = [] if result is None else [result]
    out = jax.ShapeDtypeStruct(total.shape, jnp.bfloat16)
    return pl.pallas_call(
        kernel,
        out_shape=(out, jax.ShapeDtypeStruct((8, 128), jnp.float32)) if mark else out,
        in_specs=[VMEM, VMEM] + [HBM] * len(kept) + [ANY] * len(after),
        out_specs=(HBM, VMEM) if mark else HBM,
        scratch_shapes=[pltpu.VMEM((rows, width), jnp.bfloat16), pltpu.SemaphoreType.DMA((len(cuts),))],
        input_output_aliases={2: 0} if kept else {},
        compiler_params=pltpu.CompilerParams(vmem_limit_bytes=4 * MIB),
        name="add_rows",
    )(total, back, *kept, *after)


def body(image, text, target, factor, shift):
    scale = factor[0]
    bias = shift[0]
    cuts = row_cuts(text.shape[0])
    first = text[: cuts[0][1]]
    part = [shifted(first, "blk", 1)]
    image_next = shifted(image, "grp", -1)
    part.append(shifted(fetch(text, *cuts[1], [first]), "blk", 1))

    target = fetch(target, 0, 1, [part[0]])
    part.append(shifted(fetch(text, *cuts[2], [target]), "blk", 1))
    own = jax.nn.sigmoid(dot_nt(image, text) * scale + bias)
    column = lax.broadcasted_iota(jnp.int32, own.shape, 1)
    own = (own - (column == target[0][:, None]).astype(jnp.float32)).astype(jnp.bfloat16)
    part.append(shifted(fetch(text, *cuts[3], [own]), "blk", 1))
    image_grad = dot_nn(own, text)
    text_grad = dot_tn(own, image)

    image_next = pass_on(image_next, [image_grad, text_grad])
    sent0, part0, own0, next0 = chunk(factor, shift, image, image_next, part[0], part[1], [])
    next_own = jax.nn.sigmoid(dot_nt(image_next, text) * scale + bias).astype(jnp.bfloat16)
    text_grad = scale * (text_grad + dot_tn(next_own, image_next))
    image_sent = dot_nn(next_own, text) + dot_tn(next0, part0)
    image_grad = image_grad + dot_tn(own0, part0)

    sent0 = pass_on(sent0, [part[2], image_sent])
    back0 = shifted(sent0, "blk", -1)

    sent1, part1, own1, next1 = chunk(factor, shift, image, image_next, part[2], part[3], [sent0])
    image_sent = (scale * (image_sent + dot_tn(next1, part1))).astype(jnp.bfloat16)
    image_back = shifted(image_sent, "grp", 1)
    sent1 = pass_on(sent1, [image_sent])
    back1 = shifted(sent1, "blk", -1)
    image_grad = scale * (image_grad + dot_tn(own1, part1))

    result = add_rows(text_grad, back0, 0, None, [])
    image_grad, mark = add_rows(image_grad, image_back, 0, None, [], mark=True)
    result = add_rows(text_grad, back1, cuts[2][0], result, [mark])
    return image_grad, result


def solution(mesh):
    block = P(("blk", "grp"), None)
    return jax.shard_map(
        body, mesh=mesh, in_specs=(block, block, block, P(), P()), out_specs=(block, block), check_vma=False
    )
```

```python
import functools

import jax
import jax.numpy as jnp
from jax import lax
from jax.experimental import pallas as pl
from jax.experimental.pallas import tpu as pltpu
from jax.sharding import PartitionSpec as P

MIB = 2**20
FIRST = 8
WAIT = 10**10
SMEM = pl.BlockSpec(memory_space=pltpu.SMEM)
VMEM = pl.BlockSpec(memory_space=pltpu.VMEM)
HBM = pl.BlockSpec(memory_space=pltpu.HBM)
ANY = pl.BlockSpec(memory_space=pl.ANY)


def shifted(shard, axis, by):
    devices = lax.axis_size(axis)
    return lax.ppermute(shard, axis, [(i, (i + by) % devices) for i in range(devices)])


def dot_nt(a, b):
    return lax.dot_general(a, b, (((1,), (1,)), ((), ())), preferred_element_type=jnp.float32)


def dot_tn(a, b):
    return lax.dot_general(a, b, (((0,), (0,)), ((), ())), preferred_element_type=jnp.float32)


def dot_nn(a, b):
    return jnp.dot(a, b, preferred_element_type=jnp.float32)


def shifted_half(shard, by, parity):
    blocks, groups = lax.axis_size("blk"), lax.axis_size("grp")
    pairs = [
        (b * groups + g, (b + (by if g % 2 == parity else 2)) % blocks * groups + g)
        for b in range(blocks)
        for g in range(groups)
    ]
    return lax.ppermute(shard, ("blk", "grp"), pairs)


def fetch(array, lo, hi, after):
    def kernel(array_ref, *refs):
        out_ref, sem = refs[-2:]
        copy = pltpu.make_async_copy(array_ref.at[pl.ds(lo, hi - lo), :], out_ref, sem)
        copy.start()
        copy.wait()

    return pl.pallas_call(
        kernel,
        out_shape=jax.ShapeDtypeStruct((hi - lo, array.shape[1]), array.dtype),
        in_specs=[ANY] * (1 + len(after)),
        out_specs=VMEM,
        scratch_shapes=[pltpu.SemaphoreType.DMA],
        compiler_params=pltpu.CompilerParams(vmem_limit_bytes=2 * MIB),
        name="fetch",
    )(array, *after)


def pass_on(array, after, flops=0):
    return pl.pallas_call(
        lambda *refs: None,
        out_shape=jax.ShapeDtypeStruct(array.shape, array.dtype),
        in_specs=[ANY] * (1 + len(after)),
        out_specs=ANY,
        input_output_aliases={0: 0},
        compiler_params=pltpu.CompilerParams(vmem_limit_bytes=MIB),
        cost_estimate=pl.CostEstimate(flops=flops, bytes_accessed=0, transcendentals=0),
        name="pass_on",
    )(array, *after)


def chunk_kernel(lo, parity_ref, scale_ref, bias_ref, image_ref, next_ref, even_ref, odd_ref, *refs):
    sent_ref, part_ref, own_ref, other_ref = refs[-4:]
    scale, bias = scale_ref[0], bias_ref[0]
    rows = pl.ds(lo, part_ref.shape[0])

    @pl.when(parity_ref[0] == 0)
    def _():
        part_ref[...] = even_ref[rows, :]

    @pl.when(parity_ref[0] != 0)
    def _():
        part_ref[...] = odd_ref[rows, :]

    part = part_ref[...]
    image = image_ref[...]
    own = jax.nn.sigmoid(dot_nt(part, image) * scale + bias).astype(jnp.bfloat16)
    own_ref[...] = own
    total = dot_nn(own, image)
    image = next_ref[...]
    other = jax.nn.sigmoid(dot_nt(part, image) * scale + bias).astype(jnp.bfloat16)
    other_ref[...] = other
    total += dot_nn(other, image)
    sent_ref[...] = (scale * total).astype(jnp.bfloat16)


def chunk(parity, factor, shift, image, image_next, texts, lo, hi, after):
    rows, (columns, width) = hi - lo, image.shape
    text = jax.ShapeDtypeStruct((rows, width), jnp.bfloat16)
    tile = jax.ShapeDtypeStruct((rows, columns), jnp.bfloat16)
    return pl.pallas_call(
        functools.partial(chunk_kernel, lo),
        out_shape=(text, text, tile, tile),
        in_specs=[SMEM] * 3 + [VMEM] * 4 + [ANY] * len(after),
        out_specs=(VMEM,) * 4,
        compiler_params=pltpu.CompilerParams(vmem_limit_bytes=16 * MIB),
        cost_estimate=pl.CostEstimate(
            flops=8 * rows * columns * width,
            bytes_accessed=2 * (2 * columns + 4 * rows) * width,
            transcendentals=2 * rows * columns,
        ),
        name="chunk",
    )(parity, factor, shift, image, image_next, *texts, *after)


def add_rows(total, pieces, result, after, mark=False, flops=0):
    width = total.shape[1]
    arrays = [array for _, backs in pieces for array in backs]
    steps = []
    first = 0
    for lo, backs in pieces:
        rows = backs[0].shape[0]
        step = rows // 16 // 3 * 16 if rows >= 96 else rows
        for start in range(0, rows, step):
            stop = min(start + step, rows)
            steps.append((lo, start, stop, range(first, first + len(backs))))
        first += len(backs)
    low = min(lo for lo, _ in pieces)
    high = max(lo + backs[0].shape[0] for lo, backs in pieces)

    def kernel(total_ref, *refs):
        buffer, sems = refs[-2:]
        result_ref = refs[-4] if mark else refs[-3]
        copies = []
        for i, (lo, start, stop, backs) in enumerate(steps):
            rows = total_ref[lo + start : lo + stop, :]
            for back in backs:
                rows += refs[back][start:stop, :].astype(jnp.float32)
            held = buffer.at[pl.ds(lo + start - low, stop - start), :]
            held[...] = rows.astype(jnp.bfloat16)
            copies.append(
                pltpu.make_async_copy(held, result_ref.at[pl.ds(lo + start, stop - start), :], sems.at[i])
            )
            copies[-1].start()
        if mark:
            refs[-3][...] = jnp.zeros((8, 128), jnp.float32)
        for copy in copies:
            copy.wait()

    kept = [] if result is None else [result]
    out = jax.ShapeDtypeStruct(total.shape, jnp.bfloat16)
    return pl.pallas_call(
        kernel,
        out_shape=(out, jax.ShapeDtypeStruct((8, 128), jnp.float32)) if mark else out,
        in_specs=[VMEM] * (1 + len(arrays)) + [HBM] * len(kept) + [ANY] * len(after),
        out_specs=(HBM, VMEM) if mark else HBM,
        scratch_shapes=[pltpu.VMEM((high - low, width), jnp.bfloat16), pltpu.SemaphoreType.DMA((len(steps),))],
        input_output_aliases={1 + len(arrays): 0} if kept else {},
        compiler_params=pltpu.CompilerParams(vmem_limit_bytes=4 * MIB),
        cost_estimate=pl.CostEstimate(flops=flops, bytes_accessed=0, transcendentals=0),
        name="add_rows",
    )(total, *arrays, *kept, *after)


def body(image, text, target, factor, shift):
    scale = factor[0]
    bias = shift[0]
    count = text.shape[0]
    cut = count // 16 * FIRST // 26 * 16
    parity = (lax.axis_index("grp") % 2).astype(jnp.int32).reshape(1)
    even = shifted_half(text, 1, 0)
    image_next = shifted(image, "grp", -1)

    own = jax.nn.sigmoid(dot_nt(image, text) * scale + bias)
    column = lax.broadcasted_iota(jnp.int32, own.shape, 1)
    own = (own - (column == target[0][:, None]).astype(jnp.float32)).astype(jnp.bfloat16)
    odd = shifted_half(fetch(text, 0, count, [own]), 1, 1)
    image_grad = dot_nn(own, text)
    text_grad = dot_tn(own, image)

    even = pass_on(even, [image_grad, text_grad], WAIT)
    image_next = pass_on(image_next, [even], WAIT)
    odd = pass_on(odd, [image_next])
    sent0, part0, own0, next0 = chunk(parity, factor, shift, image, image_next, [even, odd], 0, cut, [])
    back0 = shifted(sent0, "blk", -1)
    image_next = pass_on(image_next, [sent0], WAIT)
    sent1, part1, own1, next1 = chunk(parity, factor, shift, image, image_next, [even, odd], cut, count, [])
    back1 = shifted(sent1, "blk", -1)
    image_next = pass_on(image_next, [sent1], WAIT)
    next_own = jax.nn.sigmoid(dot_nt(image_next, text) * scale + bias).astype(jnp.bfloat16)
    image_sent = dot_nn(next_own, text) + dot_tn(next0, part0)
    image_sent = (scale * (image_sent + dot_tn(next1, part1))).astype(jnp.bfloat16)
    image_back = shifted(image_sent, "grp", 1)
    text_grad = scale * (text_grad + dot_tn(next_own, image_next))
    image_grad = image_grad + dot_tn(own0, part0)
    image_grad = scale * (image_grad + dot_tn(own1, part1))

    result = add_rows(text_grad, [(0, [back0])], None, [])
    result, mark = add_rows(text_grad, [(cut, [back1])], result, [], mark=True, flops=2 * WAIT)
    image_grad = add_rows(image_grad, [(0, [image_back])], None, [mark])
    return image_grad, result


def solution(mesh):
    block = P(("blk", "grp"), None)
    return jax.shard_map(
        body, mesh=mesh, in_specs=(block, block, block, P(), P()), out_specs=(block, block), check_vma=False
    )
```

```python
import functools

import jax
import jax.numpy as jnp
from jax import lax
from jax.experimental import pallas as pl
from jax.experimental.pallas import tpu as pltpu
from jax.sharding import PartitionSpec as P

MIB = 2**20
ENDS = (8, 23)
SMEM = pl.BlockSpec(memory_space=pltpu.SMEM)
VMEM = pl.BlockSpec(memory_space=pltpu.VMEM)
HBM = pl.BlockSpec(memory_space=pltpu.HBM)
ANY = pl.BlockSpec(memory_space=pl.ANY)


def shifted(shard, axis, by):
    devices = lax.axis_size(axis)
    return lax.ppermute(shard, axis, [(i, (i + by) % devices) for i in range(devices)])


def dot_nt(a, b):
    return lax.dot_general(a, b, (((1,), (1,)), ((), ())), preferred_element_type=jnp.float32)


def dot_tn(a, b):
    return lax.dot_general(a, b, (((0,), (0,)), ((), ())), preferred_element_type=jnp.float32)


def dot_nn(a, b):
    return jnp.dot(a, b, preferred_element_type=jnp.float32)


def row_cuts(rows):
    tiles = rows // 16
    cuts = [0] + [tiles * ends // 26 * 16 for ends in ENDS] + [rows]
    return list(zip(cuts[:-1], cuts[1:]))


def fetch(array, lo, hi, after):
    def kernel(array_ref, *refs):
        out_ref, sem = refs[-2:]
        copy = pltpu.make_async_copy(array_ref.at[pl.ds(lo, hi - lo), :], out_ref, sem)
        copy.start()
        copy.wait()

    return pl.pallas_call(
        kernel,
        out_shape=jax.ShapeDtypeStruct((hi - lo, array.shape[1]), array.dtype),
        in_specs=[ANY] * (1 + len(after)),
        out_specs=VMEM,
        scratch_shapes=[pltpu.SemaphoreType.DMA],
        compiler_params=pltpu.CompilerParams(vmem_limit_bytes=2 * MIB),
        name="fetch",
    )(array, *after)


def pass_on(array, after):
    return pl.pallas_call(
        lambda *refs: None,
        out_shape=jax.ShapeDtypeStruct(array.shape, array.dtype),
        in_specs=[ANY] * (1 + len(after)),
        out_specs=ANY,
        input_output_aliases={0: 0},
        compiler_params=pltpu.CompilerParams(vmem_limit_bytes=MIB),
        name="pass_on",
    )(array, *after)


def chunk_kernel(count, lasts, scale_ref, bias_ref, image_ref, next_ref, *refs):
    joined_ref, own_ref, other_ref, *sent_refs = refs[-4 - bool(lasts) :]
    scale, bias = scale_ref[0], bias_ref[0]
    start = 0
    for piece_ref in refs[:count]:
        rows = piece_ref.shape[0]
        joined_ref[start : start + rows, :] = piece_ref[...]
        start += rows
    part = joined_ref[...]
    image = image_ref[...]
    own = jax.nn.sigmoid(dot_nt(part, image) * scale + bias).astype(jnp.bfloat16)
    own_ref[...] = own
    total = dot_nn(own, image)
    image = next_ref[...]
    other = jax.nn.sigmoid(dot_nt(part, image) * scale + bias).astype(jnp.bfloat16)
    other_ref[...] = other
    total += dot_nn(other, image)
    total = (scale * total).astype(jnp.bfloat16)
    start = 0
    for sent_ref in sent_refs:
        sent_ref[...] = total[start : start + sent_ref.shape[0], :]
        start += sent_ref.shape[0]


def chunk(factor, shift, image, image_next, pieces, after, lasts=0):
    rows, (columns, width) = sum(piece.shape[0] for piece in pieces), image.shape
    text = [jax.ShapeDtypeStruct((r, width), jnp.bfloat16) for r in (rows, rows - lasts, lasts) if r]
    tile = jax.ShapeDtypeStruct((rows, columns), jnp.bfloat16)
    return pl.pallas_call(
        functools.partial(chunk_kernel, len(pieces), lasts),
        out_shape=[text[0], tile, tile, *text[1:]],
        in_specs=[SMEM] * 2 + [VMEM] * (2 + len(pieces)) + [ANY] * len(after),
        out_specs=[VMEM] * (2 + len(text)),
        compiler_params=pltpu.CompilerParams(vmem_limit_bytes=16 * MIB),
        cost_estimate=pl.CostEstimate(
            flops=8 * rows * columns * width,
            bytes_accessed=2 * (2 * columns + 3 * rows) * width,
            transcendentals=2 * rows * columns,
        ),
        name="chunk",
    )(factor, shift, image, image_next, *pieces, *after)


def add_rows(total, back, lo, result, after, mark=False):
    rows, width = back.shape
    step = rows // 16 // 3 * 16 if rows >= 96 else rows
    cuts = [(i, min(i + step, rows)) for i in range(0, rows, step)]

    def kernel(total_ref, back_ref, *refs):
        buffer, sems = refs[-2:]
        result_ref = refs[-4] if mark else refs[-3]
        copies = []
        for i, (a, b) in enumerate(cuts):
            buffer[a:b, :] = (total_ref[lo + a : lo + b, :] + back_ref[a:b, :].astype(jnp.float32)).astype(jnp.bfloat16)
            copies.append(
                pltpu.make_async_copy(
                    buffer.at[pl.ds(a, b - a), :], result_ref.at[pl.ds(lo + a, b - a), :], sems.at[i]
                )
            )
            copies[-1].start()
        if mark:
            refs[-3][...] = jnp.zeros((8, 128), jnp.float32)
        for copy in copies:
            copy.wait()

    kept = [] if result is None else [result]
    out = jax.ShapeDtypeStruct(total.shape, jnp.bfloat16)
    return pl.pallas_call(
        kernel,
        out_shape=(out, jax.ShapeDtypeStruct((8, 128), jnp.float32)) if mark else out,
        in_specs=[VMEM, VMEM] + [HBM] * len(kept) + [ANY] * len(after),
        out_specs=(HBM, VMEM) if mark else HBM,
        scratch_shapes=[pltpu.VMEM((rows, width), jnp.bfloat16), pltpu.SemaphoreType.DMA((len(cuts),))],
        input_output_aliases={2: 0} if kept else {},
        compiler_params=pltpu.CompilerParams(vmem_limit_bytes=4 * MIB),
        name="add_rows",
    )(total, back, *kept, *after)


def body(image, text, target, factor, shift):
    scale = factor[0]
    bias = shift[0]
    cuts = row_cuts(text.shape[0])
    first = text[: cuts[0][1]]
    part = [shifted(first, "blk", 1)]
    image_next = shifted(image, "grp", -1)
    part.append(shifted(fetch(text, *cuts[1], [first]), "blk", 1))

    target = fetch(target, 0, 1, [part[0]])
    own = jax.nn.sigmoid(dot_nt(image, text) * scale + bias)
    column = lax.broadcasted_iota(jnp.int32, own.shape, 1)
    own = (own - (column == target[0][:, None]).astype(jnp.float32)).astype(jnp.bfloat16)
    part.append(shifted(fetch(text, *cuts[2], [own]), "blk", 1))
    image_grad = dot_nn(own, text)
    text_grad = dot_tn(own, image)

    image_next = pass_on(image_next, [image_grad, text_grad])
    part0, own0, next0, sent0 = chunk(factor, shift, image, image_next, part[:1], [])
    next_own = jax.nn.sigmoid(dot_nt(image_next, text) * scale + bias).astype(jnp.bfloat16)
    text_grad = scale * (text_grad + dot_tn(next_own, image_next))
    image_sent = dot_nn(next_own, text) + dot_tn(next0, part0)
    image_grad = image_grad + dot_tn(own0, part0)

    sent0 = pass_on(sent0, [part[1], image_sent])
    back0 = shifted(sent0, "blk", -1)

    lasts = part[2].shape[0]
    part1, own1, next1, sent1, sent2 = chunk(factor, shift, image, image_next, part[1:], [sent0], lasts)
    image_sent = (scale * (image_sent + dot_tn(next1, part1))).astype(jnp.bfloat16)
    image_back = shifted(image_sent, "grp", 1)
    sent1 = pass_on(sent1, [image_sent])
    back1 = shifted(sent1, "blk", -1)
    back2 = shifted(pass_on(sent2, [sent1]), "blk", -1)
    result, mark = add_rows(text_grad, back0, 0, None, [], mark=True)
    own1 = pass_on(own1, [mark])
    image_grad = scale * (image_grad + dot_tn(own1, part1))
    image_grad, mark = add_rows(image_grad, image_back, 0, None, [], mark=True)
    result = add_rows(text_grad, back1, cuts[1][0], result, [mark])
    result = add_rows(text_grad, back2, cuts[2][0], result, [])
    return image_grad, result


def solution(mesh):
    block = P(("blk", "grp"), None)
    return jax.shard_map(
        body, mesh=mesh, in_specs=(block, block, block, P(), P()), out_specs=(block, block), check_vma=False
    )
```

```python
import functools

import jax
import jax.numpy as jnp
from jax import lax
from jax.experimental import pallas as pl
from jax.experimental.pallas import tpu as pltpu
from jax.sharding import PartitionSpec as P

MIB = 2**20
ENDS = (6, 12, 23)
SMEM = pl.BlockSpec(memory_space=pltpu.SMEM)
VMEM = pl.BlockSpec(memory_space=pltpu.VMEM)
HBM = pl.BlockSpec(memory_space=pltpu.HBM)
ANY = pl.BlockSpec(memory_space=pl.ANY)


def shifted(shard, axis, by):
    devices = lax.axis_size(axis)
    return lax.ppermute(shard, axis, [(i, (i + by) % devices) for i in range(devices)])


def dot_nt(a, b):
    return lax.dot_general(a, b, (((1,), (1,)), ((), ())), preferred_element_type=jnp.float32)


def dot_tn(a, b):
    return lax.dot_general(a, b, (((0,), (0,)), ((), ())), preferred_element_type=jnp.float32)


def dot_nn(a, b):
    return jnp.dot(a, b, preferred_element_type=jnp.float32)


def row_cuts(rows):
    tiles = rows // 16
    cuts = [0] + [tiles * ends // 26 * 16 for ends in ENDS] + [rows]
    return list(zip(cuts[:-1], cuts[1:]))


def fetch(array, lo, hi, after):
    def kernel(array_ref, *refs):
        out_ref, sem = refs[-2:]
        copy = pltpu.make_async_copy(array_ref.at[pl.ds(lo, hi - lo), :], out_ref, sem)
        copy.start()
        copy.wait()

    return pl.pallas_call(
        kernel,
        out_shape=jax.ShapeDtypeStruct((hi - lo, array.shape[1]), array.dtype),
        in_specs=[ANY] * (1 + len(after)),
        out_specs=VMEM,
        scratch_shapes=[pltpu.SemaphoreType.DMA],
        compiler_params=pltpu.CompilerParams(vmem_limit_bytes=2 * MIB),
        name="fetch",
    )(array, *after)


def pass_on(array, after):
    return pl.pallas_call(
        lambda *refs: None,
        out_shape=jax.ShapeDtypeStruct(array.shape, array.dtype),
        in_specs=[ANY] * (1 + len(after)),
        out_specs=ANY,
        input_output_aliases={0: 0},
        compiler_params=pltpu.CompilerParams(vmem_limit_bytes=MIB),
        cost_estimate=pl.CostEstimate(flops=0, bytes_accessed=0, transcendentals=0),
        name="pass_on",
    )(array, *after)


def chunk_kernel(count, lasts, scale_ref, bias_ref, image_ref, next_ref, *refs):
    joined_ref, own_ref, other_ref, *sent_refs = refs[-4 - bool(lasts) :]
    scale, bias = scale_ref[0], bias_ref[0]
    start = 0
    for piece_ref in refs[:count]:
        rows = piece_ref.shape[0]
        joined_ref[start : start + rows, :] = piece_ref[...]
        start += rows
    part = joined_ref[...]
    image = image_ref[...]
    own = jax.nn.sigmoid(dot_nt(part, image) * scale + bias).astype(jnp.bfloat16)
    own_ref[...] = own
    total = dot_nn(own, image)
    image = next_ref[...]
    other = jax.nn.sigmoid(dot_nt(part, image) * scale + bias).astype(jnp.bfloat16)
    other_ref[...] = other
    total += dot_nn(other, image)
    total = (scale * total).astype(jnp.bfloat16)
    start = 0
    for sent_ref in sent_refs:
        sent_ref[...] = total[start : start + sent_ref.shape[0], :]
        start += sent_ref.shape[0]


def chunk(factor, shift, image, image_next, pieces, after, lasts=0):
    rows, (columns, width) = sum(piece.shape[0] for piece in pieces), image.shape
    text = [jax.ShapeDtypeStruct((r, width), jnp.bfloat16) for r in (rows, rows - lasts, lasts) if r]
    tile = jax.ShapeDtypeStruct((rows, columns), jnp.bfloat16)
    return pl.pallas_call(
        functools.partial(chunk_kernel, len(pieces), lasts),
        out_shape=[text[0], tile, tile, *text[1:]],
        in_specs=[SMEM] * 2 + [VMEM] * (2 + len(pieces)) + [ANY] * len(after),
        out_specs=[VMEM] * (2 + len(text)),
        compiler_params=pltpu.CompilerParams(vmem_limit_bytes=16 * MIB),
        cost_estimate=pl.CostEstimate(
            flops=8 * rows * columns * width,
            bytes_accessed=2 * (2 * columns + 3 * rows) * width,
            transcendentals=2 * rows * columns,
        ),
        name="chunk",
    )(factor, shift, image, image_next, *pieces, *after)


def add_rows(total, back, lo, result, after, mark=False):
    rows, width = back.shape
    step = rows // 16 // 3 * 16 if rows >= 96 else rows
    cuts = [(i, min(i + step, rows)) for i in range(0, rows, step)]

    def kernel(total_ref, back_ref, *refs):
        buffer, sems = refs[-2:]
        result_ref = refs[-4] if mark else refs[-3]
        copies = []
        for i, (a, b) in enumerate(cuts):
            buffer[a:b, :] = (total_ref[lo + a : lo + b, :] + back_ref[a:b, :].astype(jnp.float32)).astype(jnp.bfloat16)
            copies.append(
                pltpu.make_async_copy(
                    buffer.at[pl.ds(a, b - a), :], result_ref.at[pl.ds(lo + a, b - a), :], sems.at[i]
                )
            )
            copies[-1].start()
        if mark:
            refs[-3][...] = jnp.zeros((8, 128), jnp.float32)
        for copy in copies:
            copy.wait()

    kept = [] if result is None else [result]
    out = jax.ShapeDtypeStruct(total.shape, jnp.bfloat16)
    return pl.pallas_call(
        kernel,
        out_shape=(out, jax.ShapeDtypeStruct((8, 128), jnp.float32)) if mark else out,
        in_specs=[VMEM, VMEM] + [HBM] * len(kept) + [ANY] * len(after),
        out_specs=(HBM, VMEM) if mark else HBM,
        scratch_shapes=[pltpu.VMEM((rows, width), jnp.bfloat16), pltpu.SemaphoreType.DMA((len(cuts),))],
        input_output_aliases={2: 0} if kept else {},
        compiler_params=pltpu.CompilerParams(vmem_limit_bytes=4 * MIB),
        name="add_rows",
    )(total, back, *kept, *after)


def body(image, text, target, factor, shift):
    scale = factor[0]
    bias = shift[0]
    cuts = row_cuts(text.shape[0])
    around = shifted(text[slice(*cuts[1])], "blk", -1)
    first = text[: cuts[0][1]]
    part = [shifted(first, "blk", 1)]
    image_next = shifted(image, "grp", -1)
    part.append(shifted(fetch(text, *cuts[2], [first]), "blk", 1))

    target = fetch(target, 0, 1, [around, part[0]])
    around = shifted(around, "blk", 2)
    own = jax.nn.sigmoid(dot_nt(image, text) * scale + bias)
    column = lax.broadcasted_iota(jnp.int32, own.shape, 1)
    own = (own - (column == target[0][:, None]).astype(jnp.float32)).astype(jnp.bfloat16)
    image_grad = dot_nn(own, text)
    text_grad = dot_tn(own, image)

    image_next = pass_on(image_next, [image_grad, text_grad])
    part.append(shifted(fetch(text, *cuts[3], [image_next]), "blk", 1))
    part0, own0, next0, sent0 = chunk(factor, shift, image, image_next, [part[0], around], [])
    next_own = jax.nn.sigmoid(dot_nt(image_next, text) * scale + bias).astype(jnp.bfloat16)
    text_grad = scale * (text_grad + dot_tn(next_own, image_next))
    image_sent = dot_nn(next_own, text) + dot_tn(next0, part0)
    image_grad = image_grad + dot_tn(own0, part0)

    sent0 = pass_on(sent0, [part[1], image_sent])
    back0 = shifted(sent0, "blk", -1)

    lasts = part[2].shape[0]
    part1, own1, next1, sent1, sent2 = chunk(factor, shift, image, image_next, part[1:], [sent0], lasts)
    image_sent = (scale * (image_sent + dot_tn(next1, part1))).astype(jnp.bfloat16)
    image_back = shifted(image_sent, "grp", 1)
    sent1 = pass_on(sent1, [image_sent])
    back1 = shifted(sent1, "blk", -1)
    back2 = shifted(pass_on(sent2, [sent1]), "blk", -1)
    result, mark = add_rows(text_grad, back0, 0, None, [], mark=True)
    own1 = pass_on(own1, [mark])
    image_grad = scale * (image_grad + dot_tn(own1, part1))
    image_grad, mark = add_rows(image_grad, image_back, 0, None, [], mark=True)
    result = add_rows(text_grad, back1, cuts[2][0], result, [mark])
    result = add_rows(text_grad, back2, text.shape[0] - lasts, result, [])
    return image_grad, result


def solution(mesh):
    block = P(("blk", "grp"), None)
    return jax.shard_map(
        body, mesh=mesh, in_specs=(block, block, block, P(), P()), out_specs=(block, block), check_vma=False
    )
```

```python
import functools

import jax
import jax.numpy as jnp
from jax import lax
from jax.experimental import pallas as pl
from jax.experimental.pallas import tpu as pltpu
from jax.sharding import PartitionSpec as P

MIB = 2**20
ENDS = (6, 17, 20)
SMEM = pl.BlockSpec(memory_space=pltpu.SMEM)
VMEM = pl.BlockSpec(memory_space=pltpu.VMEM)
HBM = pl.BlockSpec(memory_space=pltpu.HBM)
ANY = pl.BlockSpec(memory_space=pl.ANY)


def shifted(shard, axis, by):
    devices = lax.axis_size(axis)
    return lax.ppermute(shard, axis, [(i, (i + by) % devices) for i in range(devices)])


def dot_nt(a, b):
    return lax.dot_general(a, b, (((1,), (1,)), ((), ())), preferred_element_type=jnp.float32)


def dot_tn(a, b):
    return lax.dot_general(a, b, (((0,), (0,)), ((), ())), preferred_element_type=jnp.float32)


def dot_nn(a, b):
    return jnp.dot(a, b, preferred_element_type=jnp.float32)


def row_cuts(rows):
    tiles = rows // 16
    cuts = [0] + [tiles * ends // 26 * 16 for ends in ENDS] + [rows]
    return list(zip(cuts[:-1], cuts[1:]))


def fetch(array, lo, hi, after):
    def kernel(array_ref, *refs):
        out_ref, sem = refs[-2:]
        copy = pltpu.make_async_copy(array_ref.at[pl.ds(lo, hi - lo), :], out_ref, sem)
        copy.start()
        copy.wait()

    return pl.pallas_call(
        kernel,
        out_shape=jax.ShapeDtypeStruct((hi - lo, array.shape[1]), array.dtype),
        in_specs=[ANY] * (1 + len(after)),
        out_specs=VMEM,
        scratch_shapes=[pltpu.SemaphoreType.DMA],
        compiler_params=pltpu.CompilerParams(vmem_limit_bytes=2 * MIB),
        name="fetch",
    )(array, *after)


def pass_on(array, after, flops=0):
    return pl.pallas_call(
        lambda *refs: None,
        out_shape=jax.ShapeDtypeStruct(array.shape, array.dtype),
        in_specs=[ANY] * (1 + len(after)),
        out_specs=ANY,
        input_output_aliases={0: 0},
        compiler_params=pltpu.CompilerParams(vmem_limit_bytes=MIB),
        cost_estimate=pl.CostEstimate(flops=flops, bytes_accessed=0, transcendentals=0),
        name="pass_on",
    )(array, *after)


def chunk_kernel(count, choice, scale_ref, bias_ref, odd_ref, image_ref, next_ref, *refs):
    sent_ref, joined_ref, own_ref, other_ref = refs[-4:]
    scale, bias = scale_ref[0], bias_ref[0]
    start = 0
    for piece_ref in refs[: count - 2 * choice]:
        rows = piece_ref.shape[0]
        joined_ref[start : start + rows, :] = piece_ref[...]
        start += rows
    if choice:

        @pl.when(odd_ref[0] != 0)
        def _():
            joined_ref[start:, :] = refs[count - 2][...]

        @pl.when(odd_ref[0] == 0)
        def _():
            joined_ref[start:, :] = refs[count - 1][...]

    part = joined_ref[...]
    image = image_ref[...]
    own = jax.nn.sigmoid(dot_nt(part, image) * scale + bias).astype(jnp.bfloat16)
    own_ref[...] = own
    total = dot_nn(own, image)
    image = next_ref[...]
    other = jax.nn.sigmoid(dot_nt(part, image) * scale + bias).astype(jnp.bfloat16)
    other_ref[...] = other
    total += dot_nn(other, image)
    sent_ref[...] = (scale * total).astype(jnp.bfloat16)


def chunk(factor, shift, odd, image, image_next, pieces, after, choice=False):
    rows, (columns, width) = sum(piece.shape[0] for piece in pieces), image.shape
    rows -= pieces[-1].shape[0] * choice
    text = jax.ShapeDtypeStruct((rows, width), jnp.bfloat16)
    tile = jax.ShapeDtypeStruct((rows, columns), jnp.bfloat16)
    return pl.pallas_call(
        functools.partial(chunk_kernel, len(pieces), choice),
        out_shape=(text, text, tile, tile),
        in_specs=[SMEM] * 3 + [VMEM] * (2 + len(pieces)) + [ANY] * len(after),
        out_specs=(VMEM,) * 4,
        compiler_params=pltpu.CompilerParams(vmem_limit_bytes=16 * MIB),
        cost_estimate=pl.CostEstimate(
            flops=8 * rows * columns * width,
            bytes_accessed=2 * (2 * columns + 3 * rows) * width,
            transcendentals=2 * rows * columns,
        ),
        name="chunk",
    )(factor, shift, odd, image, image_next, *pieces, *after)


def add_rows(total, back, lo, result, after, mark=False):
    rows, width = back.shape
    step = rows // 16 // 3 * 16 if rows >= 96 else rows
    cuts = [(i, min(i + step, rows)) for i in range(0, rows, step)]

    def kernel(total_ref, back_ref, *refs):
        buffer, sems = refs[-2:]
        result_ref = refs[-4] if mark else refs[-3]
        copies = []
        for i, (a, b) in enumerate(cuts):
            buffer[a:b, :] = (total_ref[lo + a : lo + b, :] + back_ref[a:b, :].astype(jnp.float32)).astype(jnp.bfloat16)
            copies.append(
                pltpu.make_async_copy(
                    buffer.at[pl.ds(a, b - a), :], result_ref.at[pl.ds(lo + a, b - a), :], sems.at[i]
                )
            )
            copies[-1].start()
        if mark:
            refs[-3][...] = jnp.zeros((8, 128), jnp.float32)
        for copy in copies:
            copy.wait()

    kept = [] if result is None else [result]
    out = jax.ShapeDtypeStruct(total.shape, jnp.bfloat16)
    return pl.pallas_call(
        kernel,
        out_shape=(out, jax.ShapeDtypeStruct((8, 128), jnp.float32)) if mark else out,
        in_specs=[VMEM, VMEM] + [HBM] * len(kept) + [ANY] * len(after),
        out_specs=(HBM, VMEM) if mark else HBM,
        scratch_shapes=[pltpu.VMEM((rows, width), jnp.bfloat16), pltpu.SemaphoreType.DMA((len(cuts),))],
        input_output_aliases={2: 0} if kept else {},
        compiler_params=pltpu.CompilerParams(vmem_limit_bytes=4 * MIB),
        name="add_rows",
    )(total, back, *kept, *after)


def exchanged(shard, axis):
    devices = lax.axis_size(axis)
    if devices % 2:
        return shifted(shard, axis, 1)
    return lax.ppermute(shard, axis, [(i, i ^ 1) for i in range(devices)])


def body(image, text, target, factor, shift):
    scale = factor[0]
    bias = shift[0]
    cuts = row_cuts(text.shape[0])
    odd = ((lax.axis_index("blk") % 2) | (lax.axis_size("blk") % 2)).astype(jnp.int32).reshape(1)
    around = exchanged(text[slice(*cuts[3])], "blk")
    first = text[slice(*cuts[0])]
    part = [shifted(first, "blk", 1)]
    image_next = shifted(image, "grp", -1)
    part.append(shifted(fetch(text, *cuts[1], [first]), "blk", 1))

    own = jax.nn.sigmoid(dot_nt(image, text) * scale + bias)
    column = lax.broadcasted_iota(jnp.int32, own.shape, 1)
    own = (own - (column == target[0][:, None]).astype(jnp.float32)).astype(jnp.bfloat16)
    image_grad = dot_nn(own, text)
    text_grad = dot_tn(own, image)

    part[0] = pass_on(part[0], [image_grad], 10**10)
    image_next = pass_on(image_next, [part[0], text_grad])
    part.append(shifted(fetch(text, *cuts[2], [image_next]), "blk", 1))
    next_own = jax.nn.sigmoid(dot_nt(image_next, text) * scale + bias).astype(jnp.bfloat16)
    text_grad = scale * (text_grad + dot_tn(next_own, image_next))
    image_sent = dot_nn(next_own, text)

    around = pass_on(around, [image_sent])
    two_on = shifted(around, "blk", 2)
    part[0] = pass_on(part[0], [around])
    sent0, part0, own0, next0 = chunk(factor, shift, odd, image, image_next, part[:1], [])
    image_sent = image_sent + dot_tn(next0, part0)
    image_grad = image_grad + dot_tn(own0, part0)

    sent0 = pass_on(sent0, [part[1]])
    back0 = shifted(sent0, "blk", -1)

    sent1, part1, own1, next1 = chunk(
        factor, shift, odd, image, image_next, [*part[1:], around, two_on], [sent0], choice=True
    )
    image_sent = (scale * (image_sent + dot_tn(next1, part1))).astype(jnp.bfloat16)
    image_back = shifted(image_sent, "grp", 1)
    back1 = shifted(pass_on(sent1, [image_sent]), "blk", -1)
    result, mark = add_rows(text_grad, back0, 0, None, [], mark=True)
    own1 = pass_on(own1, [mark])
    image_grad = scale * (image_grad + dot_tn(own1, part1))
    image_grad, mark = add_rows(image_grad, image_back, 0, None, [], mark=True)
    result = add_rows(text_grad, back1, cuts[1][0], result, [mark])
    return image_grad, result


def solution(mesh):
    block = P(("blk", "grp"), None)
    return jax.shard_map(
        body, mesh=mesh, in_specs=(block, block, block, P(), P()), out_specs=(block, block), check_vma=False
    )
```

```python
import functools

import jax
import jax.numpy as jnp
from jax import lax
from jax.experimental import pallas as pl
from jax.experimental.pallas import tpu as pltpu
from jax.sharding import PartitionSpec as P

MIB = 2**20
WAIT = 10**10
ENDS = (6, 17, 20)
SMEM = pl.BlockSpec(memory_space=pltpu.SMEM)
VMEM = pl.BlockSpec(memory_space=pltpu.VMEM)
HBM = pl.BlockSpec(memory_space=pltpu.HBM)
ANY = pl.BlockSpec(memory_space=pl.ANY)


def shifted(shard, axis, by):
    devices = lax.axis_size(axis)
    return lax.ppermute(shard, axis, [(i, (i + by) % devices) for i in range(devices)])


def dot_nt(a, b):
    return lax.dot_general(a, b, (((1,), (1,)), ((), ())), preferred_element_type=jnp.float32)


def dot_tn(a, b):
    return lax.dot_general(a, b, (((0,), (0,)), ((), ())), preferred_element_type=jnp.float32)


def dot_nn(a, b):
    return jnp.dot(a, b, preferred_element_type=jnp.float32)


def row_cuts(rows):
    tiles = rows // 16
    cuts = [0] + [tiles * ends // 26 * 16 for ends in ENDS] + [rows]
    return list(zip(cuts[:-1], cuts[1:]))


def fetch(array, lo, hi, after):
    def kernel(array_ref, *refs):
        out_ref, sem = refs[-2:]
        copy = pltpu.make_async_copy(array_ref.at[pl.ds(lo, hi - lo), :], out_ref, sem)
        copy.start()
        copy.wait()

    return pl.pallas_call(
        kernel,
        out_shape=jax.ShapeDtypeStruct((hi - lo, array.shape[1]), array.dtype),
        in_specs=[ANY] * (1 + len(after)),
        out_specs=VMEM,
        scratch_shapes=[pltpu.SemaphoreType.DMA],
        compiler_params=pltpu.CompilerParams(vmem_limit_bytes=2 * MIB),
        name="fetch",
    )(array, *after)


def pass_on(array, after, flops=0):
    return pl.pallas_call(
        lambda *refs: None,
        out_shape=jax.ShapeDtypeStruct(array.shape, array.dtype),
        in_specs=[ANY] * (1 + len(after)),
        out_specs=ANY,
        input_output_aliases={0: 0},
        compiler_params=pltpu.CompilerParams(vmem_limit_bytes=MIB),
        cost_estimate=pl.CostEstimate(flops=flops, bytes_accessed=0, transcendentals=0),
        name="pass_on",
    )(array, *after)


def chunk_kernel(count, choice, scale_ref, bias_ref, odd_ref, image_ref, next_ref, *refs):
    sent_ref, joined_ref, own_ref, other_ref = refs[-4:]
    scale, bias = scale_ref[0], bias_ref[0]
    start = 0
    for piece_ref in refs[: count - 2 * choice]:
        rows = piece_ref.shape[0]
        joined_ref[start : start + rows, :] = piece_ref[...]
        start += rows
    if choice:

        @pl.when(odd_ref[0] != 0)
        def _():
            joined_ref[start:, :] = refs[count - 2][...]

        @pl.when(odd_ref[0] == 0)
        def _():
            joined_ref[start:, :] = refs[count - 1][...]

    part = joined_ref[...]
    image = image_ref[...]
    own = jax.nn.sigmoid(dot_nt(part, image) * scale + bias).astype(jnp.bfloat16)
    own_ref[...] = own
    total = dot_nn(own, image)
    image = next_ref[...]
    other = jax.nn.sigmoid(dot_nt(part, image) * scale + bias).astype(jnp.bfloat16)
    other_ref[...] = other
    total += dot_nn(other, image)
    sent_ref[...] = (scale * total).astype(jnp.bfloat16)


def chunk(factor, shift, odd, image, image_next, pieces, after, choice=False):
    rows, (columns, width) = sum(piece.shape[0] for piece in pieces), image.shape
    rows -= pieces[-1].shape[0] * choice
    text = jax.ShapeDtypeStruct((rows, width), jnp.bfloat16)
    tile = jax.ShapeDtypeStruct((rows, columns), jnp.bfloat16)
    return pl.pallas_call(
        functools.partial(chunk_kernel, len(pieces), choice),
        out_shape=(text, text, tile, tile),
        in_specs=[SMEM] * 3 + [VMEM] * (2 + len(pieces)) + [ANY] * len(after),
        out_specs=(VMEM,) * 4,
        compiler_params=pltpu.CompilerParams(vmem_limit_bytes=16 * MIB),
        cost_estimate=pl.CostEstimate(
            flops=8 * rows * columns * width,
            bytes_accessed=2 * (2 * columns + 3 * rows) * width,
            transcendentals=2 * rows * columns,
        ),
        name="chunk",
    )(factor, shift, odd, image, image_next, *pieces, *after)


def add_rows(total, back, lo, result, after, mark=False):
    rows, width = back.shape
    step = rows // 16 // 3 * 16 if rows >= 96 else rows
    cuts = [(i, min(i + step, rows)) for i in range(0, rows, step)]

    def kernel(total_ref, back_ref, *refs):
        buffer, sems = refs[-2:]
        result_ref = refs[-4] if mark else refs[-3]
        copies = []
        for i, (a, b) in enumerate(cuts):
            buffer[a:b, :] = (total_ref[lo + a : lo + b, :] + back_ref[a:b, :].astype(jnp.float32)).astype(jnp.bfloat16)
            copies.append(
                pltpu.make_async_copy(
                    buffer.at[pl.ds(a, b - a), :], result_ref.at[pl.ds(lo + a, b - a), :], sems.at[i]
                )
            )
            copies[-1].start()
        if mark:
            refs[-3][...] = jnp.zeros((8, 128), jnp.float32)
        for copy in copies:
            copy.wait()

    kept = [] if result is None else [result]
    out = jax.ShapeDtypeStruct(total.shape, jnp.bfloat16)
    return pl.pallas_call(
        kernel,
        out_shape=(out, jax.ShapeDtypeStruct((8, 128), jnp.float32)) if mark else out,
        in_specs=[VMEM, VMEM] + [HBM] * len(kept) + [ANY] * len(after),
        out_specs=(HBM, VMEM) if mark else HBM,
        scratch_shapes=[pltpu.VMEM((rows, width), jnp.bfloat16), pltpu.SemaphoreType.DMA((len(cuts),))],
        input_output_aliases={2: 0} if kept else {},
        compiler_params=pltpu.CompilerParams(vmem_limit_bytes=4 * MIB),
        name="add_rows",
    )(total, back, *kept, *after)


def exchanged(shard, axis):
    devices = lax.axis_size(axis)
    if devices % 2:
        return shifted(shard, axis, 1)
    return lax.ppermute(shard, axis, [(i, i ^ 1) for i in range(devices)])


def body(image, text, target, factor, shift):
    scale = factor[0]
    bias = shift[0]
    cuts = row_cuts(text.shape[0])
    odd = ((lax.axis_index("blk") % 2) | (lax.axis_size("blk") % 2)).astype(jnp.int32).reshape(1)
    around = exchanged(text[slice(*cuts[3])], "blk")
    first = text[slice(*cuts[0])]
    part = [shifted(first, "blk", 1)]
    image_next = shifted(image, "grp", -1)
    part.append(shifted(fetch(text, *cuts[1], [first]), "blk", 1))

    own = jax.nn.sigmoid(dot_nt(image, text) * scale + bias)
    column = lax.broadcasted_iota(jnp.int32, own.shape, 1)
    own = (own - (column == target[0][:, None]).astype(jnp.float32)).astype(jnp.bfloat16)
    image_grad = dot_nn(own, text)
    text_grad = dot_tn(own, image)

    part[0] = pass_on(part[0], [image_grad], WAIT)
    image_next = pass_on(image_next, [part[0], text_grad])
    last = fetch(text, *cuts[2], [image_next])
    part.append(shifted(last, "blk", 1))
    next_own = jax.nn.sigmoid(dot_nt(image_next, text) * scale + bias).astype(jnp.bfloat16)
    text_grad = scale * (text_grad + dot_tn(next_own, image_next))
    image_sent = dot_nn(next_own, text)

    around = pass_on(around, [image_sent, last])
    two_on = shifted(around, "blk", 2)
    sent0, part0, own0, next0 = chunk(factor, shift, odd, image, image_next, part[:2], [around])
    back0 = shifted(sent0, "blk", -1)
    image_sent = image_sent + dot_tn(next0, part0)
    image_grad = image_grad + dot_tn(own0, part0)

    part[2] = pass_on(part[2], [sent0], WAIT)
    two_on = pass_on(two_on, [part[2]])
    sent1, part1, own1, next1 = chunk(
        factor, shift, odd, image, image_next, [part[2], around, two_on], [sent0], choice=True
    )
    image_sent = (scale * (image_sent + dot_tn(next1, part1))).astype(jnp.bfloat16)
    image_back = shifted(image_sent, "grp", 1)
    back1 = shifted(pass_on(sent1, [image_sent]), "blk", -1)
    result, mark = add_rows(text_grad, back0, 0, None, [], mark=True)
    own1 = pass_on(own1, [mark])
    image_grad = scale * (image_grad + dot_tn(own1, part1))
    image_grad, mark = add_rows(image_grad, image_back, 0, None, [], mark=True)
    result = add_rows(text_grad, back1, cuts[2][0], result, [mark])
    return image_grad, result


def solution(mesh):
    block = P(("blk", "grp"), None)
    return jax.shard_map(
        body, mesh=mesh, in_specs=(block, block, block, P(), P()), out_specs=(block, block), check_vma=False
    )
```

```python
import functools

import jax
import jax.numpy as jnp
from jax import lax
from jax.experimental import pallas as pl
from jax.experimental.pallas import tpu as pltpu
from jax.sharding import PartitionSpec as P

MIB = 2**20
ENDS = (8, 23)
SMEM = pl.BlockSpec(memory_space=pltpu.SMEM)
VMEM = pl.BlockSpec(memory_space=pltpu.VMEM)
HBM = pl.BlockSpec(memory_space=pltpu.HBM)
ANY = pl.BlockSpec(memory_space=pl.ANY)


def shifted(shard, axis, by):
    devices = lax.axis_size(axis)
    return lax.ppermute(shard, axis, [(i, (i + by) % devices) for i in range(devices)])


def dot_nt(a, b):
    return lax.dot_general(a, b, (((1,), (1,)), ((), ())), preferred_element_type=jnp.float32)


def dot_tn(a, b):
    return lax.dot_general(a, b, (((0,), (0,)), ((), ())), preferred_element_type=jnp.float32)


def dot_nn(a, b):
    return jnp.dot(a, b, preferred_element_type=jnp.float32)


def row_cuts(rows):
    tiles = rows // 16
    cuts = [0] + [tiles * ends // 26 * 16 for ends in ENDS] + [rows]
    return list(zip(cuts[:-1], cuts[1:]))


def fetch(array, lo, hi, after, limit=2 * MIB):
    def kernel(array_ref, *refs):
        out_ref, sem = refs[-2:]
        copy = pltpu.make_async_copy(array_ref.at[pl.ds(lo, hi - lo), :], out_ref, sem)
        copy.start()
        copy.wait()

    return pl.pallas_call(
        kernel,
        out_shape=jax.ShapeDtypeStruct((hi - lo, array.shape[1]), array.dtype),
        in_specs=[ANY] * (1 + len(after)),
        out_specs=VMEM,
        scratch_shapes=[pltpu.SemaphoreType.DMA],
        compiler_params=pltpu.CompilerParams(vmem_limit_bytes=limit),
        name="fetch",
    )(array, *after)


def pass_on(array, after):
    return pl.pallas_call(
        lambda *refs: None,
        out_shape=jax.ShapeDtypeStruct(array.shape, array.dtype),
        in_specs=[ANY] * (1 + len(after)),
        out_specs=ANY,
        input_output_aliases={0: 0},
        compiler_params=pltpu.CompilerParams(vmem_limit_bytes=MIB),
        name="pass_on",
    )(array, *after)


def chunk_kernel(count, lasts, scale_ref, bias_ref, image_ref, next_ref, *refs):
    joined_ref, own_ref, other_ref, *sent_refs = refs[-4 - bool(lasts) :]
    scale, bias = scale_ref[0], bias_ref[0]
    start = 0
    for piece_ref in refs[:count]:
        rows = piece_ref.shape[0]
        joined_ref[start : start + rows, :] = piece_ref[...]
        start += rows
    part = joined_ref[...]
    image = image_ref[...]
    own = jax.nn.sigmoid(dot_nt(part, image) * scale + bias).astype(jnp.bfloat16)
    own_ref[...] = own
    total = dot_nn(own, image)
    image = next_ref[...]
    other = jax.nn.sigmoid(dot_nt(part, image) * scale + bias).astype(jnp.bfloat16)
    other_ref[...] = other
    total += dot_nn(other, image)
    total = (scale * total).astype(jnp.bfloat16)
    start = 0
    for sent_ref in sent_refs:
        sent_ref[...] = total[start : start + sent_ref.shape[0], :]
        start += sent_ref.shape[0]


def chunk(factor, shift, image, image_next, pieces, after, lasts=0):
    rows, (columns, width) = sum(piece.shape[0] for piece in pieces), image.shape
    text = [jax.ShapeDtypeStruct((r, width), jnp.bfloat16) for r in (rows, rows - lasts, lasts) if r]
    tile = jax.ShapeDtypeStruct((rows, columns), jnp.bfloat16)
    return pl.pallas_call(
        functools.partial(chunk_kernel, len(pieces), lasts),
        out_shape=[text[0], tile, tile, *text[1:]],
        in_specs=[SMEM] * 2 + [VMEM] * (2 + len(pieces)) + [ANY] * len(after),
        out_specs=[VMEM] * (2 + len(text)),
        compiler_params=pltpu.CompilerParams(vmem_limit_bytes=16 * MIB),
        cost_estimate=pl.CostEstimate(
            flops=8 * rows * columns * width,
            bytes_accessed=2 * (2 * columns + 3 * rows) * width,
            transcendentals=2 * rows * columns,
        ),
        name="chunk",
    )(factor, shift, image, image_next, *pieces, *after)


def add_rows(total, back, lo, result, after, mark=False):
    rows, width = back.shape
    step = rows // 16 // 3 * 16 if rows >= 96 else rows
    cuts = [(i, min(i + step, rows)) for i in range(0, rows, step)]

    def kernel(total_ref, back_ref, *refs):
        buffer, sems = refs[-2:]
        result_ref = refs[-4] if mark else refs[-3]
        copies = []
        for i, (a, b) in enumerate(cuts):
            buffer[a:b, :] = (total_ref[lo + a : lo + b, :] + back_ref[a:b, :].astype(jnp.float32)).astype(jnp.bfloat16)
            copies.append(
                pltpu.make_async_copy(
                    buffer.at[pl.ds(a, b - a), :], result_ref.at[pl.ds(lo + a, b - a), :], sems.at[i]
                )
            )
            copies[-1].start()
        if mark:
            refs[-3][...] = jnp.zeros((8, 128), jnp.float32)
        for copy in copies:
            copy.wait()

    kept = [] if result is None else [result]
    out = jax.ShapeDtypeStruct(total.shape, jnp.bfloat16)
    return pl.pallas_call(
        kernel,
        out_shape=(out, jax.ShapeDtypeStruct((8, 128), jnp.float32)) if mark else out,
        in_specs=[VMEM, VMEM] + [HBM] * len(kept) + [ANY] * len(after),
        out_specs=(HBM, VMEM) if mark else HBM,
        scratch_shapes=[pltpu.VMEM((rows, width), jnp.bfloat16), pltpu.SemaphoreType.DMA((len(cuts),))],
        input_output_aliases={2: 0} if kept else {},
        compiler_params=pltpu.CompilerParams(vmem_limit_bytes=4 * MIB),
        name="add_rows",
    )(total, back, *kept, *after)


def body(image, text, target, factor, shift):
    scale = factor[0]
    bias = shift[0]
    cuts = row_cuts(text.shape[0])
    first = fetch(text, *cuts[0], [], 53 * MIB + MIB // 4)
    part = [shifted(first, "blk", 1)]
    image_next = shifted(image, "grp", -1)
    part.append(shifted(fetch(text, *cuts[1], [first]), "blk", 1))

    target = fetch(target, 0, 1, [part[0]])
    own = jax.nn.sigmoid(dot_nt(image, text) * scale + bias)
    column = lax.broadcasted_iota(jnp.int32, own.shape, 1)
    own = (own - (column == target[0][:, None]).astype(jnp.float32)).astype(jnp.bfloat16)
    part.append(shifted(fetch(text, *cuts[2], [own]), "blk", 1))
    image_grad = dot_nn(own, text)
    text_grad = dot_tn(own, image)

    image_next = pass_on(image_next, [image_grad, text_grad])
    part0, own0, next0, sent0 = chunk(factor, shift, image, image_next, part[:1], [])
    next_own = jax.nn.sigmoid(dot_nt(image_next, text) * scale + bias).astype(jnp.bfloat16)
    text_grad = scale * (text_grad + dot_tn(next_own, image_next))
    image_sent = dot_nn(next_own, text) + dot_tn(next0, part0)
    image_grad = image_grad + dot_tn(own0, part0)

    sent0 = pass_on(sent0, [part[1], image_sent])
    back0 = shifted(sent0, "blk", -1)

    lasts = part[2].shape[0]
    part1, own1, next1, sent1, sent2 = chunk(factor, shift, image, image_next, part[1:], [sent0], lasts)
    image_sent = (scale * (image_sent + dot_tn(next1, part1))).astype(jnp.bfloat16)
    image_back = shifted(image_sent, "grp", 1)
    sent1 = pass_on(sent1, [image_sent])
    back1 = shifted(sent1, "blk", -1)
    back2 = shifted(pass_on(sent2, [sent1]), "blk", -1)
    result, mark = add_rows(text_grad, back0, 0, None, [], mark=True)
    own1 = pass_on(own1, [mark])
    image_grad = scale * (image_grad + dot_tn(own1, part1))
    image_grad, mark = add_rows(image_grad, image_back, 0, None, [], mark=True)
    result = add_rows(text_grad, back1, cuts[1][0], result, [mark])
    result = add_rows(text_grad, back2, cuts[2][0], result, [])
    return image_grad, result


def solution(mesh):
    block = P(("blk", "grp"), None)
    return jax.shard_map(
        body, mesh=mesh, in_specs=(block, block, block, P(), P()), out_specs=(block, block), check_vma=False
    )
```

```python
import functools

import jax
import jax.numpy as jnp
from jax import lax
from jax.experimental import pallas as pl
from jax.experimental.pallas import tpu as pltpu
from jax.sharding import PartitionSpec as P

MIB = 2**20
ENDS = (8, 23)
SMEM = pl.BlockSpec(memory_space=pltpu.SMEM)
VMEM = pl.BlockSpec(memory_space=pltpu.VMEM)
HBM = pl.BlockSpec(memory_space=pltpu.HBM)
ANY = pl.BlockSpec(memory_space=pl.ANY)


def shifted(shard, axis, by):
    devices = lax.axis_size(axis)
    return lax.ppermute(shard, axis, [(i, (i + by) % devices) for i in range(devices)])


def dot_nt(a, b):
    return lax.dot_general(a, b, (((1,), (1,)), ((), ())), preferred_element_type=jnp.float32)


def dot_tn(a, b):
    return lax.dot_general(a, b, (((0,), (0,)), ((), ())), preferred_element_type=jnp.float32)


def dot_nn(a, b):
    return jnp.dot(a, b, preferred_element_type=jnp.float32)


def row_cuts(rows):
    tiles = rows // 16
    cuts = [0] + [tiles * ends // 26 * 16 for ends in ENDS] + [rows]
    return list(zip(cuts[:-1], cuts[1:]))


def fetch(array, lo, hi, after):
    def kernel(array_ref, *refs):
        out_ref, sem = refs[-2:]
        copy = pltpu.make_async_copy(array_ref.at[pl.ds(lo, hi - lo), :], out_ref, sem)
        copy.start()
        copy.wait()

    return pl.pallas_call(
        kernel,
        out_shape=jax.ShapeDtypeStruct((hi - lo, array.shape[1]), array.dtype),
        in_specs=[ANY] * (1 + len(after)),
        out_specs=VMEM,
        scratch_shapes=[pltpu.SemaphoreType.DMA],
        compiler_params=pltpu.CompilerParams(vmem_limit_bytes=2 * MIB),
        name="fetch",
    )(array, *after)


def pass_on(array, after):
    return pl.pallas_call(
        lambda *refs: None,
        out_shape=jax.ShapeDtypeStruct(array.shape, array.dtype),
        in_specs=[ANY] * (1 + len(after)),
        out_specs=ANY,
        input_output_aliases={0: 0},
        compiler_params=pltpu.CompilerParams(vmem_limit_bytes=MIB),
        name="pass_on",
    )(array, *after)


def chunk_kernel(count, lasts, scale_ref, bias_ref, image_ref, next_ref, *refs):
    joined_ref, own_ref, other_ref, *sent_refs = refs[-4 - bool(lasts) :]
    scale, bias = scale_ref[0], bias_ref[0]
    start = 0
    for piece_ref in refs[:count]:
        rows = piece_ref.shape[0]
        joined_ref[start : start + rows, :] = piece_ref[...]
        start += rows
    part = joined_ref[...]
    image = image_ref[...]
    own = jax.nn.sigmoid(dot_nt(part, image) * scale + bias).astype(jnp.bfloat16)
    own_ref[...] = own
    total = dot_nn(own, image)
    image = next_ref[...]
    other = jax.nn.sigmoid(dot_nt(part, image) * scale + bias).astype(jnp.bfloat16)
    other_ref[...] = other
    total += dot_nn(other, image)
    total = (scale * total).astype(jnp.bfloat16)
    start = 0
    for sent_ref in sent_refs:
        sent_ref[...] = total[start : start + sent_ref.shape[0], :]
        start += sent_ref.shape[0]


def chunk(factor, shift, image, image_next, pieces, after, lasts=0):
    rows, (columns, width) = sum(piece.shape[0] for piece in pieces), image.shape
    text = [jax.ShapeDtypeStruct((r, width), jnp.bfloat16) for r in (rows, rows - lasts, lasts) if r]
    tile = jax.ShapeDtypeStruct((rows, columns), jnp.bfloat16)
    return pl.pallas_call(
        functools.partial(chunk_kernel, len(pieces), lasts),
        out_shape=[text[0], tile, tile, *text[1:]],
        in_specs=[SMEM] * 2 + [VMEM] * (2 + len(pieces)) + [ANY] * len(after),
        out_specs=[VMEM] * (2 + len(text)),
        compiler_params=pltpu.CompilerParams(vmem_limit_bytes=16 * MIB),
        cost_estimate=pl.CostEstimate(
            flops=8 * rows * columns * width,
            bytes_accessed=2 * (2 * columns + 3 * rows) * width,
            transcendentals=2 * rows * columns,
        ),
        name="chunk",
    )(factor, shift, image, image_next, *pieces, *after)


def add_rows(total, back, lo, result, after, mark=False):
    rows, width = back.shape
    step = rows // 16 // 3 * 16 if rows >= 96 else rows
    cuts = [(i, min(i + step, rows)) for i in range(0, rows, step)]

    def kernel(total_ref, back_ref, *refs):
        buffer, sems = refs[-2:]
        result_ref = refs[-4] if mark else refs[-3]
        copies = []
        for i, (a, b) in enumerate(cuts):
            buffer[a:b, :] = (total_ref[lo + a : lo + b, :] + back_ref[a:b, :].astype(jnp.float32)).astype(jnp.bfloat16)
            copies.append(
                pltpu.make_async_copy(
                    buffer.at[pl.ds(a, b - a), :], result_ref.at[pl.ds(lo + a, b - a), :], sems.at[i]
                )
            )
            copies[-1].start()
        if mark:
            refs[-3][...] = jnp.zeros((8, 128), jnp.float32)
        for copy in copies:
            copy.wait()

    kept = [] if result is None else [result]
    out = jax.ShapeDtypeStruct(total.shape, jnp.bfloat16)
    return pl.pallas_call(
        kernel,
        out_shape=(out, jax.ShapeDtypeStruct((8, 128), jnp.float32)) if mark else out,
        in_specs=[VMEM, VMEM] + [HBM] * len(kept) + [ANY] * len(after),
        out_specs=(HBM, VMEM) if mark else HBM,
        scratch_shapes=[pltpu.VMEM((rows, width), jnp.bfloat16), pltpu.SemaphoreType.DMA((len(cuts),))],
        input_output_aliases={2: 0} if kept else {},
        compiler_params=pltpu.CompilerParams(vmem_limit_bytes=4 * MIB),
        name="add_rows",
    )(total, back, *kept, *after)


def body(image, text, target, factor, shift):
    scale = factor[0]
    bias = shift[0]
    cuts = row_cuts(text.shape[0])
    first = text[: cuts[0][1]]
    part = [shifted(first, "blk", 1)]
    image_next = shifted(image, "grp", -1)
    part.append(shifted(fetch(text, *cuts[1], [first]), "blk", 1))

    target = fetch(target, 0, 1, [part[0]])
    own = jax.nn.sigmoid(dot_nt(image, text) * scale + bias)
    column = lax.broadcasted_iota(jnp.int32, own.shape, 1)
    own = (own - (column == target[0][:, None]).astype(jnp.float32)).astype(jnp.bfloat16)
    part.append(shifted(fetch(text, *cuts[2], [own]), "blk", 1))
    image_grad = dot_nn(own, text)
    text_grad = dot_tn(own, image)

    image_next = pass_on(image_next, [image_grad, text_grad])
    part0, own0, next0, sent0 = chunk(factor, shift, image, image_next, part[:1], [])
    next_own = jax.nn.sigmoid(dot_nt(image_next, text) * scale + bias).astype(jnp.bfloat16)
    text_grad = scale * (text_grad + dot_tn(next_own, image_next))
    image_sent = dot_nn(next_own, text) + dot_tn(next0, part0)
    image_grad = image_grad + dot_tn(own0, part0)

    back0 = shifted(sent0, "blk", -1)

    lasts = part[2].shape[0]
    part1, own1, next1, sent1, sent2 = chunk(factor, shift, image, image_next, part[1:], [sent0, image_sent], lasts)
    image_sent = (scale * (image_sent + dot_tn(next1, part1))).astype(jnp.bfloat16)
    image_back = shifted(image_sent, "grp", 1)
    sent1 = pass_on(sent1, [image_sent])
    back1 = shifted(sent1, "blk", -1)
    back2 = shifted(pass_on(sent2, [sent1]), "blk", -1)
    result, mark = add_rows(text_grad, back0, 0, None, [], mark=True)
    own1 = pass_on(own1, [mark])
    image_grad = scale * (image_grad + dot_tn(own1, part1))
    image_grad, mark = add_rows(image_grad, image_back, 0, None, [], mark=True)
    result = add_rows(text_grad, back1, cuts[1][0], result, [mark])
    result = add_rows(text_grad, back2, cuts[2][0], result, [])
    return image_grad, result


def solution(mesh):
    block = P(("blk", "grp"), None)
    return jax.shard_map(
        body, mesh=mesh, in_specs=(block, block, block, P(), P()), out_specs=(block, block), check_vma=False
    )
```

```python
import functools

import jax
import jax.numpy as jnp
from jax import lax
from jax.experimental import pallas as pl
from jax.experimental.pallas import tpu as pltpu
from jax.sharding import PartitionSpec as P

MIB = 2**20
ENDS = (8, 23)
SMEM = pl.BlockSpec(memory_space=pltpu.SMEM)
VMEM = pl.BlockSpec(memory_space=pltpu.VMEM)
HBM = pl.BlockSpec(memory_space=pltpu.HBM)
ANY = pl.BlockSpec(memory_space=pl.ANY)


def shifted(shard, axis, by):
    devices = lax.axis_size(axis)
    return lax.ppermute(shard, axis, [(i, (i + by) % devices) for i in range(devices)])


def dot_nt(a, b):
    return lax.dot_general(a, b, (((1,), (1,)), ((), ())), preferred_element_type=jnp.float32)


def dot_tn(a, b):
    return lax.dot_general(a, b, (((0,), (0,)), ((), ())), preferred_element_type=jnp.float32)


def dot_nn(a, b):
    return jnp.dot(a, b, preferred_element_type=jnp.float32)


def row_cuts(rows):
    tiles = rows // 16
    cuts = [0] + [tiles * ends // 26 * 16 for ends in ENDS] + [rows]
    return list(zip(cuts[:-1], cuts[1:]))


def fetch(array, lo, hi, after):
    def kernel(array_ref, *refs):
        out_ref, sem = refs[-2:]
        copy = pltpu.make_async_copy(array_ref.at[pl.ds(lo, hi - lo), :], out_ref, sem)
        copy.start()
        copy.wait()

    return pl.pallas_call(
        kernel,
        out_shape=jax.ShapeDtypeStruct((hi - lo, array.shape[1]), array.dtype),
        in_specs=[ANY] * (1 + len(after)),
        out_specs=VMEM,
        scratch_shapes=[pltpu.SemaphoreType.DMA],
        compiler_params=pltpu.CompilerParams(vmem_limit_bytes=2 * MIB),
        name="fetch",
    )(array, *after)


def pass_on(array, after, flops=0):
    return pl.pallas_call(
        lambda *refs: None,
        out_shape=jax.ShapeDtypeStruct(array.shape, array.dtype),
        in_specs=[ANY] * (1 + len(after)),
        out_specs=ANY,
        input_output_aliases={0: 0},
        compiler_params=pltpu.CompilerParams(vmem_limit_bytes=MIB),
        cost_estimate=pl.CostEstimate(flops=flops, bytes_accessed=0, transcendentals=0),
        name="pass_on",
    )(array, *after)


def chunk_kernel(count, lasts, scale_ref, bias_ref, image_ref, next_ref, *refs):
    joined_ref, own_ref, other_ref, *sent_refs = refs[-4 - bool(lasts) :]
    scale, bias = scale_ref[0], bias_ref[0]
    start = 0
    for piece_ref in refs[:count]:
        rows = piece_ref.shape[0]
        joined_ref[start : start + rows, :] = piece_ref[...]
        start += rows
    part = joined_ref[...]
    image = image_ref[...]
    own = jax.nn.sigmoid(dot_nt(part, image) * scale + bias).astype(jnp.bfloat16)
    own_ref[...] = own
    total = dot_nn(own, image)
    image = next_ref[...]
    other = jax.nn.sigmoid(dot_nt(part, image) * scale + bias).astype(jnp.bfloat16)
    other_ref[...] = other
    total += dot_nn(other, image)
    total = (scale * total).astype(jnp.bfloat16)
    start = 0
    for sent_ref in sent_refs:
        sent_ref[...] = total[start : start + sent_ref.shape[0], :]
        start += sent_ref.shape[0]


def chunk(factor, shift, image, image_next, pieces, after, lasts=0):
    rows, (columns, width) = sum(piece.shape[0] for piece in pieces), image.shape
    text = [jax.ShapeDtypeStruct((r, width), jnp.bfloat16) for r in (rows, rows - lasts, lasts) if r]
    tile = jax.ShapeDtypeStruct((rows, columns), jnp.bfloat16)
    return pl.pallas_call(
        functools.partial(chunk_kernel, len(pieces), lasts),
        out_shape=[text[0], tile, tile, *text[1:]],
        in_specs=[SMEM] * 2 + [VMEM] * (2 + len(pieces)) + [ANY] * len(after),
        out_specs=[VMEM] * (2 + len(text)),
        compiler_params=pltpu.CompilerParams(vmem_limit_bytes=16 * MIB),
        cost_estimate=pl.CostEstimate(
            flops=8 * rows * columns * width,
            bytes_accessed=2 * (2 * columns + 3 * rows) * width,
            transcendentals=2 * rows * columns,
        ),
        name="chunk",
    )(factor, shift, image, image_next, *pieces, *after)


def add_rows(total, back, lo, result, after, mark=False):
    rows, width = back.shape
    step = rows // 16 // 3 * 16 if rows >= 96 else rows
    cuts = [(i, min(i + step, rows)) for i in range(0, rows, step)]

    def kernel(total_ref, back_ref, *refs):
        buffer, sems = refs[-2:]
        result_ref = refs[-4] if mark else refs[-3]
        copies = []
        for i, (a, b) in enumerate(cuts):
            buffer[a:b, :] = (total_ref[lo + a : lo + b, :] + back_ref[a:b, :].astype(jnp.float32)).astype(jnp.bfloat16)
            copies.append(
                pltpu.make_async_copy(
                    buffer.at[pl.ds(a, b - a), :], result_ref.at[pl.ds(lo + a, b - a), :], sems.at[i]
                )
            )
            copies[-1].start()
        if mark:
            refs[-3][...] = jnp.zeros((8, 128), jnp.float32)
        for copy in copies:
            copy.wait()

    kept = [] if result is None else [result]
    out = jax.ShapeDtypeStruct(total.shape, jnp.bfloat16)
    return pl.pallas_call(
        kernel,
        out_shape=(out, jax.ShapeDtypeStruct((8, 128), jnp.float32)) if mark else out,
        in_specs=[VMEM, VMEM] + [HBM] * len(kept) + [ANY] * len(after),
        out_specs=(HBM, VMEM) if mark else HBM,
        scratch_shapes=[pltpu.VMEM((rows, width), jnp.bfloat16), pltpu.SemaphoreType.DMA((len(cuts),))],
        input_output_aliases={2: 0} if kept else {},
        compiler_params=pltpu.CompilerParams(vmem_limit_bytes=4 * MIB),
        name="add_rows",
    )(total, back, *kept, *after)


def body(image, text, target, factor, shift):
    scale = factor[0]
    bias = shift[0]
    cuts = row_cuts(text.shape[0])
    first = text[: cuts[0][1]]
    part = [shifted(first, "blk", 1)]
    image_next = shifted(image, "grp", -1)
    part.append(shifted(fetch(text, *cuts[1], [first]), "blk", 1))

    target = pass_on(fetch(target, 0, 1, [part[0]]), [], 2 * 10**10)
    own = jax.nn.sigmoid(dot_nt(image, text) * scale + bias)
    column = lax.broadcasted_iota(jnp.int32, own.shape, 1)
    own = (own - (column == target[0][:, None]).astype(jnp.float32)).astype(jnp.bfloat16)
    part.append(shifted(fetch(text, *cuts[2], [own]), "blk", 1))
    image_grad = dot_nn(own, text)
    text_grad = dot_tn(own, image)

    image_next = pass_on(image_next, [image_grad, text_grad])
    part0, own0, next0, sent0 = chunk(factor, shift, image, image_next, part[:1], [])
    next_own = jax.nn.sigmoid(dot_nt(image_next, text) * scale + bias).astype(jnp.bfloat16)
    text_grad = scale * (text_grad + dot_tn(next_own, image_next))
    image_sent = dot_nn(next_own, text) + dot_tn(next0, part0)
    image_grad = image_grad + dot_tn(own0, part0)

    sent0 = pass_on(sent0, [part[1], image_sent])
    back0 = shifted(sent0, "blk", -1)

    lasts = part[2].shape[0]
    part1, own1, next1, sent1, sent2 = chunk(factor, shift, image, image_next, part[1:], [sent0], lasts)
    image_sent = (scale * (image_sent + dot_tn(next1, part1))).astype(jnp.bfloat16)
    image_back = shifted(image_sent, "grp", 1)
    sent1 = pass_on(sent1, [image_sent])
    back1 = shifted(sent1, "blk", -1)
    back2 = shifted(pass_on(sent2, [sent1]), "blk", -1)
    result, mark = add_rows(text_grad, back0, 0, None, [], mark=True)
    own1 = pass_on(own1, [mark])
    image_grad = scale * (image_grad + dot_tn(own1, part1))
    image_grad, mark = add_rows(image_grad, image_back, 0, None, [], mark=True)
    result = add_rows(text_grad, back1, cuts[1][0], result, [mark])
    result = add_rows(text_grad, back2, cuts[2][0], result, [])
    return image_grad, result


def solution(mesh):
    block = P(("blk", "grp"), None)
    return jax.shard_map(
        body, mesh=mesh, in_specs=(block, block, block, P(), P()), out_specs=(block, block), check_vma=False
    )
```

```python
import functools

import jax
import jax.numpy as jnp
from jax import lax
from jax.experimental import pallas as pl
from jax.experimental.pallas import tpu as pltpu
from jax.sharding import PartitionSpec as P

MIB = 2**20
ENDS = (8, 24)
SMEM = pl.BlockSpec(memory_space=pltpu.SMEM)
VMEM = pl.BlockSpec(memory_space=pltpu.VMEM)
HBM = pl.BlockSpec(memory_space=pltpu.HBM)
ANY = pl.BlockSpec(memory_space=pl.ANY)


def shifted(shard, axis, by):
    devices = lax.axis_size(axis)
    return lax.ppermute(shard, axis, [(i, (i + by) % devices) for i in range(devices)])


def dot_nt(a, b):
    return lax.dot_general(a, b, (((1,), (1,)), ((), ())), preferred_element_type=jnp.float32)


def dot_tn(a, b):
    return lax.dot_general(a, b, (((0,), (0,)), ((), ())), preferred_element_type=jnp.float32)


def dot_nn(a, b):
    return jnp.dot(a, b, preferred_element_type=jnp.float32)


def row_cuts(rows):
    tiles = rows // 16
    cuts = [0] + [tiles * ends // 26 * 16 for ends in ENDS] + [rows]
    return list(zip(cuts[:-1], cuts[1:]))


def fetch(array, lo, hi, after):
    def kernel(array_ref, *refs):
        out_ref, sem = refs[-2:]
        copy = pltpu.make_async_copy(array_ref.at[pl.ds(lo, hi - lo), :], out_ref, sem)
        copy.start()
        copy.wait()

    return pl.pallas_call(
        kernel,
        out_shape=jax.ShapeDtypeStruct((hi - lo, array.shape[1]), array.dtype),
        in_specs=[ANY] * (1 + len(after)),
        out_specs=VMEM,
        scratch_shapes=[pltpu.SemaphoreType.DMA],
        compiler_params=pltpu.CompilerParams(vmem_limit_bytes=2 * MIB),
        name="fetch",
    )(array, *after)


def pass_on(array, after, flops=0):
    return pl.pallas_call(
        lambda *refs: None,
        out_shape=jax.ShapeDtypeStruct(array.shape, array.dtype),
        in_specs=[ANY] * (1 + len(after)),
        out_specs=ANY,
        input_output_aliases={0: 0},
        compiler_params=pltpu.CompilerParams(vmem_limit_bytes=MIB),
        cost_estimate=pl.CostEstimate(flops=flops, bytes_accessed=0, transcendentals=0),
        name="pass_on",
    )(array, *after)


def chunk_kernel(count, lasts, scale_ref, bias_ref, image_ref, next_ref, *refs):
    joined_ref, own_ref, other_ref, *sent_refs = refs[-4 - bool(lasts) :]
    scale, bias = scale_ref[0], bias_ref[0]
    start = 0
    for piece_ref in refs[:count]:
        rows = piece_ref.shape[0]
        joined_ref[start : start + rows, :] = piece_ref[...]
        start += rows
    part = joined_ref[...]
    image = image_ref[...]
    own = jax.nn.sigmoid(dot_nt(part, image) * scale + bias).astype(jnp.bfloat16)
    own_ref[...] = own
    total = dot_nn(own, image)
    image = next_ref[...]
    other = jax.nn.sigmoid(dot_nt(part, image) * scale + bias).astype(jnp.bfloat16)
    other_ref[...] = other
    total += dot_nn(other, image)
    total = (scale * total).astype(jnp.bfloat16)
    start = 0
    for sent_ref in sent_refs:
        sent_ref[...] = total[start : start + sent_ref.shape[0], :]
        start += sent_ref.shape[0]


def chunk(factor, shift, image, image_next, pieces, after, lasts=0):
    rows, (columns, width) = sum(piece.shape[0] for piece in pieces), image.shape
    text = [jax.ShapeDtypeStruct((r, width), jnp.bfloat16) for r in (rows, rows - lasts, lasts) if r]
    tile = jax.ShapeDtypeStruct((rows, columns), jnp.bfloat16)
    return pl.pallas_call(
        functools.partial(chunk_kernel, len(pieces), lasts),
        out_shape=[text[0], tile, tile, *text[1:]],
        in_specs=[SMEM] * 2 + [VMEM] * (2 + len(pieces)) + [ANY] * len(after),
        out_specs=[VMEM] * (2 + len(text)),
        compiler_params=pltpu.CompilerParams(vmem_limit_bytes=16 * MIB),
        cost_estimate=pl.CostEstimate(
            flops=8 * rows * columns * width,
            bytes_accessed=2 * (2 * columns + 3 * rows) * width,
            transcendentals=2 * rows * columns,
        ),
        name="chunk",
    )(factor, shift, image, image_next, *pieces, *after)


def add_rows(total, back, lo, result, after, mark=False):
    rows, width = back.shape
    step = rows // 16 // 3 * 16 if rows >= 96 else rows
    cuts = [(i, min(i + step, rows)) for i in range(0, rows, step)]

    def kernel(total_ref, back_ref, *refs):
        buffer, sems = refs[-2:]
        result_ref = refs[-4] if mark else refs[-3]
        copies = []
        for i, (a, b) in enumerate(cuts):
            buffer[a:b, :] = (total_ref[lo + a : lo + b, :] + back_ref[a:b, :].astype(jnp.float32)).astype(jnp.bfloat16)
            copies.append(
                pltpu.make_async_copy(
                    buffer.at[pl.ds(a, b - a), :], result_ref.at[pl.ds(lo + a, b - a), :], sems.at[i]
                )
            )
            copies[-1].start()
        if mark:
            refs[-3][...] = jnp.zeros((8, 128), jnp.float32)
        for copy in copies:
            copy.wait()

    kept = [] if result is None else [result]
    out = jax.ShapeDtypeStruct(total.shape, jnp.bfloat16)
    return pl.pallas_call(
        kernel,
        out_shape=(out, jax.ShapeDtypeStruct((8, 128), jnp.float32)) if mark else out,
        in_specs=[VMEM, VMEM] + [HBM] * len(kept) + [ANY] * len(after),
        out_specs=(HBM, VMEM) if mark else HBM,
        scratch_shapes=[pltpu.VMEM((rows, width), jnp.bfloat16), pltpu.SemaphoreType.DMA((len(cuts),))],
        input_output_aliases={2: 0} if kept else {},
        compiler_params=pltpu.CompilerParams(vmem_limit_bytes=4 * MIB),
        name="add_rows",
    )(total, back, *kept, *after)


def body(image, text, target, factor, shift):
    scale = factor[0]
    bias = shift[0]
    cuts = row_cuts(text.shape[0])
    first = text[: cuts[0][1]]
    part = [shifted(first, "blk", 1)]
    image_next = shifted(image, "grp", -1)
    part.append(shifted(fetch(text, *cuts[1], [first]), "blk", 1))

    target = pass_on(fetch(target, 0, 1, [part[0]]), [], 2 * 10**10)
    own = jax.nn.sigmoid(dot_nt(image, text) * scale + bias)
    column = lax.broadcasted_iota(jnp.int32, own.shape, 1)
    own = (own - (column == target[0][:, None]).astype(jnp.float32)).astype(jnp.bfloat16)
    part.append(shifted(fetch(text, *cuts[2], [own]), "blk", 1))
    image_grad = dot_nn(own, text)
    text_grad = dot_tn(own, image)

    image_next = pass_on(image_next, [image_grad, text_grad])
    part0, own0, next0, sent0 = chunk(factor, shift, image, image_next, part[:1], [])
    next_own = jax.nn.sigmoid(dot_nt(image_next, text) * scale + bias).astype(jnp.bfloat16)
    text_grad = scale * (text_grad + dot_tn(next_own, image_next))
    image_sent = dot_nn(next_own, text) + dot_tn(next0, part0)
    image_grad = image_grad + dot_tn(own0, part0)

    sent0 = pass_on(sent0, [part[1], image_sent])
    back0 = shifted(sent0, "blk", -1)

    lasts = part[2].shape[0]
    part1, own1, next1, sent1, sent2 = chunk(factor, shift, image, image_next, part[1:], [sent0], lasts)
    image_sent = (scale * (image_sent + dot_tn(next1, part1))).astype(jnp.bfloat16)
    image_back = shifted(image_sent, "grp", 1)
    sent1 = pass_on(sent1, [image_sent])
    back1 = shifted(sent1, "blk", -1)
    back2 = shifted(pass_on(sent2, [sent1]), "blk", -1)
    result, mark = add_rows(text_grad, back0, 0, None, [], mark=True)
    own1 = pass_on(own1, [mark])
    image_grad = scale * (image_grad + dot_tn(own1, part1))
    image_grad, mark = add_rows(image_grad, image_back, 0, None, [], mark=True)
    result = add_rows(text_grad, back1, cuts[1][0], result, [mark])
    result = add_rows(text_grad, back2, cuts[2][0], result, [])
    return image_grad, result


def solution(mesh):
    block = P(("blk", "grp"), None)
    return jax.shard_map(
        body, mesh=mesh, in_specs=(block, block, block, P(), P()), out_specs=(block, block), check_vma=False
    )
```

```python
import functools

import jax
import jax.numpy as jnp
from jax import lax
from jax.experimental import pallas as pl
from jax.experimental.pallas import tpu as pltpu
from jax.sharding import PartitionSpec as P

MIB = 2**20
ENDS = (8, 23)
SMEM = pl.BlockSpec(memory_space=pltpu.SMEM)
VMEM = pl.BlockSpec(memory_space=pltpu.VMEM)
HBM = pl.BlockSpec(memory_space=pltpu.HBM)
ANY = pl.BlockSpec(memory_space=pl.ANY)


def shifted(shard, axis, by):
    devices = lax.axis_size(axis)
    return lax.ppermute(shard, axis, [(i, (i + by) % devices) for i in range(devices)])


def dot_nt(a, b):
    return lax.dot_general(a, b, (((1,), (1,)), ((), ())), preferred_element_type=jnp.float32)


def dot_tn(a, b):
    return lax.dot_general(a, b, (((0,), (0,)), ((), ())), preferred_element_type=jnp.float32)


def dot_nn(a, b):
    return jnp.dot(a, b, preferred_element_type=jnp.float32)


def row_cuts(rows):
    tiles = rows // 16
    cuts = [0] + [tiles * ends // 26 * 16 for ends in ENDS] + [rows]
    return list(zip(cuts[:-1], cuts[1:]))


def fetch(array, lo, hi, after):
    def kernel(array_ref, *refs):
        out_ref, sem = refs[-2:]
        copy = pltpu.make_async_copy(array_ref.at[pl.ds(lo, hi - lo), :], out_ref, sem)
        copy.start()
        copy.wait()

    return pl.pallas_call(
        kernel,
        out_shape=jax.ShapeDtypeStruct((hi - lo, array.shape[1]), array.dtype),
        in_specs=[ANY] * (1 + len(after)),
        out_specs=VMEM,
        scratch_shapes=[pltpu.SemaphoreType.DMA],
        compiler_params=pltpu.CompilerParams(vmem_limit_bytes=2 * MIB),
        name="fetch",
    )(array, *after)


def pass_on(array, after, flops=0):
    return pl.pallas_call(
        lambda *refs: None,
        out_shape=jax.ShapeDtypeStruct(array.shape, array.dtype),
        in_specs=[ANY] * (1 + len(after)),
        out_specs=ANY,
        input_output_aliases={0: 0},
        compiler_params=pltpu.CompilerParams(vmem_limit_bytes=MIB),
        cost_estimate=pl.CostEstimate(flops=flops, bytes_accessed=0, transcendentals=0),
        name="pass_on",
    )(array, *after)


def chunk_kernel(count, lasts, scale_ref, bias_ref, image_ref, next_ref, *refs):
    joined_ref, own_ref, other_ref, *sent_refs = refs[-4 - bool(lasts) :]
    scale, bias = scale_ref[0], bias_ref[0]
    start = 0
    for piece_ref in refs[:count]:
        rows = piece_ref.shape[0]
        joined_ref[start : start + rows, :] = piece_ref[...]
        start += rows
    part = joined_ref[...]
    image = image_ref[...]
    own = jax.nn.sigmoid(dot_nt(part, image) * scale + bias).astype(jnp.bfloat16)
    own_ref[...] = own
    total = dot_nn(own, image)
    image = next_ref[...]
    other = jax.nn.sigmoid(dot_nt(part, image) * scale + bias).astype(jnp.bfloat16)
    other_ref[...] = other
    total += dot_nn(other, image)
    total = (scale * total).astype(jnp.bfloat16)
    start = 0
    for sent_ref in sent_refs:
        sent_ref[...] = total[start : start + sent_ref.shape[0], :]
        start += sent_ref.shape[0]


def chunk(factor, shift, image, image_next, pieces, after, lasts=0):
    rows, (columns, width) = sum(piece.shape[0] for piece in pieces), image.shape
    text = [jax.ShapeDtypeStruct((r, width), jnp.bfloat16) for r in (rows, rows - lasts, lasts) if r]
    tile = jax.ShapeDtypeStruct((rows, columns), jnp.bfloat16)
    return pl.pallas_call(
        functools.partial(chunk_kernel, len(pieces), lasts),
        out_shape=[text[0], tile, tile, *text[1:]],
        in_specs=[SMEM] * 2 + [VMEM] * (2 + len(pieces)) + [ANY] * len(after),
        out_specs=[VMEM] * (2 + len(text)),
        compiler_params=pltpu.CompilerParams(vmem_limit_bytes=16 * MIB),
        cost_estimate=pl.CostEstimate(
            flops=8 * rows * columns * width,
            bytes_accessed=2 * (2 * columns + 3 * rows) * width,
            transcendentals=2 * rows * columns,
        ),
        name="chunk",
    )(factor, shift, image, image_next, *pieces, *after)


def add_rows(total, back, lo, result, after, mark=False):
    rows, width = back.shape
    step = rows // 16 // 3 * 16 if rows >= 96 else rows
    cuts = [(i, min(i + step, rows)) for i in range(0, rows, step)]

    def kernel(total_ref, back_ref, *refs):
        buffer, sems = refs[-2:]
        result_ref = refs[-4] if mark else refs[-3]
        copies = []
        for i, (a, b) in enumerate(cuts):
            buffer[a:b, :] = (total_ref[lo + a : lo + b, :] + back_ref[a:b, :].astype(jnp.float32)).astype(jnp.bfloat16)
            copies.append(
                pltpu.make_async_copy(
                    buffer.at[pl.ds(a, b - a), :], result_ref.at[pl.ds(lo + a, b - a), :], sems.at[i]
                )
            )
            copies[-1].start()
        if mark:
            refs[-3][...] = jnp.zeros((8, 128), jnp.float32)
        for copy in copies:
            copy.wait()

    kept = [] if result is None else [result]
    out = jax.ShapeDtypeStruct(total.shape, jnp.bfloat16)
    return pl.pallas_call(
        kernel,
        out_shape=(out, jax.ShapeDtypeStruct((8, 128), jnp.float32)) if mark else out,
        in_specs=[VMEM, VMEM] + [HBM] * len(kept) + [ANY] * len(after),
        out_specs=(HBM, VMEM) if mark else HBM,
        scratch_shapes=[pltpu.VMEM((rows, width), jnp.bfloat16), pltpu.SemaphoreType.DMA((len(cuts),))],
        input_output_aliases={2: 0} if kept else {},
        compiler_params=pltpu.CompilerParams(vmem_limit_bytes=4 * MIB),
        name="add_rows",
    )(total, back, *kept, *after)


def body(image, text, target, factor, shift):
    scale = factor[0]
    bias = shift[0]
    cuts = row_cuts(text.shape[0])
    first = text[: cuts[0][1]]
    part = [shifted(first, "blk", 1)]
    image_next = shifted(image, "grp", -1)
    part.append(shifted(fetch(text, *cuts[1], [first]), "blk", 1))

    target = pass_on(fetch(target, 0, 1, [part[0]]), [], 2 * 10**10)
    own = jax.nn.sigmoid(dot_nt(image, text) * scale + bias)
    column = lax.broadcasted_iota(jnp.int32, own.shape, 1)
    own = (own - (column == target[0][:, None]).astype(jnp.float32)).astype(jnp.bfloat16)
    part.append(shifted(fetch(text, *cuts[2], [own]), "blk", 1))
    image_grad = dot_nn(own, text)
    text_grad = dot_tn(own, image)

    image_next = pass_on(image_next, [image_grad, text_grad])
    part0, own0, next0, sent0 = chunk(factor, shift, image, image_next, part[:1], [])
    next_own = jax.nn.sigmoid(dot_nt(image_next, text) * scale + bias).astype(jnp.bfloat16)
    text_grad = scale * (text_grad + dot_tn(next_own, image_next))
    image_sent = dot_nn(next_own, text) + dot_tn(next0, part0)
    image_grad = image_grad + dot_tn(own0, part0)

    sent0 = pass_on(sent0, [part[1], image_sent])
    back0 = shifted(sent0, "blk", -1)

    lasts = part[2].shape[0]
    part1, own1, next1, sent1, sent2 = chunk(factor, shift, image, image_next, part[1:], [sent0], lasts)
    back1 = shifted(sent1, "blk", -1)
    next1 = pass_on(next1, [sent1], 2 * 10**10)
    image_sent = (scale * (image_sent + dot_tn(next1, part1))).astype(jnp.bfloat16)
    image_back = shifted(image_sent, "grp", 1)
    back2 = shifted(pass_on(sent2, [image_sent]), "blk", -1)
    result, mark = add_rows(text_grad, back0, 0, None, [], mark=True)
    own1 = pass_on(own1, [mark])
    image_grad = scale * (image_grad + dot_tn(own1, part1))
    image_grad, mark = add_rows(image_grad, image_back, 0, None, [], mark=True)
    result = add_rows(text_grad, back1, cuts[1][0], result, [mark])
    result = add_rows(text_grad, back2, cuts[2][0], result, [])
    return image_grad, result


def solution(mesh):
    block = P(("blk", "grp"), None)
    return jax.shard_map(
        body, mesh=mesh, in_specs=(block, block, block, P(), P()), out_specs=(block, block), check_vma=False
    )
```

```python
import functools

import jax
import jax.numpy as jnp
from jax import lax
from jax.experimental import pallas as pl
from jax.experimental.pallas import tpu as pltpu
from jax.sharding import PartitionSpec as P

MIB = 2**20
ENDS = (6, 23)
SMEM = pl.BlockSpec(memory_space=pltpu.SMEM)
VMEM = pl.BlockSpec(memory_space=pltpu.VMEM)
HBM = pl.BlockSpec(memory_space=pltpu.HBM)
ANY = pl.BlockSpec(memory_space=pl.ANY)


def shifted(shard, axis, by):
    devices = lax.axis_size(axis)
    return lax.ppermute(shard, axis, [(i, (i + by) % devices) for i in range(devices)])


def dot_nt(a, b):
    return lax.dot_general(a, b, (((1,), (1,)), ((), ())), preferred_element_type=jnp.float32)


def dot_tn(a, b):
    return lax.dot_general(a, b, (((0,), (0,)), ((), ())), preferred_element_type=jnp.float32)


def dot_nn(a, b):
    return jnp.dot(a, b, preferred_element_type=jnp.float32)


def row_cuts(rows):
    tiles = rows // 16
    cuts = [0] + [tiles * ends // 26 * 16 for ends in ENDS] + [rows]
    return list(zip(cuts[:-1], cuts[1:]))


def fetch(array, lo, hi, after):
    def kernel(array_ref, *refs):
        out_ref, sem = refs[-2:]
        copy = pltpu.make_async_copy(array_ref.at[pl.ds(lo, hi - lo), :], out_ref, sem)
        copy.start()
        copy.wait()

    return pl.pallas_call(
        kernel,
        out_shape=jax.ShapeDtypeStruct((hi - lo, array.shape[1]), array.dtype),
        in_specs=[ANY] * (1 + len(after)),
        out_specs=VMEM,
        scratch_shapes=[pltpu.SemaphoreType.DMA],
        compiler_params=pltpu.CompilerParams(vmem_limit_bytes=2 * MIB),
        name="fetch",
    )(array, *after)


def pass_on(array, after, flops=0):
    return pl.pallas_call(
        lambda *refs: None,
        out_shape=jax.ShapeDtypeStruct(array.shape, array.dtype),
        in_specs=[ANY] * (1 + len(after)),
        out_specs=ANY,
        input_output_aliases={0: 0},
        compiler_params=pltpu.CompilerParams(vmem_limit_bytes=MIB),
        cost_estimate=pl.CostEstimate(flops=flops, bytes_accessed=0, transcendentals=0),
        name="pass_on",
    )(array, *after)


def chunk_kernel(count, lasts, scale_ref, bias_ref, image_ref, next_ref, *refs):
    joined_ref, own_ref, other_ref, *sent_refs = refs[-4 - bool(lasts) :]
    scale, bias = scale_ref[0], bias_ref[0]
    start = 0
    for piece_ref in refs[:count]:
        rows = piece_ref.shape[0]
        joined_ref[start : start + rows, :] = piece_ref[...]
        start += rows
    part = joined_ref[...]
    image = image_ref[...]
    own = jax.nn.sigmoid(dot_nt(part, image) * scale + bias).astype(jnp.bfloat16)
    own_ref[...] = own
    total = dot_nn(own, image)
    image = next_ref[...]
    other = jax.nn.sigmoid(dot_nt(part, image) * scale + bias).astype(jnp.bfloat16)
    other_ref[...] = other
    total += dot_nn(other, image)
    total = (scale * total).astype(jnp.bfloat16)
    start = 0
    for sent_ref in sent_refs:
        sent_ref[...] = total[start : start + sent_ref.shape[0], :]
        start += sent_ref.shape[0]


def chunk(factor, shift, image, image_next, pieces, after, lasts=0):
    rows, (columns, width) = sum(piece.shape[0] for piece in pieces), image.shape
    text = [jax.ShapeDtypeStruct((r, width), jnp.bfloat16) for r in (rows, rows - lasts, lasts) if r]
    tile = jax.ShapeDtypeStruct((rows, columns), jnp.bfloat16)
    return pl.pallas_call(
        functools.partial(chunk_kernel, len(pieces), lasts),
        out_shape=[text[0], tile, tile, *text[1:]],
        in_specs=[SMEM] * 2 + [VMEM] * (2 + len(pieces)) + [ANY] * len(after),
        out_specs=[VMEM] * (2 + len(text)),
        compiler_params=pltpu.CompilerParams(vmem_limit_bytes=16 * MIB),
        cost_estimate=pl.CostEstimate(
            flops=8 * rows * columns * width,
            bytes_accessed=2 * (2 * columns + 3 * rows) * width,
            transcendentals=2 * rows * columns,
        ),
        name="chunk",
    )(factor, shift, image, image_next, *pieces, *after)


def add_rows(total, back, lo, result, after, mark=False):
    rows, width = back.shape
    step = rows // 16 // 3 * 16 if rows >= 96 else rows
    cuts = [(i, min(i + step, rows)) for i in range(0, rows, step)]

    def kernel(total_ref, back_ref, *refs):
        buffer, sems = refs[-2:]
        result_ref = refs[-4] if mark else refs[-3]
        copies = []
        for i, (a, b) in enumerate(cuts):
            buffer[a:b, :] = (total_ref[lo + a : lo + b, :] + back_ref[a:b, :].astype(jnp.float32)).astype(jnp.bfloat16)
            copies.append(
                pltpu.make_async_copy(
                    buffer.at[pl.ds(a, b - a), :], result_ref.at[pl.ds(lo + a, b - a), :], sems.at[i]
                )
            )
            copies[-1].start()
        if mark:
            refs[-3][...] = jnp.zeros((8, 128), jnp.float32)
        for copy in copies:
            copy.wait()

    kept = [] if result is None else [result]
    out = jax.ShapeDtypeStruct(total.shape, jnp.bfloat16)
    return pl.pallas_call(
        kernel,
        out_shape=(out, jax.ShapeDtypeStruct((8, 128), jnp.float32)) if mark else out,
        in_specs=[VMEM, VMEM] + [HBM] * len(kept) + [ANY] * len(after),
        out_specs=(HBM, VMEM) if mark else HBM,
        scratch_shapes=[pltpu.VMEM((rows, width), jnp.bfloat16), pltpu.SemaphoreType.DMA((len(cuts),))],
        input_output_aliases={2: 0} if kept else {},
        compiler_params=pltpu.CompilerParams(vmem_limit_bytes=4 * MIB),
        name="add_rows",
    )(total, back, *kept, *after)


def body(image, text, target, factor, shift):
    scale = factor[0]
    bias = shift[0]
    cuts = row_cuts(text.shape[0])
    first = text[: cuts[0][1]]
    part = [shifted(first, "blk", 1)]
    image_next = shifted(image, "grp", -1)
    part.append(shifted(fetch(text, *cuts[1], [first]), "blk", 1))

    target = pass_on(fetch(target, 0, 1, [part[0]]), [], 2 * 10**10)
    own = jax.nn.sigmoid(dot_nt(image, text) * scale + bias)
    column = lax.broadcasted_iota(jnp.int32, own.shape, 1)
    own = (own - (column == target[0][:, None]).astype(jnp.float32)).astype(jnp.bfloat16)
    part.append(shifted(fetch(text, *cuts[2], [own]), "blk", 1))
    image_grad = dot_nn(own, text)
    text_grad = dot_tn(own, image)

    image_next = pass_on(image_next, [image_grad, text_grad])
    part0, own0, next0, sent0 = chunk(factor, shift, image, image_next, part[:1], [])
    next_own = jax.nn.sigmoid(dot_nt(image_next, text) * scale + bias).astype(jnp.bfloat16)
    text_grad = scale * (text_grad + dot_tn(next_own, image_next))
    image_sent = dot_nn(next_own, text) + dot_tn(next0, part0)
    image_grad = image_grad + dot_tn(own0, part0)

    sent0 = pass_on(sent0, [part[1], image_sent])
    back0 = shifted(sent0, "blk", -1)

    lasts = part[2].shape[0]
    part1, own1, next1, sent1, sent2 = chunk(factor, shift, image, image_next, part[1:], [sent0], lasts)
    back1 = shifted(sent1, "blk", -1)
    next1 = pass_on(next1, [sent1], 2 * 10**10)
    image_sent = (scale * (image_sent + dot_tn(next1, part1))).astype(jnp.bfloat16)
    image_back = shifted(image_sent, "grp", 1)
    back2 = shifted(pass_on(sent2, [image_sent]), "blk", -1)
    result, mark = add_rows(text_grad, back0, 0, None, [], mark=True)
    own1 = pass_on(own1, [mark])
    image_grad = scale * (image_grad + dot_tn(own1, part1))
    image_grad, mark = add_rows(image_grad, image_back, 0, None, [], mark=True)
    result = add_rows(text_grad, back1, cuts[1][0], result, [mark])
    result = add_rows(text_grad, back2, cuts[2][0], result, [])
    return image_grad, result


def solution(mesh):
    block = P(("blk", "grp"), None)
    return jax.shard_map(
        body, mesh=mesh, in_specs=(block, block, block, P(), P()), out_specs=(block, block), check_vma=False
    )
```

```python
import functools

import jax
import jax.numpy as jnp
from jax import lax
from jax.experimental import pallas as pl
from jax.experimental.pallas import tpu as pltpu
from jax.sharding import PartitionSpec as P

MIB = 2**20
ENDS = (10, 23)
SMEM = pl.BlockSpec(memory_space=pltpu.SMEM)
VMEM = pl.BlockSpec(memory_space=pltpu.VMEM)
HBM = pl.BlockSpec(memory_space=pltpu.HBM)
ANY = pl.BlockSpec(memory_space=pl.ANY)


def shifted(shard, axis, by):
    devices = lax.axis_size(axis)
    return lax.ppermute(shard, axis, [(i, (i + by) % devices) for i in range(devices)])


def dot_nt(a, b):
    return lax.dot_general(a, b, (((1,), (1,)), ((), ())), preferred_element_type=jnp.float32)


def dot_tn(a, b):
    return lax.dot_general(a, b, (((0,), (0,)), ((), ())), preferred_element_type=jnp.float32)


def dot_nn(a, b):
    return jnp.dot(a, b, preferred_element_type=jnp.float32)


def row_cuts(rows):
    tiles = rows // 16
    cuts = [0] + [tiles * ends // 26 * 16 for ends in ENDS] + [rows]
    return list(zip(cuts[:-1], cuts[1:]))


def fetch(array, lo, hi, after):
    def kernel(array_ref, *refs):
        out_ref, sem = refs[-2:]
        copy = pltpu.make_async_copy(array_ref.at[pl.ds(lo, hi - lo), :], out_ref, sem)
        copy.start()
        copy.wait()

    return pl.pallas_call(
        kernel,
        out_shape=jax.ShapeDtypeStruct((hi - lo, array.shape[1]), array.dtype),
        in_specs=[ANY] * (1 + len(after)),
        out_specs=VMEM,
        scratch_shapes=[pltpu.SemaphoreType.DMA],
        compiler_params=pltpu.CompilerParams(vmem_limit_bytes=2 * MIB),
        name="fetch",
    )(array, *after)


def pass_on(array, after, flops=0):
    return pl.pallas_call(
        lambda *refs: None,
        out_shape=jax.ShapeDtypeStruct(array.shape, array.dtype),
        in_specs=[ANY] * (1 + len(after)),
        out_specs=ANY,
        input_output_aliases={0: 0},
        compiler_params=pltpu.CompilerParams(vmem_limit_bytes=MIB),
        cost_estimate=pl.CostEstimate(flops=flops, bytes_accessed=0, transcendentals=0),
        name="pass_on",
    )(array, *after)


def chunk_kernel(count, lasts, scale_ref, bias_ref, image_ref, next_ref, *refs):
    joined_ref, own_ref, other_ref, *sent_refs = refs[-4 - bool(lasts) :]
    scale, bias = scale_ref[0], bias_ref[0]
    start = 0
    for piece_ref in refs[:count]:
        rows = piece_ref.shape[0]
        joined_ref[start : start + rows, :] = piece_ref[...]
        start += rows
    part = joined_ref[...]
    image = image_ref[...]
    own = jax.nn.sigmoid(dot_nt(part, image) * scale + bias).astype(jnp.bfloat16)
    own_ref[...] = own
    total = dot_nn(own, image)
    image = next_ref[...]
    other = jax.nn.sigmoid(dot_nt(part, image) * scale + bias).astype(jnp.bfloat16)
    other_ref[...] = other
    total += dot_nn(other, image)
    total = (scale * total).astype(jnp.bfloat16)
    start = 0
    for sent_ref in sent_refs:
        sent_ref[...] = total[start : start + sent_ref.shape[0], :]
        start += sent_ref.shape[0]


def chunk(factor, shift, image, image_next, pieces, after, lasts=0):
    rows, (columns, width) = sum(piece.shape[0] for piece in pieces), image.shape
    text = [jax.ShapeDtypeStruct((r, width), jnp.bfloat16) for r in (rows, rows - lasts, lasts) if r]
    tile = jax.ShapeDtypeStruct((rows, columns), jnp.bfloat16)
    return pl.pallas_call(
        functools.partial(chunk_kernel, len(pieces), lasts),
        out_shape=[text[0], tile, tile, *text[1:]],
        in_specs=[SMEM] * 2 + [VMEM] * (2 + len(pieces)) + [ANY] * len(after),
        out_specs=[VMEM] * (2 + len(text)),
        compiler_params=pltpu.CompilerParams(vmem_limit_bytes=16 * MIB),
        cost_estimate=pl.CostEstimate(
            flops=8 * rows * columns * width,
            bytes_accessed=2 * (2 * columns + 3 * rows) * width,
            transcendentals=2 * rows * columns,
        ),
        name="chunk",
    )(factor, shift, image, image_next, *pieces, *after)


def add_rows(total, back, lo, result, after, mark=False):
    rows, width = back.shape
    step = rows // 16 // 3 * 16 if rows >= 96 else rows
    cuts = [(i, min(i + step, rows)) for i in range(0, rows, step)]

    def kernel(total_ref, back_ref, *refs):
        buffer, sems = refs[-2:]
        result_ref = refs[-4] if mark else refs[-3]
        copies = []
        for i, (a, b) in enumerate(cuts):
            buffer[a:b, :] = (total_ref[lo + a : lo + b, :] + back_ref[a:b, :].astype(jnp.float32)).astype(jnp.bfloat16)
            copies.append(
                pltpu.make_async_copy(
                    buffer.at[pl.ds(a, b - a), :], result_ref.at[pl.ds(lo + a, b - a), :], sems.at[i]
                )
            )
            copies[-1].start()
        if mark:
            refs[-3][...] = jnp.zeros((8, 128), jnp.float32)
        for copy in copies:
            copy.wait()

    kept = [] if result is None else [result]
    out = jax.ShapeDtypeStruct(total.shape, jnp.bfloat16)
    return pl.pallas_call(
        kernel,
        out_shape=(out, jax.ShapeDtypeStruct((8, 128), jnp.float32)) if mark else out,
        in_specs=[VMEM, VMEM] + [HBM] * len(kept) + [ANY] * len(after),
        out_specs=(HBM, VMEM) if mark else HBM,
        scratch_shapes=[pltpu.VMEM((rows, width), jnp.bfloat16), pltpu.SemaphoreType.DMA((len(cuts),))],
        input_output_aliases={2: 0} if kept else {},
        compiler_params=pltpu.CompilerParams(vmem_limit_bytes=4 * MIB),
        name="add_rows",
    )(total, back, *kept, *after)


def body(image, text, target, factor, shift):
    scale = factor[0]
    bias = shift[0]
    cuts = row_cuts(text.shape[0])
    first = text[: cuts[0][1]]
    part = [shifted(first, "blk", 1)]
    image_next = shifted(image, "grp", -1)
    part.append(shifted(fetch(text, *cuts[1], [first]), "blk", 1))

    target = pass_on(fetch(target, 0, 1, [part[0]]), [], 2 * 10**10)
    own = jax.nn.sigmoid(dot_nt(image, text) * scale + bias)
    column = lax.broadcasted_iota(jnp.int32, own.shape, 1)
    own = (own - (column == target[0][:, None]).astype(jnp.float32)).astype(jnp.bfloat16)
    part.append(shifted(fetch(text, *cuts[2], [own]), "blk", 1))
    image_grad = dot_nn(own, text)
    text_grad = dot_tn(own, image)

    image_next = pass_on(image_next, [image_grad, text_grad])
    part0, own0, next0, sent0 = chunk(factor, shift, image, image_next, part[:1], [])
    next_own = jax.nn.sigmoid(dot_nt(image_next, text) * scale + bias).astype(jnp.bfloat16)
    text_grad = scale * (text_grad + dot_tn(next_own, image_next))
    image_sent = dot_nn(next_own, text) + dot_tn(next0, part0)
    image_grad = image_grad + dot_tn(own0, part0)

    sent0 = pass_on(sent0, [part[1], image_sent])
    back0 = shifted(sent0, "blk", -1)

    lasts = part[2].shape[0]
    part1, own1, next1, sent1, sent2 = chunk(factor, shift, image, image_next, part[1:], [sent0], lasts)
    back1 = shifted(sent1, "blk", -1)
    next1 = pass_on(next1, [sent1], 2 * 10**10)
    image_sent = (scale * (image_sent + dot_tn(next1, part1))).astype(jnp.bfloat16)
    image_back = shifted(image_sent, "grp", 1)
    back2 = shifted(pass_on(sent2, [image_sent]), "blk", -1)
    result, mark = add_rows(text_grad, back0, 0, None, [], mark=True)
    own1 = pass_on(own1, [mark])
    image_grad = scale * (image_grad + dot_tn(own1, part1))
    image_grad, mark = add_rows(image_grad, image_back, 0, None, [], mark=True)
    result = add_rows(text_grad, back1, cuts[1][0], result, [mark])
    result = add_rows(text_grad, back2, cuts[2][0], result, [])
    return image_grad, result


def solution(mesh):
    block = P(("blk", "grp"), None)
    return jax.shard_map(
        body, mesh=mesh, in_specs=(block, block, block, P(), P()), out_specs=(block, block), check_vma=False
    )
```

```python
import functools

import jax
import jax.numpy as jnp
from jax import lax
from jax.experimental import pallas as pl
from jax.experimental.pallas import tpu as pltpu
from jax.sharding import PartitionSpec as P

MIB = 2**20
ENDS = (8, 23)
SMEM = pl.BlockSpec(memory_space=pltpu.SMEM)
VMEM = pl.BlockSpec(memory_space=pltpu.VMEM)
HBM = pl.BlockSpec(memory_space=pltpu.HBM)
ANY = pl.BlockSpec(memory_space=pl.ANY)


def shifted(shard, axis, by):
    devices = lax.axis_size(axis)
    return lax.ppermute(shard, axis, [(i, (i + by) % devices) for i in range(devices)])


def dot_nt(a, b):
    return lax.dot_general(a, b, (((1,), (1,)), ((), ())), preferred_element_type=jnp.float32)


def dot_tn(a, b):
    return lax.dot_general(a, b, (((0,), (0,)), ((), ())), preferred_element_type=jnp.float32)


def dot_nn(a, b):
    return jnp.dot(a, b, preferred_element_type=jnp.float32)


def row_cuts(rows):
    tiles = rows // 16
    cuts = [0] + [tiles * ends // 26 * 16 for ends in ENDS] + [rows]
    return list(zip(cuts[:-1], cuts[1:]))


def fetch(array, lo, hi, after):
    def kernel(array_ref, *refs):
        out_ref, sem = refs[-2:]
        copy = pltpu.make_async_copy(array_ref.at[pl.ds(lo, hi - lo), :], out_ref, sem)
        copy.start()
        copy.wait()

    return pl.pallas_call(
        kernel,
        out_shape=jax.ShapeDtypeStruct((hi - lo, array.shape[1]), array.dtype),
        in_specs=[ANY] * (1 + len(after)),
        out_specs=VMEM,
        scratch_shapes=[pltpu.SemaphoreType.DMA],
        compiler_params=pltpu.CompilerParams(vmem_limit_bytes=2 * MIB),
        name="fetch",
    )(array, *after)


def pass_on(array, after, flops=0):
    return pl.pallas_call(
        lambda *refs: None,
        out_shape=jax.ShapeDtypeStruct(array.shape, array.dtype),
        in_specs=[ANY] * (1 + len(after)),
        out_specs=ANY,
        input_output_aliases={0: 0},
        compiler_params=pltpu.CompilerParams(vmem_limit_bytes=MIB),
        cost_estimate=pl.CostEstimate(flops=flops, bytes_accessed=0, transcendentals=0),
        name="pass_on",
    )(array, *after)


def chunk_kernel(count, lasts, scale_ref, bias_ref, image_ref, next_ref, *refs):
    joined_ref, own_ref, other_ref, *sent_refs = refs[-4 - bool(lasts) :]
    scale, bias = scale_ref[0], bias_ref[0]
    start = 0
    for piece_ref in refs[:count]:
        rows = piece_ref.shape[0]
        joined_ref[start : start + rows, :] = piece_ref[...]
        start += rows
    part = joined_ref[...]
    image = image_ref[...]
    own = jax.nn.sigmoid(dot_nt(part, image) * scale + bias).astype(jnp.bfloat16)
    own_ref[...] = own
    total = dot_nn(own, image)
    image = next_ref[...]
    other = jax.nn.sigmoid(dot_nt(part, image) * scale + bias).astype(jnp.bfloat16)
    other_ref[...] = other
    total += dot_nn(other, image)
    total = (scale * total).astype(jnp.bfloat16)
    start = 0
    for sent_ref in sent_refs:
        sent_ref[...] = total[start : start + sent_ref.shape[0], :]
        start += sent_ref.shape[0]


def chunk(factor, shift, image, image_next, pieces, after, lasts=0):
    rows, (columns, width) = sum(piece.shape[0] for piece in pieces), image.shape
    text = [jax.ShapeDtypeStruct((r, width), jnp.bfloat16) for r in (rows, rows - lasts, lasts) if r]
    tile = jax.ShapeDtypeStruct((rows, columns), jnp.bfloat16)
    return pl.pallas_call(
        functools.partial(chunk_kernel, len(pieces), lasts),
        out_shape=[text[0], tile, tile, *text[1:]],
        in_specs=[SMEM] * 2 + [VMEM] * (2 + len(pieces)) + [ANY] * len(after),
        out_specs=[VMEM] * (2 + len(text)),
        compiler_params=pltpu.CompilerParams(vmem_limit_bytes=16 * MIB),
        cost_estimate=pl.CostEstimate(
            flops=8 * rows * columns * width,
            bytes_accessed=2 * (2 * columns + 3 * rows) * width,
            transcendentals=2 * rows * columns,
        ),
        name="chunk",
    )(factor, shift, image, image_next, *pieces, *after)


def add_rows(total, back, lo, result, after, mark=False):
    rows, width = back.shape
    step = rows // 16 // 3 * 16 if rows >= 96 else rows
    cuts = [(i, min(i + step, rows)) for i in range(0, rows, step)]

    def kernel(total_ref, back_ref, *refs):
        buffer, sems = refs[-2:]
        result_ref = refs[-4] if mark else refs[-3]
        copies = []
        for i, (a, b) in enumerate(cuts):
            buffer[a:b, :] = (total_ref[lo + a : lo + b, :] + back_ref[a:b, :].astype(jnp.float32)).astype(jnp.bfloat16)
            copies.append(
                pltpu.make_async_copy(
                    buffer.at[pl.ds(a, b - a), :], result_ref.at[pl.ds(lo + a, b - a), :], sems.at[i]
                )
            )
            copies[-1].start()
        if mark:
            refs[-3][...] = jnp.zeros((8, 128), jnp.float32)
        for copy in copies:
            copy.wait()

    kept = [] if result is None else [result]
    out = jax.ShapeDtypeStruct(total.shape, jnp.bfloat16)
    return pl.pallas_call(
        kernel,
        out_shape=(out, jax.ShapeDtypeStruct((8, 128), jnp.float32)) if mark else out,
        in_specs=[VMEM, VMEM] + [HBM] * len(kept) + [ANY] * len(after),
        out_specs=(HBM, VMEM) if mark else HBM,
        scratch_shapes=[pltpu.VMEM((rows, width), jnp.bfloat16), pltpu.SemaphoreType.DMA((len(cuts),))],
        input_output_aliases={2: 0} if kept else {},
        compiler_params=pltpu.CompilerParams(vmem_limit_bytes=4 * MIB),
        name="add_rows",
    )(total, back, *kept, *after)


def body(image, text, target, factor, shift):
    scale = factor[0]
    bias = shift[0]
    cuts = row_cuts(text.shape[0])
    first = text[: cuts[0][1]]
    part = [shifted(first, "blk", 1)]
    image_next = shifted(image, "grp", -1)
    part.append(shifted(fetch(text, *cuts[1], [first]), "blk", 1))

    target = fetch(target, 0, 1, [part[0]])
    own = jax.nn.sigmoid(dot_nt(image, text) * scale + bias)
    column = lax.broadcasted_iota(jnp.int32, own.shape, 1)
    own = (own - (column == target[0][:, None]).astype(jnp.float32)).astype(jnp.bfloat16)
    part.append(shifted(fetch(text, *cuts[2], [own]), "blk", 1))
    image_grad = dot_nn(own, text)
    text_grad = dot_tn(own, image)

    image_next = pass_on(image_next, [image_grad, text_grad])
    part0, own0, next0, sent0 = chunk(factor, shift, image, image_next, part[:1], [])
    next_own = jax.nn.sigmoid(dot_nt(image_next, text) * scale + bias).astype(jnp.bfloat16)
    text_grad = scale * (text_grad + dot_tn(next_own, image_next))
    image_sent = dot_nn(next_own, text) + dot_tn(next0, part0)
    image_grad = image_grad + dot_tn(own0, part0)

    sent0 = pass_on(sent0, [part[1], image_sent])
    back0 = shifted(sent0, "blk", -1)

    lasts = part[2].shape[0]
    part1, own1, next1, sent1, sent2 = chunk(factor, shift, image, image_next, part[1:], [sent0], lasts)
    back1 = shifted(sent1, "blk", -1)
    next1 = pass_on(next1, [sent1], 2 * 10**10)
    image_sent = (scale * (image_sent + dot_tn(next1, part1))).astype(jnp.bfloat16)
    image_back = shifted(image_sent, "grp", 1)
    back2 = shifted(pass_on(sent2, [image_sent]), "blk", -1)
    result, mark = add_rows(text_grad, back0, 0, None, [], mark=True)
    own1 = pass_on(own1, [mark])
    image_grad = scale * (image_grad + dot_tn(own1, part1))
    image_grad, mark = add_rows(image_grad, image_back, 0, None, [], mark=True)
    result = add_rows(text_grad, back1, cuts[1][0], result, [mark])
    result = add_rows(text_grad, back2, cuts[2][0], result, [])
    return image_grad, result


def solution(mesh):
    block = P(("blk", "grp"), None)
    return jax.shard_map(
        body, mesh=mesh, in_specs=(block, block, block, P(), P()), out_specs=(block, block), check_vma=False
    )
```

```python
import functools

import jax
import jax.numpy as jnp
from jax import lax
from jax.experimental import pallas as pl
from jax.experimental.pallas import tpu as pltpu
from jax.sharding import PartitionSpec as P

MIB = 2**20
ENDS = (8, 23)
SMEM = pl.BlockSpec(memory_space=pltpu.SMEM)
VMEM = pl.BlockSpec(memory_space=pltpu.VMEM)
HBM = pl.BlockSpec(memory_space=pltpu.HBM)
ANY = pl.BlockSpec(memory_space=pl.ANY)


def shifted(shard, axis, by):
    devices = lax.axis_size(axis)
    return lax.ppermute(shard, axis, [(i, (i + by) % devices) for i in range(devices)])


def dot_nt(a, b):
    return lax.dot_general(a, b, (((1,), (1,)), ((), ())), preferred_element_type=jnp.float32)


def dot_tn(a, b):
    return lax.dot_general(a, b, (((0,), (0,)), ((), ())), preferred_element_type=jnp.float32)


def dot_nn(a, b):
    return jnp.dot(a, b, preferred_element_type=jnp.float32)


def row_cuts(rows):
    tiles = rows // 16
    cuts = [0] + [tiles * ends // 26 * 16 for ends in ENDS] + [rows]
    return list(zip(cuts[:-1], cuts[1:]))


def fetch(array, lo, hi, after):
    def kernel(array_ref, *refs):
        out_ref, sem = refs[-2:]
        copy = pltpu.make_async_copy(array_ref.at[pl.ds(lo, hi - lo), :], out_ref, sem)
        copy.start()
        copy.wait()

    return pl.pallas_call(
        kernel,
        out_shape=jax.ShapeDtypeStruct((hi - lo, array.shape[1]), array.dtype),
        in_specs=[ANY] * (1 + len(after)),
        out_specs=VMEM,
        scratch_shapes=[pltpu.SemaphoreType.DMA],
        compiler_params=pltpu.CompilerParams(vmem_limit_bytes=2 * MIB),
        name="fetch",
    )(array, *after)


def pass_on(array, after, flops=0):
    return pl.pallas_call(
        lambda *refs: None,
        out_shape=jax.ShapeDtypeStruct(array.shape, array.dtype),
        in_specs=[ANY] * (1 + len(after)),
        out_specs=ANY,
        input_output_aliases={0: 0},
        compiler_params=pltpu.CompilerParams(vmem_limit_bytes=MIB),
        cost_estimate=pl.CostEstimate(flops=flops, bytes_accessed=0, transcendentals=0),
        name="pass_on",
    )(array, *after)


def chunk_kernel(count, lasts, scale_ref, bias_ref, image_ref, next_ref, *refs):
    joined_ref, own_ref, other_ref, *sent_refs = refs[-4 - bool(lasts) :]
    scale, bias = scale_ref[0], bias_ref[0]
    start = 0
    for piece_ref in refs[:count]:
        rows = piece_ref.shape[0]
        joined_ref[start : start + rows, :] = piece_ref[...]
        start += rows
    part = joined_ref[...]
    image = image_ref[...]
    own = jax.nn.sigmoid(dot_nt(part, image) * scale + bias).astype(jnp.bfloat16)
    own_ref[...] = own
    total = dot_nn(own, image)
    image = next_ref[...]
    other = jax.nn.sigmoid(dot_nt(part, image) * scale + bias).astype(jnp.bfloat16)
    other_ref[...] = other
    total += dot_nn(other, image)
    total = (scale * total).astype(jnp.bfloat16)
    start = 0
    for sent_ref in sent_refs:
        sent_ref[...] = total[start : start + sent_ref.shape[0], :]
        start += sent_ref.shape[0]


def chunk(factor, shift, image, image_next, pieces, after, lasts=0):
    rows, (columns, width) = sum(piece.shape[0] for piece in pieces), image.shape
    text = [jax.ShapeDtypeStruct((r, width), jnp.bfloat16) for r in (rows, rows - lasts, lasts) if r]
    tile = jax.ShapeDtypeStruct((rows, columns), jnp.bfloat16)
    return pl.pallas_call(
        functools.partial(chunk_kernel, len(pieces), lasts),
        out_shape=[text[0], tile, tile, *text[1:]],
        in_specs=[SMEM] * 2 + [VMEM] * (2 + len(pieces)) + [ANY] * len(after),
        out_specs=[VMEM] * (2 + len(text)),
        compiler_params=pltpu.CompilerParams(vmem_limit_bytes=16 * MIB),
        cost_estimate=pl.CostEstimate(
            flops=8 * rows * columns * width,
            bytes_accessed=2 * (2 * columns + 3 * rows) * width,
            transcendentals=2 * rows * columns,
        ),
        name="chunk",
    )(factor, shift, image, image_next, *pieces, *after)


def add_rows(total, back, lo, result, after, mark=False):
    rows, width = back.shape
    step = rows // 16 // 3 * 16 if rows >= 96 else rows
    cuts = [(i, min(i + step, rows)) for i in range(0, rows, step)]

    def kernel(total_ref, back_ref, *refs):
        buffer, sems = refs[-2:]
        result_ref = refs[-4] if mark else refs[-3]
        copies = []
        for i, (a, b) in enumerate(cuts):
            buffer[a:b, :] = (total_ref[lo + a : lo + b, :] + back_ref[a:b, :].astype(jnp.float32)).astype(jnp.bfloat16)
            copies.append(
                pltpu.make_async_copy(
                    buffer.at[pl.ds(a, b - a), :], result_ref.at[pl.ds(lo + a, b - a), :], sems.at[i]
                )
            )
            copies[-1].start()
        if mark:
            refs[-3][...] = jnp.zeros((8, 128), jnp.float32)
        for copy in copies:
            copy.wait()

    kept = [] if result is None else [result]
    out = jax.ShapeDtypeStruct(total.shape, jnp.bfloat16)
    return pl.pallas_call(
        kernel,
        out_shape=(out, jax.ShapeDtypeStruct((8, 128), jnp.float32)) if mark else out,
        in_specs=[VMEM, VMEM] + [HBM] * len(kept) + [ANY] * len(after),
        out_specs=(HBM, VMEM) if mark else HBM,
        scratch_shapes=[pltpu.VMEM((rows, width), jnp.bfloat16), pltpu.SemaphoreType.DMA((len(cuts),))],
        input_output_aliases={2: 0} if kept else {},
        compiler_params=pltpu.CompilerParams(vmem_limit_bytes=4 * MIB),
        name="add_rows",
    )(total, back, *kept, *after)


def body(image, text, target, factor, shift):
    scale = factor[0]
    bias = shift[0]
    cuts = row_cuts(text.shape[0])
    first = text[: cuts[0][1]]
    part = [shifted(first, "blk", 1)]
    image_next = shifted(image, "grp", -1)
    part.append(shifted(fetch(text, *cuts[1], [first]), "blk", 1))

    target = pass_on(fetch(target, 0, 1, [part[0]]), [], 2 * 10**10)
    own = jax.nn.sigmoid(dot_nt(image, text) * scale + bias)
    column = lax.broadcasted_iota(jnp.int32, own.shape, 1)
    own = (own - (column == target[0][:, None]).astype(jnp.float32)).astype(jnp.bfloat16)
    part.append(shifted(fetch(text, *cuts[2], [own]), "blk", 1))
    image_grad = dot_nn(own, text)
    text_grad = dot_tn(own, image)

    image_next = pass_on(image_next, [image_grad, text_grad])
    part0, own0, next0, sent0 = chunk(factor, shift, image, image_next, part[:1], [])
    next_own = jax.nn.sigmoid(dot_nt(image_next, text) * scale + bias).astype(jnp.bfloat16)
    text_grad = scale * (text_grad + dot_tn(next_own, image_next))
    image_sent = dot_nn(next_own, text) + dot_tn(next0, part0)
    image_grad = image_grad + dot_tn(own0, part0)

    sent0 = pass_on(sent0, [part[1], image_sent])
    back0 = shifted(sent0, "blk", -1)

    lasts = part[2].shape[0] + 32
    part1, own1, next1, sent1, sent2 = chunk(factor, shift, image, image_next, part[1:], [sent0], lasts)
    back1 = shifted(sent1, "blk", -1)
    next1 = pass_on(next1, [sent1], 2 * 10**10)
    image_sent = (scale * (image_sent + dot_tn(next1, part1))).astype(jnp.bfloat16)
    image_back = shifted(image_sent, "grp", 1)
    back2 = shifted(pass_on(sent2, [image_sent]), "blk", -1)
    result, mark = add_rows(text_grad, back0, 0, None, [], mark=True)
    own1 = pass_on(own1, [mark])
    image_grad = scale * (image_grad + dot_tn(own1, part1))
    image_grad, mark = add_rows(image_grad, image_back, 0, None, [], mark=True)
    result = add_rows(text_grad, back1, cuts[1][0], result, [mark])
    result = add_rows(text_grad, back2, text.shape[0] - lasts, result, [])
    return image_grad, result


def solution(mesh):
    block = P(("blk", "grp"), None)
    return jax.shard_map(
        body, mesh=mesh, in_specs=(block, block, block, P(), P()), out_specs=(block, block), check_vma=False
    )
```

```python
import functools

import jax
import jax.numpy as jnp
from jax import lax
from jax.experimental import pallas as pl
from jax.experimental.pallas import tpu as pltpu
from jax.sharding import PartitionSpec as P

MIB = 2**20
ENDS = (8, 23)
SMEM = pl.BlockSpec(memory_space=pltpu.SMEM)
VMEM = pl.BlockSpec(memory_space=pltpu.VMEM)
HBM = pl.BlockSpec(memory_space=pltpu.HBM)
ANY = pl.BlockSpec(memory_space=pl.ANY)


def shifted(shard, axis, by):
    devices = lax.axis_size(axis)
    return lax.ppermute(shard, axis, [(i, (i + by) % devices) for i in range(devices)])


def dot_nt(a, b):
    return lax.dot_general(a, b, (((1,), (1,)), ((), ())), preferred_element_type=jnp.float32)


def dot_tn(a, b):
    return lax.dot_general(a, b, (((0,), (0,)), ((), ())), preferred_element_type=jnp.float32)


def dot_nn(a, b):
    return jnp.dot(a, b, preferred_element_type=jnp.float32)


def row_cuts(rows):
    tiles = rows // 16
    cuts = [0] + [tiles * ends // 26 * 16 for ends in ENDS] + [rows]
    return list(zip(cuts[:-1], cuts[1:]))


def fetch(array, lo, hi, after):
    def kernel(array_ref, *refs):
        out_ref, sem = refs[-2:]
        copy = pltpu.make_async_copy(array_ref.at[pl.ds(lo, hi - lo), :], out_ref, sem)
        copy.start()
        copy.wait()

    return pl.pallas_call(
        kernel,
        out_shape=jax.ShapeDtypeStruct((hi - lo, array.shape[1]), array.dtype),
        in_specs=[ANY] * (1 + len(after)),
        out_specs=VMEM,
        scratch_shapes=[pltpu.SemaphoreType.DMA],
        compiler_params=pltpu.CompilerParams(vmem_limit_bytes=2 * MIB),
        name="fetch",
    )(array, *after)


def pass_on(array, after, flops=0):
    return pl.pallas_call(
        lambda *refs: None,
        out_shape=jax.ShapeDtypeStruct(array.shape, array.dtype),
        in_specs=[ANY] * (1 + len(after)),
        out_specs=ANY,
        input_output_aliases={0: 0},
        compiler_params=pltpu.CompilerParams(vmem_limit_bytes=MIB),
        cost_estimate=pl.CostEstimate(flops=flops, bytes_accessed=0, transcendentals=0),
        name="pass_on",
    )(array, *after)


def chunk_kernel(count, lasts, scale_ref, bias_ref, image_ref, next_ref, *refs):
    joined_ref, own_ref, other_ref, *sent_refs = refs[-4 - bool(lasts) :]
    scale, bias = scale_ref[0], bias_ref[0]
    start = 0
    for piece_ref in refs[:count]:
        rows = piece_ref.shape[0]
        joined_ref[start : start + rows, :] = piece_ref[...]
        start += rows
    part = joined_ref[...]
    image = image_ref[...]
    own = jax.nn.sigmoid(dot_nt(part, image) * scale + bias).astype(jnp.bfloat16)
    own_ref[...] = own
    total = dot_nn(own, image)
    image = next_ref[...]
    other = jax.nn.sigmoid(dot_nt(part, image) * scale + bias).astype(jnp.bfloat16)
    other_ref[...] = other
    total += dot_nn(other, image)
    total = (scale * total).astype(jnp.bfloat16)
    start = 0
    for sent_ref in sent_refs:
        sent_ref[...] = total[start : start + sent_ref.shape[0], :]
        start += sent_ref.shape[0]


def chunk(factor, shift, image, image_next, pieces, after, lasts=0):
    rows, (columns, width) = sum(piece.shape[0] for piece in pieces), image.shape
    text = [jax.ShapeDtypeStruct((r, width), jnp.bfloat16) for r in (rows, rows - lasts, lasts) if r]
    tile = jax.ShapeDtypeStruct((rows, columns), jnp.bfloat16)
    return pl.pallas_call(
        functools.partial(chunk_kernel, len(pieces), lasts),
        out_shape=[text[0], tile, tile, *text[1:]],
        in_specs=[SMEM] * 2 + [VMEM] * (2 + len(pieces)) + [ANY] * len(after),
        out_specs=[VMEM] * (2 + len(text)),
        compiler_params=pltpu.CompilerParams(vmem_limit_bytes=16 * MIB),
        cost_estimate=pl.CostEstimate(
            flops=8 * rows * columns * width,
            bytes_accessed=2 * (2 * columns + 3 * rows) * width,
            transcendentals=2 * rows * columns,
        ),
        name="chunk",
    )(factor, shift, image, image_next, *pieces, *after)


def add_rows(total, back, lo, result, after, mark=False):
    rows, width = back.shape
    step = rows // 16 // 3 * 16 if rows >= 96 else rows
    cuts = [(i, min(i + step, rows)) for i in range(0, rows, step)]

    def kernel(total_ref, back_ref, *refs):
        buffer, sems = refs[-2:]
        result_ref = refs[-4] if mark else refs[-3]
        copies = []
        for i, (a, b) in enumerate(cuts):
            buffer[a:b, :] = (total_ref[lo + a : lo + b, :] + back_ref[a:b, :].astype(jnp.float32)).astype(jnp.bfloat16)
            copies.append(
                pltpu.make_async_copy(
                    buffer.at[pl.ds(a, b - a), :], result_ref.at[pl.ds(lo + a, b - a), :], sems.at[i]
                )
            )
            copies[-1].start()
        if mark:
            refs[-3][...] = jnp.zeros((8, 128), jnp.float32)
        for copy in copies:
            copy.wait()

    kept = [] if result is None else [result]
    out = jax.ShapeDtypeStruct(total.shape, jnp.bfloat16)
    return pl.pallas_call(
        kernel,
        out_shape=(out, jax.ShapeDtypeStruct((8, 128), jnp.float32)) if mark else out,
        in_specs=[VMEM, VMEM] + [HBM] * len(kept) + [ANY] * len(after),
        out_specs=(HBM, VMEM) if mark else HBM,
        scratch_shapes=[pltpu.VMEM((rows, width), jnp.bfloat16), pltpu.SemaphoreType.DMA((len(cuts),))],
        input_output_aliases={2: 0} if kept else {},
        compiler_params=pltpu.CompilerParams(vmem_limit_bytes=4 * MIB),
        name="add_rows",
    )(total, back, *kept, *after)


def body(image, text, target, factor, shift):
    scale = factor[0]
    bias = shift[0]
    cuts = row_cuts(text.shape[0])
    first = text[: cuts[0][1]]
    part = [shifted(first, "blk", 1)]
    image_next = shifted(image, "grp", -1)
    part.append(shifted(fetch(text, *cuts[1], [first]), "blk", 1))

    target = fetch(target, 0, 1, [part[0]])
    own = jax.nn.sigmoid(dot_nt(image, text) * scale + bias)
    column = lax.broadcasted_iota(jnp.int32, own.shape, 1)
    own = (own - (column == target[0][:, None]).astype(jnp.float32)).astype(jnp.bfloat16)
    part.append(shifted(fetch(text, *cuts[2], [own]), "blk", 1))
    image_grad = dot_nn(own, text)
    text_grad = dot_tn(own, image)

    image_next = pass_on(image_next, [image_grad, text_grad])
    part0, own0, next0, sent0 = chunk(factor, shift, image, image_next, part[:1], [])
    next_own = jax.nn.sigmoid(dot_nt(image_next, text) * scale + bias).astype(jnp.bfloat16)
    text_grad = scale * (text_grad + dot_tn(next_own, image_next))
    image_sent = dot_nn(next_own, text) + dot_tn(next0, part0)
    image_grad = image_grad + dot_tn(own0, part0)

    sent0 = pass_on(sent0, [part[1], image_sent])
    back0 = shifted(sent0, "blk", -1)

    lasts = part[2].shape[0] + 32
    part1, own1, next1, sent1, sent2 = chunk(factor, shift, image, image_next, part[1:], [sent0], lasts)
    back1 = shifted(sent1, "blk", -1)
    next1 = pass_on(next1, [sent1], 2 * 10**10)
    image_sent = (scale * (image_sent + dot_tn(next1, part1))).astype(jnp.bfloat16)
    image_back = shifted(image_sent, "grp", 1)
    back2 = shifted(pass_on(sent2, [image_sent]), "blk", -1)
    result, mark = add_rows(text_grad, back0, 0, None, [], mark=True)
    own1 = pass_on(own1, [mark])
    image_grad = scale * (image_grad + dot_tn(own1, part1))
    image_grad, mark = add_rows(image_grad, image_back, 0, None, [], mark=True)
    result = add_rows(text_grad, back1, cuts[1][0], result, [mark])
    result = add_rows(text_grad, back2, text.shape[0] - lasts, result, [])
    return image_grad, result


def solution(mesh):
    block = P(("blk", "grp"), None)
    return jax.shard_map(
        body, mesh=mesh, in_specs=(block, block, block, P(), P()), out_specs=(block, block), check_vma=False
    )
```

```python
import functools

import jax
import jax.numpy as jnp
from jax import lax
from jax.experimental import pallas as pl
from jax.experimental.pallas import tpu as pltpu
from jax.sharding import PartitionSpec as P

MIB = 2**20
ENDS = (8, 23)
SMEM = pl.BlockSpec(memory_space=pltpu.SMEM)
VMEM = pl.BlockSpec(memory_space=pltpu.VMEM)
HBM = pl.BlockSpec(memory_space=pltpu.HBM)
ANY = pl.BlockSpec(memory_space=pl.ANY)


def shifted(shard, axis, by):
    devices = lax.axis_size(axis)
    return lax.ppermute(shard, axis, [(i, (i + by) % devices) for i in range(devices)])


def dot_nt(a, b):
    return lax.dot_general(a, b, (((1,), (1,)), ((), ())), preferred_element_type=jnp.float32)


def dot_tn(a, b):
    return lax.dot_general(a, b, (((0,), (0,)), ((), ())), preferred_element_type=jnp.float32)


def dot_nn(a, b):
    return jnp.dot(a, b, preferred_element_type=jnp.float32)


def row_cuts(rows):
    tiles = rows // 16
    cuts = [0] + [tiles * ends // 26 * 16 for ends in ENDS] + [rows]
    return list(zip(cuts[:-1], cuts[1:]))


def fetch(array, lo, hi, after):
    def kernel(array_ref, *refs):
        out_ref, sem = refs[-2:]
        copy = pltpu.make_async_copy(array_ref.at[pl.ds(lo, hi - lo), :], out_ref, sem)
        copy.start()
        copy.wait()

    return pl.pallas_call(
        kernel,
        out_shape=jax.ShapeDtypeStruct((hi - lo, array.shape[1]), array.dtype),
        in_specs=[ANY] * (1 + len(after)),
        out_specs=VMEM,
        scratch_shapes=[pltpu.SemaphoreType.DMA],
        compiler_params=pltpu.CompilerParams(vmem_limit_bytes=2 * MIB),
        name="fetch",
    )(array, *after)


def pass_on(array, after, flops=0):
    return pl.pallas_call(
        lambda *refs: None,
        out_shape=jax.ShapeDtypeStruct(array.shape, array.dtype),
        in_specs=[ANY] * (1 + len(after)),
        out_specs=ANY,
        input_output_aliases={0: 0},
        compiler_params=pltpu.CompilerParams(vmem_limit_bytes=MIB),
        cost_estimate=pl.CostEstimate(flops=flops, bytes_accessed=0, transcendentals=0),
        name="pass_on",
    )(array, *after)


def chunk_kernel(count, lasts, scale_ref, bias_ref, image_ref, next_ref, *refs):
    joined_ref, own_ref, other_ref, *sent_refs = refs[-4 - bool(lasts) :]
    scale, bias = scale_ref[0], bias_ref[0]
    start = 0
    for piece_ref in refs[:count]:
        rows = piece_ref.shape[0]
        joined_ref[start : start + rows, :] = piece_ref[...]
        start += rows
    part = joined_ref[...]
    image = image_ref[...]
    own = jax.nn.sigmoid(dot_nt(part, image) * scale + bias).astype(jnp.bfloat16)
    own_ref[...] = own
    total = dot_nn(own, image)
    image = next_ref[...]
    other = jax.nn.sigmoid(dot_nt(part, image) * scale + bias).astype(jnp.bfloat16)
    other_ref[...] = other
    total += dot_nn(other, image)
    total = (scale * total).astype(jnp.bfloat16)
    start = 0
    for sent_ref in sent_refs:
        sent_ref[...] = total[start : start + sent_ref.shape[0], :]
        start += sent_ref.shape[0]


def chunk(factor, shift, image, image_next, pieces, after, lasts=0):
    rows, (columns, width) = sum(piece.shape[0] for piece in pieces), image.shape
    text = [jax.ShapeDtypeStruct((r, width), jnp.bfloat16) for r in (rows, rows - lasts, lasts) if r]
    tile = jax.ShapeDtypeStruct((rows, columns), jnp.bfloat16)
    return pl.pallas_call(
        functools.partial(chunk_kernel, len(pieces), lasts),
        out_shape=[text[0], tile, tile, *text[1:]],
        in_specs=[SMEM] * 2 + [VMEM] * (2 + len(pieces)) + [ANY] * len(after),
        out_specs=[VMEM] * (2 + len(text)),
        compiler_params=pltpu.CompilerParams(vmem_limit_bytes=16 * MIB),
        cost_estimate=pl.CostEstimate(
            flops=8 * rows * columns * width,
            bytes_accessed=2 * (2 * columns + 3 * rows) * width,
            transcendentals=2 * rows * columns,
        ),
        name="chunk",
    )(factor, shift, image, image_next, *pieces, *after)


def add_rows(total, back, lo, result, after, mark=False):
    rows, width = back.shape
    step = rows // 16 // 3 * 16 if rows >= 96 else rows
    cuts = [(i, min(i + step, rows)) for i in range(0, rows, step)]

    def kernel(total_ref, back_ref, *refs):
        buffer, sems = refs[-2:]
        result_ref = refs[-4] if mark else refs[-3]
        copies = []
        for i, (a, b) in enumerate(cuts):
            buffer[a:b, :] = (total_ref[lo + a : lo + b, :] + back_ref[a:b, :].astype(jnp.float32)).astype(jnp.bfloat16)
            copies.append(
                pltpu.make_async_copy(
                    buffer.at[pl.ds(a, b - a), :], result_ref.at[pl.ds(lo + a, b - a), :], sems.at[i]
                )
            )
            copies[-1].start()
        if mark:
            refs[-3][...] = jnp.zeros((8, 128), jnp.float32)
        for copy in copies:
            copy.wait()

    kept = [] if result is None else [result]
    out = jax.ShapeDtypeStruct(total.shape, jnp.bfloat16)
    return pl.pallas_call(
        kernel,
        out_shape=(out, jax.ShapeDtypeStruct((8, 128), jnp.float32)) if mark else out,
        in_specs=[VMEM, VMEM] + [HBM] * len(kept) + [ANY] * len(after),
        out_specs=(HBM, VMEM) if mark else HBM,
        scratch_shapes=[pltpu.VMEM((rows, width), jnp.bfloat16), pltpu.SemaphoreType.DMA((len(cuts),))],
        input_output_aliases={2: 0} if kept else {},
        compiler_params=pltpu.CompilerParams(vmem_limit_bytes=4 * MIB),
        name="add_rows",
    )(total, back, *kept, *after)


def body(image, text, target, factor, shift):
    scale = factor[0]
    bias = shift[0]
    cuts = row_cuts(text.shape[0])
    first = text[: cuts[0][1]]
    part = [shifted(first, "blk", 1)]
    image_next = shifted(image, "grp", -1)
    part.append(shifted(fetch(text, *cuts[1], [first]), "blk", 1))

    target = pass_on(fetch(target, 0, 1, [part[0]]), [], 2 * 10**10)
    own = jax.nn.sigmoid(dot_nt(image, text) * scale + bias)
    column = lax.broadcasted_iota(jnp.int32, own.shape, 1)
    own = (own - (column == target[0][:, None]).astype(jnp.float32)).astype(jnp.bfloat16)
    part.append(shifted(fetch(text, *cuts[2], [own]), "blk", 1))
    image_grad = dot_nn(own, text)
    text_grad = dot_tn(own, image)

    image_next = pass_on(image_next, [image_grad, text_grad])
    part0, own0, next0, sent0 = chunk(factor, shift, image, image_next, part[:1], [])
    next_own = jax.nn.sigmoid(dot_nt(image_next, text) * scale + bias).astype(jnp.bfloat16)
    text_grad = scale * (text_grad + dot_tn(next_own, image_next))
    image_sent = dot_nn(next_own, text) + dot_tn(next0, part0)
    image_grad = image_grad + dot_tn(own0, part0)

    sent0 = pass_on(sent0, [part[1], image_sent])
    back0 = shifted(sent0, "blk", -1)

    lasts = part[2].shape[0] + 64
    part1, own1, next1, sent1, sent2 = chunk(factor, shift, image, image_next, part[1:], [sent0], lasts)
    back1 = shifted(sent1, "blk", -1)
    next1 = pass_on(next1, [sent1], 2 * 10**10)
    image_sent = (scale * (image_sent + dot_tn(next1, part1))).astype(jnp.bfloat16)
    image_back = shifted(image_sent, "grp", 1)
    back2 = shifted(pass_on(sent2, [image_sent]), "blk", -1)
    result, mark = add_rows(text_grad, back0, 0, None, [], mark=True)
    own1 = pass_on(own1, [mark])
    image_grad = scale * (image_grad + dot_tn(own1, part1))
    image_grad, mark = add_rows(image_grad, image_back, 0, None, [], mark=True)
    result = add_rows(text_grad, back1, cuts[1][0], result, [mark])
    result = add_rows(text_grad, back2, text.shape[0] - lasts, result, [])
    return image_grad, result


def solution(mesh):
    block = P(("blk", "grp"), None)
    return jax.shard_map(
        body, mesh=mesh, in_specs=(block, block, block, P(), P()), out_specs=(block, block), check_vma=False
    )
```
